32 devices in a mesh: slab: 4 (over z), sub: 8 (over y, x, core).
Axes of the slice: x: 2, y: 2, z: 4, core: 2. Of those that a mesh axis runs over, the one named last changes fastest.
Arguments:
- velocity_field: float32 [3, 64, 256, 512], P(None, 'slab', 'sub'), may hold values from -6 to 6
- particle_state: float32 [1024, 6, 256], P(('slab', 'sub')), as said below
- stokes_time: float32 [1024, 256], P(('slab', 'sub')), may hold values from 0.2 to 2
- box_base: int32 [1024, 3], P(('slab', 'sub')), may hold values from -2 to 511, as said below
- live_bins: int32 [32], P(('slab', 'sub')), may hold values from 1 to 32, as said below
Outputs:
- state_out: float32 [1024, 6, 256], P(('slab', 'sub'))
The draws below stay inside these ranges and needn't reach their ends.
Inputs may be any that keep to these rules, and one draw needn't show every extreme that they name: `box_base`: columns 0 and 1 lie from -2 to 14 and from -2 to 30, column 2 from 0 to 511; bin 0 has column 0 at -2 and column 2 at 511. `live_bins`: some device has all 32 slots occupied. `particle_state`: positions lie in the box's central cell, 0 to 1 in each coordinate.
All inputs are finite; a program needn't handle non-finite values.
Results may differ from the reference program's by a relative error of at most 0.0003.
Values sent between devices are 32-bit elements; how exact they have to be, the bound alone decides.
No kernel may reach another device: no remote copies, remote signals or barrier semaphores. Data moves between devices by JAX's collectives and lax.ppermute only.
A program may use at most 64 MiB of HBM per device.

```python
import math
import jax
import jax.numpy as jnp
from jax import lax

CX = 16
CY = 32
NZ = 512
BIN_DEV = 32
PART = 256
SUBSTEPS = 4
NX = 64
NY = 256
BINS = 1024
N_SUB = 8
DEVICES = 32


def draw_particle_state(key, part):
    key_pos = jax.random.fold_in(key, 11)
    key_vel = jax.random.fold_in(key, 12)
    position = jax.random.uniform(key_pos, (BINS, 3, PART), jnp.float32, 0.0, 1.0)
    velocity = 0.5 * jax.random.normal(key_vel, (BINS, 3, PART), jnp.float32)
    return jnp.concatenate([position, velocity], axis=1).astype(jnp.float32)


def draw_box_base(key, part):
    key_x = jax.random.fold_in(key, 21)
    key_y = jax.random.fold_in(key, 22)
    key_z = jax.random.fold_in(key, 23)
    base_x = jax.random.randint(key_x, (BINS,), -2, CX - 1)
    base_y = jax.random.randint(key_y, (BINS,), -2, CY - 1)
    base_z = jax.random.randint(key_z, (BINS,), 0, NZ)
    bases = jnp.stack([base_x, base_y, base_z], axis=1).astype(jnp.int32)
    bases = bases.at[0, 0].set(-2)
    bases = bases.at[0, 2].set(NZ - 1)
    return bases


def draw_live_bins(key, part):
    key_flag = jax.random.fold_in(key, 31)
    key_high = jax.random.fold_in(key, 32)
    key_low = jax.random.fold_in(key, 33)
    key_pick = jax.random.fold_in(key, 34)
    crowded = jax.random.randint(key_flag, (DEVICES,), 0, 4) == 0
    high_count = jax.random.randint(key_high, (DEVICES,), BIN_DEV // 2, BIN_DEV + 1)
    low_count = jax.random.randint(key_low, (DEVICES,), 1, BIN_DEV // 4 + 1)
    counts = jnp.where(crowded, high_count, low_count).astype(jnp.int32)
    chosen = jax.random.randint(key_pick, (), 0, DEVICES)
    return counts.at[chosen].set(BIN_DEV)


def shard_levels(stream_key, dims, split, least, top_value):
    factor_of, own = 1.0, jax.random.fold_in(stream_key, 6)
    for axis_at, shards_of in split:
        heights = jnp.exp(jax.random.uniform(jax.random.fold_in(own, axis_at), (shards_of,), jnp.float32, least / len(split), top_value / len(split)))
        factor_of = factor_of * jnp.repeat(heights, dims[axis_at] // shards_of).reshape([-1 if axis == axis_at else 1 for axis in range(len(dims))])
    return factor_of


def gaussian(rng, dims, scale, limit, shards=(), kind=jnp.bfloat16):
    gain = shard_levels(rng, dims, shards, -0.22, 0.18) if shards else 1.0
    array = jax.random.normal(rng, dims, jnp.float32) * scale * gain
    return jnp.minimum(jnp.maximum(array, -limit), limit).astype(kind)


def setup_inputs(seed: int = 0) -> dict:
    keys = jax.random.split(jax.random.key(seed), 6)
    velocity_field = gaussian(keys[0], (3, NX, NY, NZ), 1.0, 6.0, ((1, 4), (2, 8)), jnp.float32)
    particle_state = draw_particle_state(jax.random.fold_in(keys[5], 71), 0)
    stokes_time = jnp.clip(jnp.exp(math.log(2.0) - 2.3025851 * jax.random.uniform(keys[2], (BINS, PART), jnp.float32) ** shard_levels(keys[2], (BINS, PART), ((0, 32),), -0.2, 0.2)), 0.2, 2.0)
    box_base = draw_box_base(jax.random.fold_in(keys[5], 71), 0)
    live_bins = draw_live_bins(jax.random.fold_in(keys[5], 71), 0)
    return dict(velocity_field=velocity_field, particle_state=particle_state, stokes_time=stokes_time, box_base=box_base, live_bins=live_bins)


STEP_SIZE = 0.2


def cubic_weights(offset):
    plus = offset + 1.0
    minus = offset - 1.0
    minus_two = offset - 2.0
    return jnp.stack([-offset * minus * minus_two / 6.0, plus * minus * minus_two / 2.0,
                      -plus * offset * minus_two / 2.0, plus * offset * minus / 6.0], axis=1)


def sample(boxes, position):
    along_x = cubic_weights(position[:, 0])
    along_y = cubic_weights(position[:, 1])
    along_z = cubic_weights(position[:, 2])
    weights = along_x[:, :, None, None, :] * along_y[:, None, :, None, :] * along_z[:, None, None, :, :]
    return jnp.sum(boxes[:, :, :, :, :, None] * weights[:, None], axis=(2, 3, 4))


def advance(boxes, states, stokes):
    position = states[:, :3]
    velocity = states[:, 3:]
    rate = (1.0 / stokes)[:, None, :]
    for substep in range(SUBSTEPS):
        slope = (sample(boxes, position) - velocity) * rate
        middle_pos = position + 0.5 * STEP_SIZE * velocity
        middle_vel = velocity + 0.5 * STEP_SIZE * slope
        position = position + STEP_SIZE * middle_vel
        velocity = velocity + STEP_SIZE * (sample(boxes, middle_pos) - middle_vel) * rate
    return jnp.concatenate([position, velocity], axis=1)


def reference(velocity_field, particle_state, stokes_time, box_base, live_bins):
    all_states = particle_state.reshape(DEVICES, BIN_DEV, 6, PART)
    all_stokes = stokes_time.reshape(DEVICES, BIN_DEV, PART)
    all_bases = box_base.reshape(DEVICES, BIN_DEV, 3)

    def one_device(inputs):
        device, states, stokes, bases, live_count = inputs
        slab_index = device // N_SUB
        sub_index = device % N_SUB
        offsets = jnp.arange(4, dtype=jnp.int32)
        rows_x = (slab_index * CX + bases[:, 0:1] + offsets[None, :]) % NX
        rows_y = (sub_index * CY + bases[:, 1:2] + offsets[None, :]) % NY
        rows_z = (bases[:, 2:3] + offsets[None, :]) % NZ
        boxes = velocity_field[:, rows_x[:, :, None, None], rows_y[:, None, :, None], rows_z[:, None, None, :]]
        boxes = jnp.moveaxis(boxes, 0, 1)
        moved = advance(boxes, states, stokes)
        keep = jnp.arange(BIN_DEV, dtype=jnp.int32) < live_count
        return jnp.where(keep[:, None, None], moved, states)

    devices = jnp.arange(DEVICES, dtype=jnp.int32)
    result = lax.map(one_device, (devices, all_states, all_stokes, all_bases, live_bins))
    return result.reshape(BINS, 6, PART)
```

```python
import functools

import jax
import jax.numpy as jnp
import numpy as np
from jax import lax
from jax.experimental import pallas as pl
from jax.experimental.pallas import tpu as pltpu
from jax.sharding import PartitionSpec as P

SUBSTEPS = 4
STEP_SIZE = 0.2
LANES = 128
NODES = 16
BLOCK = 8
TOP = 8
VMEM_LIMIT = 48 * 1024 * 1024


def lane_nodes():
    row = lax.broadcasted_iota(jnp.int32, (8, LANES), 0)
    lane = lax.broadcasted_iota(jnp.int32, (8, LANES), 1)
    return jnp.where(row < 4, lane // 4, -1000)


def flatten_rows(rows):
    return jnp.sum(pltpu.roll(rows, 0, 1, stride=4, stride_axis=0), axis=0, keepdims=True)


def gather_rows(padded, index, first_y, first_z, slot, nodes, lane, valid):
    tile = first_z // LANES
    offset = first_z % LANES
    tiles = padded.shape[-3]
    here = padded[(*index, tile, pl.ds(TOP + first_y, 8), slice(None))]
    there = padded[(*index, (tile + 1) % tiles, pl.ds(TOP + first_y, 8), slice(None))]
    rows = jnp.where(lane >= offset, here, there)
    rows = pltpu.roll(rows, (NODES * slot - first_z) & (LANES - 1), 1)
    wanted = jnp.where(valid, 4 * slot, -5000)
    return jnp.where(nodes == wanted, rows, 0.0)


def fill_halo(padded, before, after, plane_pairs, length):
    tiles = padded.shape[-3]
    for into, source in plane_pairs:
        for tile in range(tiles):
            lanes = slice(tile * LANES, (tile + 1) * LANES)
            padded[(*into, tile, slice(TOP - 2, TOP), slice(None))] = before[(*source, slice(None), lanes)]
            padded[(*into, tile, slice(TOP + length, TOP + length + 2), slice(None))] = after[
                (*source, slice(None), lanes)
            ]


def answer_kernel(upper_table, lower_table, field, before, after, upper_out, lower_out, edge, acc, hits, sems):
    comps, depth, length, cells = field.shape
    tiles = cells // LANES
    bins = upper_table.shape[0]
    copies = []
    for side, start in enumerate((depth - 2, 0)):
        for tile in range(tiles):
            copy = pltpu.make_async_copy(
                field.at[:, pl.ds(start, 2), :, pl.ds(tile * LANES, LANES)],
                edge.at[side, :, :, tile, pl.ds(TOP, length), :],
                sems.at[side * tiles + tile],
            )
            copy.start()
            copies.append(copy)
    pairs = [
        ((side, c, layer), (c, start + layer))
        for side, start in enumerate((depth - 2, 0))
        for c in range(comps)
        for layer in range(2)
    ]
    fill_halo(edge, before, after, pairs, length)
    acc[...] = jnp.zeros_like(acc)
    nodes = lane_nodes()
    lane = lax.broadcasted_iota(jnp.int32, (8, LANES), 1)
    counts = []
    for side, table in enumerate((upper_table, lower_table)):
        found = jnp.int32(0)
        for b in range(bins):
            first_x = table[b, 0]
            hits[side, found] = b
            wanted = first_x < 0 if side == 0 else first_x > depth - 4
            found = found + wanted.astype(jnp.int32)
        counts.append(found)
    for copy in copies:
        copy.wait()
    for side, table in enumerate((upper_table, lower_table)):

        def one_bin(n, _, side=side, table=table):
            b = hits[side, n]
            first_x, first_y, first_z = table[b, 0], table[b, 1], table[b, 2]
            for slot in range(2):
                layer = first_x + 2 + slot if side == 0 else first_x + 2 - depth + slot
                valid = (layer >= 0) & (layer < 2)
                layer = jnp.clip(layer, 0, 1)
                for c in range(comps):
                    acc[side, slot, c, b // BLOCK] += gather_rows(
                        edge, (side, c, layer), first_y, first_z, b % BLOCK, nodes, lane, valid
                    )
            return 0

        lax.fori_loop(0, counts[side], one_bin, 0)
    for side, out in enumerate((upper_out, lower_out)):
        out[...] = jnp.zeros_like(out)
        for slot in range(2):
            for c in range(comps):
                for tile in range(bins // BLOCK):
                    out[tile, slot * 4 + c : slot * 4 + c + 1, :] = flatten_rows(acc[side, slot, c, tile])


def cubic(t, row_node):
    lead = jnp.where(row_node == 0, -1.0 / 6.0, jnp.where(row_node == 1, 0.5, jnp.where(row_node == 2, -0.5, 1.0 / 6.0)))
    first = jnp.where(row_node == 0, 0.0, -1.0)
    second = jnp.where(row_node <= 1, 1.0, 0.0)
    third = jnp.where(row_node == 3, 1.0, 2.0)
    return (lead * (t - first)) * ((t - second) * (t - third))


def sample(lhs, position, patterns):
    fine, low, high = patterns
    n = position.shape[1]
    px = jnp.broadcast_to(position[0:1], (8, n))
    py = jnp.broadcast_to(position[1:2], (8, n))
    pz = jnp.broadcast_to(position[2:3], (8, n))
    along_z = cubic(pz, fine)
    weights = jnp.concatenate([along_z * cubic(py, low), along_z * cubic(py, high)], axis=0)
    head = weights.astype(jnp.bfloat16)
    tail = (weights - head.astype(jnp.float32)).astype(jnp.bfloat16)
    planes = jnp.dot(lhs, jnp.concatenate([head, head, tail], axis=0), preferred_element_type=jnp.float32)
    total = planes[0:8] * cubic(px, low) + planes[8:16] * cubic(px, high)
    return total[0:4] + total[4:8]


def pack_box(table, slot):
    box = pltpu.roll(table, (LANES - NODES * slot) & (LANES - 1), 1)
    head = box.astype(jnp.bfloat16).astype(jnp.float32)
    tail = box - head
    lane = lax.broadcasted_iota(jnp.int32, box.shape, 1)
    packed = jnp.where(
        lane < NODES,
        head,
        jnp.where(lane < 2 * NODES, pltpu.roll(tail, NODES, 1), pltpu.roll(head, 2 * NODES, 1)),
    )
    return packed[:, : 3 * NODES].astype(jnp.bfloat16)


def advance_bins(bins, load_table, state, stokes, store):
    row = lax.broadcasted_iota(jnp.int32, (8, 1), 0)
    patterns = (row % 4, row // 4, 2 + row // 4)
    boxes = [pack_box(load_table(b // BLOCK), b % BLOCK) for b in bins]
    states = [state[b] for b in bins]
    rates = [1.0 / stokes[pl.ds(b, 1), :] for b in bins]
    carry = [(s[0:3], s[3:6]) for s in states]

    def substep(_, carry):
        moved = []
        for (position, velocity), box, rate in zip(carry, boxes, rates):
            middle_pos = position + 0.5 * STEP_SIZE * velocity
            here = sample(box, position, patterns)[0:3]
            there = sample(box, middle_pos, patterns)[0:3]
            slope = (here - velocity) * rate
            middle_vel = velocity + 0.5 * STEP_SIZE * slope
            moved.append(
                (position + STEP_SIZE * middle_vel, velocity + STEP_SIZE * (there - middle_vel) * rate)
            )
        return moved

    carry = lax.fori_loop(0, SUBSTEPS, substep, carry)
    for b, (position, velocity) in zip(bins, carry):
        store(b, position, velocity)


def main_kernel(
    table, live, field, before, after, state, stokes, out, box_table, late, padded, acc, early, sems
):
    comps, depth, length, cells = field.shape
    tiles = cells // LANES
    bins = table.shape[0]
    copies = []
    for tile in range(tiles):
        copy = pltpu.make_async_copy(
            field.at[:, :, :, pl.ds(tile * LANES, LANES)],
            padded.at[:, :, tile, pl.ds(TOP, length), :],
            sems.at[tile],
        )
        copy.start()
        copies.append(copy)
    fill_halo(padded, before, after, [((c, x), (c, x)) for c in range(comps) for x in range(depth)], length)
    out[...] = state[...]
    count = live[0]
    early_count, late_count = jnp.int32(0), jnp.int32(0)
    for b in range(bins):
        first_x = table[b, 0]
        alone = (first_x >= 0) & (first_x <= depth - 4)
        is_live = b < count
        early[early_count] = b
        late[late_count] = b
        early_count = early_count + (alone & is_live).astype(jnp.int32)
        late_count = late_count + (jnp.logical_not(alone) & is_live).astype(jnp.int32)
    late[bins] = late_count
    for copy in copies:
        copy.wait()
    nodes = lane_nodes()
    lane = lax.broadcasted_iota(jnp.int32, (8, LANES), 1)
    box_table[...] = jnp.zeros_like(box_table)

    def one_tile(tile, _):
        acc[...] = jnp.zeros_like(acc)

        def one_bin(slot, _):
            b = tile * BLOCK + slot
            first_x, first_y, first_z = table[b, 0], table[b, 1], table[b, 2]
            for i in range(4):
                x = first_x + i
                valid = (x >= 0) & (x < depth)
                x = jnp.clip(x, 0, depth - 1)
                for c in range(comps):
                    acc[i, c] += gather_rows(padded, (c, x), first_y, first_z, slot, nodes, lane, valid)
            return 0

        lax.fori_loop(0, BLOCK, one_bin, 0)
        for i in range(4):
            for c in range(comps):
                box_table[tile, i * 4 + c : i * 4 + c + 1, :] = flatten_rows(acc[i, c])
        return 0

    lax.fori_loop(0, (count + BLOCK - 1) // BLOCK, one_tile, 0)

    def store(b, position, velocity):
        out[b, 0:3] = position
        out[b, 3:6] = velocity

    def one_block(n, _):
        chosen = [early[jnp.minimum(n * BLOCK + k, early_count - 1)] for k in range(BLOCK)]
        advance_bins(chosen, lambda tile: box_table[tile], state, stokes, store)
        return 0

    lax.fori_loop(0, (early_count + BLOCK - 1) // BLOCK, one_block, 0)


def late_kernel(late, box_table, from_lower, from_upper, state, stokes, done, out, full):
    bins = state.shape[0]
    full[:, 0:8, :] = box_table[:, 0:8, :] + from_lower[...]
    full[:, 8:16, :] = box_table[:, 8:16, :] + from_upper[...]
    out[...] = done[...]
    count = late[bins]

    def store(b, position, velocity):
        out[b, 0:3] = position
        out[b, 3:6] = velocity

    def one_block(n, _):
        chosen = [late[jnp.minimum(n * BLOCK + k, count - 1)] for k in range(BLOCK)]
        advance_bins(chosen, lambda tile: full[tile], state, stokes, store)
        return 0

    lax.fori_loop(0, (count + BLOCK - 1) // BLOCK, one_block, 0)


def in_smem():
    return pl.BlockSpec(memory_space=pltpu.SMEM)


def in_vmem():
    return pl.BlockSpec(memory_space=pltpu.VMEM)


def in_place():
    return pl.BlockSpec(memory_space=pl.ANY)


def body(velocity_field, particle_state, stokes_time, box_base, live_bins):
    comps, depth, length, cells = velocity_field.shape
    bins = box_base.shape[0]
    tiles = cells // LANES
    groups = bins // BLOCK

    def shift(array, axis, step):
        devices = lax.axis_size(axis)
        return lax.ppermute(array, axis, [(i, (i + step) % devices) for i in range(devices)])

    before = shift(velocity_field[:, :, length - 2 :, :], "sub", 1)
    after = shift(velocity_field[:, :, :2, :], "sub", -1)
    upper_table = shift(box_base, "slab", -1)
    lower_table = shift(box_base, "slab", 1)

    answer = jax.ShapeDtypeStruct((groups, 8, LANES), jnp.float32)
    for_upper, for_lower = pl.pallas_call(
        answer_kernel,
        out_shape=(answer, answer),
        in_specs=[in_smem(), in_smem(), in_place(), in_vmem(), in_vmem()],
        out_specs=(in_vmem(), in_vmem()),
        scratch_shapes=[
            pltpu.VMEM((2, comps, 2, tiles, length + 2 * TOP, LANES), jnp.float32),
            pltpu.VMEM((2, 2, comps, groups, 8, LANES), jnp.float32),
            pltpu.SMEM((2, bins + 1), jnp.int32),
            pltpu.SemaphoreType.DMA((2 * tiles,)),
        ],
        compiler_params=pltpu.CompilerParams(vmem_limit_bytes=VMEM_LIMIT),
        name="answers",
    )(upper_table, lower_table, velocity_field, before, after)
    from_lower = shift(for_upper, "slab", 1)
    from_upper = shift(for_lower, "slab", -1)

    moved, box_table, late = pl.pallas_call(
        main_kernel,
        out_shape=(
            jax.ShapeDtypeStruct(particle_state.shape, jnp.float32),
            jax.ShapeDtypeStruct((groups, NODES, LANES), jnp.float32),
            jax.ShapeDtypeStruct((bins + 1,), jnp.int32),
        ),
        in_specs=[in_smem(), in_smem(), in_place(), in_vmem(), in_vmem(), in_vmem(), in_vmem()],
        out_specs=(in_vmem(), in_vmem(), in_smem()),
        scratch_shapes=[
            pltpu.VMEM((comps, depth, tiles, length + 2 * TOP, LANES), jnp.float32),
            pltpu.VMEM((4, comps, 8, LANES), jnp.float32),
            pltpu.SMEM((bins + 1,), jnp.int32),
            pltpu.SemaphoreType.DMA((tiles,)),
        ],
        compiler_params=pltpu.CompilerParams(vmem_limit_bytes=VMEM_LIMIT),
        cost_estimate=pl.CostEstimate(flops=10_000_000, bytes_accessed=4_000_000, transcendentals=0),
        name="own_bins",
    )(box_base, live_bins, velocity_field, before, after, particle_state, stokes_time)

    return pl.pallas_call(
        late_kernel,
        out_shape=jax.ShapeDtypeStruct(particle_state.shape, jnp.float32),
        in_specs=[in_smem()] + [in_vmem()] * 6,
        out_specs=in_vmem(),
        scratch_shapes=[pltpu.VMEM((groups, NODES, LANES), jnp.float32)],
        compiler_params=pltpu.CompilerParams(vmem_limit_bytes=VMEM_LIMIT),
        name="edge_bins",
    )(late, box_table, from_lower, from_upper, particle_state, stokes_time, moved)


def solution(mesh):
    placed = (
        P(None, "slab", "sub", None),
        P(("slab", "sub"), None, None),
        P(("slab", "sub"), None),
        P(("slab", "sub"), None),
        P(("slab", "sub")),
    )
    return jax.shard_map(
        body, mesh=mesh, in_specs=placed, out_specs=P(("slab", "sub"), None, None), check_vma=False
    )
```

```python
import functools

import jax
import jax.numpy as jnp
from jax import lax
from jax.experimental import pallas as pl
from jax.experimental.pallas import tpu as pltpu
from jax.sharding import PartitionSpec as P

SUBSTEPS = 4
STEP_SIZE = 0.2
LANES = 128
NODES = 16
GROUP = 8
TOP = 8
ANSWERS = 4
VMEM_LIMIT = 48 * 1024 * 1024


def rows_and_lanes():
    return lax.broadcasted_iota(jnp.int32, (8, LANES), 0), lax.broadcasted_iota(jnp.int32, (8, LANES), 1)


def gather_pair(planes, index, valid, nodes, first_row, first_z, slot):
    row, lane = rows_and_lanes()
    tiles = planes.shape[-3]
    tile, offset = first_z // LANES, first_z % LANES
    beside = (tile + 1) % tiles
    upper = row < 4
    first, second = index

    def load(at):
        return jnp.where(
            upper,
            planes[(*first, at, pl.ds(first_row, 8), slice(None))],
            planes[(*second, at, pl.ds(first_row - 4, 8), slice(None))],
        )

    rows = jnp.where(lane >= offset, load(tile), load(beside))
    rows = pltpu.roll(rows, (NODES * slot - first_z) & (LANES - 1), 1)
    wanted = jnp.where(upper, jnp.where(valid[0], 4 * slot, -1), jnp.where(valid[1], 4 * slot, -1))
    return rows, nodes & (lane // 4 == wanted)


def flatten_pair(parts):
    row, _ = rows_and_lanes()
    total = None
    for c, part in enumerate(parts):
        part = pltpu.roll(part, 0, 1, stride=4, stride_axis=0)
        part = part + pltpu.roll(part, 7, 0)
        part = part + pltpu.roll(part, 6, 0)
        part = jnp.where(row % 4 == 0, part, 0.0)
        part = pltpu.roll(part, c, 0) if c else part
        total = part if total is None else total + part
    return total


def align_pair(tile):
    row, _ = rows_and_lanes()
    return jnp.where(row < 4, tile, pltpu.roll(tile, LANES - NODES, 1))


def load_kernel(field, padded, near, far, sems):
    comps, depth, length, cells = field.shape
    tiles = cells // LANES
    copies = []
    for tile in range(tiles):
        copy = pltpu.make_async_copy(
            field.at[:, :, :, pl.ds(tile * LANES, LANES)],
            padded.at[:, :, tile, pl.ds(TOP, length), :],
            sems.at[tile],
        )
        copy.start()
        copies.append(copy)
    even = lax.axis_index("sub") % 2 == 0
    first, last = TOP, TOP + length - 2
    near_row, far_row = jnp.where(even, last, first), jnp.where(even, first, last)
    for tile in range(tiles):
        copies[tile].wait()
        lanes = slice(tile * LANES, (tile + 1) * LANES)
        for c in range(comps):
            for x in range(depth):
                near[c, x, :, lanes] = padded[c, x, tile, pl.ds(near_row, 2), :]
                far[c, x, :, lanes] = padded[c, x, tile, pl.ds(far_row, 2), :]


def fill_halo(halo, near, far, planes):
    even = lax.axis_index("sub") % 2 == 0
    near_row, far_row = jnp.where(even, 8, 6), jnp.where(even, 6, 8)
    for c in range(halo.shape[0]):
        for into, x in enumerate(planes):
            for tile in range(halo.shape[-3]):
                lanes = slice(tile * LANES, (tile + 1) * LANES)
                halo[c, into, tile, pl.ds(near_row, 2), :] = near[c, x, :, lanes]
                halo[c, into, tile, pl.ds(far_row, 2), :] = far[c, x, :, lanes]


def halo_row(first_y, length):
    return jnp.where(first_y < 0, 8 + first_y, 8 + first_y - length)


def own_nodes(first_y, length):
    row, _ = rows_and_lanes()
    node = row % 4 + first_y
    return (node >= 0) & (node < length)


def box_planes(first_x, pair, depth):
    x = [first_x + 2 * pair, first_x + 2 * pair + 1]
    return [jnp.clip(at, 0, depth - 1) for at in x], [(at >= 0) & (at < depth) for at in x]


def own_boxes_kernel(table, live, padded, box_table):
    comps, depth, _, rows, _ = padded.shape
    length = rows - 2 * TOP
    box_table[...] = jnp.zeros_like(box_table)

    def one_group(group, _):
        parts = [[jnp.zeros((8, LANES), jnp.float32)] * comps for _ in range(2)]
        for slot in range(GROUP):
            b = group * GROUP + slot
            first_x, first_y, first_z = table[0, b], table[1, b], table[2, b]
            nodes = own_nodes(first_y, length)
            for pair in range(2):
                x, valid = box_planes(first_x, pair, depth)
                for c in range(comps):
                    found, mask = gather_pair(
                        padded, ((c, x[0]), (c, x[1])), valid, nodes, TOP + first_y, first_z, slot
                    )
                    parts[pair][c] = jnp.where(mask, found, parts[pair][c])
        for pair in range(2):
            box_table[group, 8 * pair : 8 * pair + 8, :] = align_pair(flatten_pair(parts[pair]))
        return 0

    lax.fori_loop(0, (live[0] + GROUP - 1) // GROUP, one_group, 0)


def halo_boxes_kernel(table, live, near, far, partial, box_table, halo, hits, *, length):
    comps, depth = near.shape[:2]
    bins = table.shape[1]
    found = jnp.int32(0)
    for b in range(bins):
        hits[found] = b
        crossing = (table[1, b] < 0) | (table[1, b] > length - 4)
        found = found + (crossing & (b < live[0])).astype(jnp.int32)
    box_table[...] = partial[...]
    fill_halo(halo, near, far, range(depth))

    def one_bin(n, _):
        b = hits[n]
        first_x, first_y, first_z = table[0, b], table[1, b], table[2, b]
        nodes = jnp.logical_not(own_nodes(first_y, length))
        for pair in range(2):
            x, valid = box_planes(first_x, pair, depth)
            parts = []
            for c in range(comps):
                rows, mask = gather_pair(
                    halo,
                    ((c, x[0]), (c, x[1])),
                    valid,
                    nodes,
                    halo_row(first_y, length),
                    first_z,
                    b % GROUP,
                )
                parts.append(jnp.where(mask, rows, 0.0))
            box_table[b // GROUP, 8 * pair : 8 * pair + 8, :] += align_pair(flatten_pair(parts))
        return 0

    lax.fori_loop(0, found, one_bin, 0)


def answers_kernel(near_table, far_table, padded, near, far, near_out, far_out, halo, acc, hits, crossing_hits):
    comps, depth, _, rows, _ = padded.shape
    length = rows - 2 * TOP
    bins = near_table.shape[1]
    groups = bins // GROUP
    even = lax.axis_index("slab") % 2 == 0
    acc[...] = jnp.zeros_like(acc)
    edge = [0, 1, depth - 2, depth - 1]
    found, crossing_found = jnp.int32(0), jnp.int32(0)
    for side, table in enumerate((near_table, far_table)):
        above = even if side == 0 else jnp.logical_not(even)
        for b in range(bins):
            first_x, first_y = table[0, b], table[1, b]
            wanted = jnp.where(above, first_x < 0, first_x > depth - 4)
            crossing = wanted & ((first_y < 0) | (first_y > length - 4))
            hits[found] = side * bins + b
            crossing_hits[crossing_found] = side * bins + b
            found = found + wanted.astype(jnp.int32)
            crossing_found = crossing_found + crossing.astype(jnp.int32)
    fill_halo(halo, near, far, edge)

    def one_bin(entry, used, planes, in_halo):
        side, b = entry // bins, entry % bins
        first_x, first_y, first_z = [jnp.where(side == 0, near_table[d, b], far_table[d, b]) for d in range(3)]
        above = (side == 0) == even
        x = first_x + jnp.where(above, depth, 2 - depth)
        x = [x, x + 1]
        valid = [used & (at >= 0) & (at < depth) for at in x]
        x = [jnp.clip(at, 0, depth - 1) for at in x]
        nodes = own_nodes(first_y, length)
        first_row = TOP + first_y
        if in_halo:
            x = [jnp.where(at < 2, at, jnp.maximum(at - (depth - 4), 2)) for at in x]
            nodes = jnp.logical_not(nodes)
            first_row = halo_row(first_y, length)
        parts = []
        for c in range(comps):
            gathered, mask = gather_pair(planes, ((c, x[0]), (c, x[1])), valid, nodes, first_row, first_z, b % GROUP)
            parts.append(jnp.where(mask, gathered, 0.0))
        acc[side * groups + b // GROUP] += flatten_pair(parts)

    def some_bins(n, _):
        for k in range(ANSWERS):
            at = n * ANSWERS + k
            one_bin(hits[jnp.minimum(at, found - 1)], at < found, padded, False)
        return 0

    def crossing_bin(n, _):
        one_bin(crossing_hits[n], True, halo, True)
        return 0

    lax.fori_loop(0, (found + ANSWERS - 1) // ANSWERS, some_bins, 0)
    lax.fori_loop(0, crossing_found, crossing_bin, 0)
    for g in range(groups):
        near_out[g] = align_pair(acc[g])
        far_out[g] = align_pair(acc[groups + g])


def unscaled_weights(t):
    plus, minus, minus_two = t + 1.0, t - 1.0, t - 2.0
    inner, outer = t * minus, plus * minus_two
    return inner * minus_two, outer * minus, outer * t, inner * plus


def node_factor(node):
    return jnp.where(node == 0, -1.0 / 6.0, jnp.where(node == 1, 0.5, jnp.where(node == 2, -0.5, 1.0 / 6.0)))


def split(x):
    head = x.astype(jnp.bfloat16)
    return head, (x - head.astype(jnp.float32)).astype(jnp.bfloat16)


def group_matrix(box):
    row = lax.broadcasted_iota(jnp.int32, box.shape, 0)
    lane = lax.broadcasted_iota(jnp.int32, box.shape, 1)
    box = box * (node_factor(row // 4) * node_factor(lane // 4 % 4) * node_factor(lane % 4))
    box = jnp.take_along_axis(box, lane % GROUP * NODES + lane // GROUP, axis=1)
    head = box.astype(jnp.bfloat16).astype(jnp.float32)
    own = lax.broadcasted_iota(jnp.int32, (GROUP, LANES), 1) % GROUP == lax.broadcasted_iota(
        jnp.int32, (GROUP, LANES), 0
    )

    def spread(part):
        rows = [
            jnp.where(own, jnp.broadcast_to(part[4 * i + c : 4 * i + c + 1], (GROUP, LANES)), 0.0)
            for i in range(4)
            for c in range(3)
        ]
        return jnp.concatenate(rows, axis=0).astype(jnp.bfloat16)

    heads, tails = spread(head), spread(box - head)
    return jnp.concatenate([heads, heads, tails], axis=1)


def sample(matrix, position):
    along_x, along_y, along_z = (unscaled_weights(t) for t in position)
    weights = jnp.concatenate([y * z for y in along_y for z in along_z], axis=0)
    head, tail = split(weights)
    planes = jnp.dot(
        matrix, jnp.concatenate([head, tail, head], axis=0), preferred_element_type=jnp.float32
    )
    result = []
    for c in range(3):
        plane = [planes[8 * (3 * i + c) : 8 * (3 * i + c) + 8] for i in range(4)]
        result.append(
            (plane[0] * along_x[0] + plane[1] * along_x[1]) + (plane[2] * along_x[2] + plane[3] * along_x[3])
        )
    return result


def move_kernel(live, box_table, from_near, from_far, state, stokes, out):
    groups = box_table.shape[0]
    count = live[0]
    even = lax.axis_index("slab") % 2 == 0
    matrices, carry, rates, alive = [], [], [], []
    for g in range(groups):
        rows = slice(g * GROUP, (g + 1) * GROUP)
        lower, upper = jnp.where(even, from_far[g], from_near[g]), jnp.where(even, from_near[g], from_far[g])
        answers = jnp.concatenate([lower, upper], axis=0)
        matrices.append(group_matrix(box_table[g] + answers))
        rates.append(1.0 / stokes[rows, :])
        kept = g * GROUP + lax.broadcasted_iota(jnp.int32, rates[g].shape, 0) < count
        alive.append(kept)
        start = [jnp.where(kept, state[c, rows, :], 0.0) for c in range(6)]
        carry.append((start[:3], start[3:]))

    for _ in range(SUBSTEPS):
        moved = []
        for g in range(groups):
            position, velocity = carry[g]
            rate = rates[g]
            middle_pos = [x + 0.5 * STEP_SIZE * v for x, v in zip(position, velocity)]
            here = sample(matrices[g], position)
            there = sample(matrices[g], middle_pos)
            middle_vel = [v + 0.5 * STEP_SIZE * ((u - v) * rate) for u, v in zip(here, velocity)]
            moved.append(
                (
                    [x + STEP_SIZE * m for x, m in zip(position, middle_vel)],
                    [v + STEP_SIZE * (u - m) * rate for v, u, m in zip(velocity, there, middle_vel)],
                )
            )
        carry = moved
    for g in range(groups):
        rows = slice(g * GROUP, (g + 1) * GROUP)
        for c, value in enumerate([*carry[g][0], *carry[g][1]]):
            out[c, rows, :] = jnp.where(alive[g], value, state[c, rows, :])


def in_smem():
    return pl.BlockSpec(memory_space=pltpu.SMEM)


def in_vmem():
    return pl.BlockSpec(memory_space=pltpu.VMEM)


def exchange(near, far, axis):
    devices = lax.axis_size(axis)
    near_pairs = [(i, i ^ 1) for i in range(devices)]
    far_pairs = [(i, (i + 1 if i % 2 else i - 1) % devices) for i in range(devices)]
    return lax.ppermute(near, axis, near_pairs), lax.ppermute(far, axis, far_pairs)


def body(velocity_field, particle_state, stokes_time, box_base, live_bins):
    comps, depth, length, cells = velocity_field.shape
    bins = box_base.shape[0]
    tiles = cells // LANES
    groups = bins // GROUP
    table = box_base.T
    state = particle_state.transpose(1, 0, 2)
    block = pltpu.with_memory_space_constraint(velocity_field, pltpu.HBM)
    params = pltpu.CompilerParams(vmem_limit_bytes=VMEM_LIMIT)

    near_table, far_table = exchange(table, table, "slab")
    edge_rows = jax.ShapeDtypeStruct((comps, depth, 2, cells), jnp.float32)
    padded, near, far = pl.pallas_call(
        load_kernel,
        out_shape=(pltpu.VMEM((comps, depth, tiles, length + 2 * TOP, LANES), jnp.float32), edge_rows, edge_rows),
        in_specs=[pl.BlockSpec(memory_space=pl.ANY)],
        out_specs=(in_vmem(), in_vmem(), in_vmem()),
        scratch_shapes=[pltpu.SemaphoreType.DMA((tiles,))],
        compiler_params=params,
        cost_estimate=pl.CostEstimate(flops=1_000_000, bytes_accessed=4_000_000, transcendentals=0),
        name="load",
    )(block)
    near, far = exchange(near, far, "sub")

    box_tables = jax.ShapeDtypeStruct((groups, NODES, LANES), jnp.float32)
    box_table = pl.pallas_call(
        own_boxes_kernel,
        out_shape=box_tables,
        in_specs=[in_smem(), in_smem(), in_vmem()],
        out_specs=in_vmem(),
        compiler_params=params,
        cost_estimate=pl.CostEstimate(flops=1_000_000, bytes_accessed=8_000_000, transcendentals=0),
        name="own_boxes",
    )(table, live_bins, padded)

    answer = jax.ShapeDtypeStruct((groups, 8, LANES), jnp.float32)
    near_answer, far_answer = pl.pallas_call(
        answers_kernel,
        out_shape=(answer, answer),
        in_specs=[in_smem(), in_smem(), in_vmem(), in_vmem(), in_vmem()],
        out_specs=(in_vmem(), in_vmem()),
        scratch_shapes=[
            pltpu.VMEM((comps, 4, tiles, 16, LANES), jnp.float32),
            pltpu.VMEM((2 * groups, 8, LANES), jnp.float32),
            pltpu.SMEM((2 * bins + 1,), jnp.int32),
            pltpu.SMEM((2 * bins + 1,), jnp.int32),
        ],
        compiler_params=params,
        name="answers",
    )(near_table, far_table, padded, near, far)
    from_near, from_far = exchange(near_answer, far_answer, "slab")

    box_table = pl.pallas_call(
        functools.partial(halo_boxes_kernel, length=length),
        out_shape=box_tables,
        in_specs=[in_smem(), in_smem(), in_vmem(), in_vmem(), in_vmem()],
        out_specs=in_vmem(),
        scratch_shapes=[
            pltpu.VMEM((comps, depth, tiles, 16, LANES), jnp.float32),
            pltpu.SMEM((bins + 1,), jnp.int32),
        ],
        compiler_params=params,
        cost_estimate=pl.CostEstimate(flops=1_000_000, bytes_accessed=4_000_000, transcendentals=0),
        name="halo_boxes",
    )(table, live_bins, near, far, box_table)

    moved = pl.pallas_call(
        move_kernel,
        out_shape=jax.ShapeDtypeStruct(state.shape, jnp.float32),
        in_specs=[in_smem()] + [in_vmem()] * 5,
        out_specs=in_vmem(),
        compiler_params=params,
        name="move",
    )(live_bins, box_table, from_near, from_far, state, stokes_time)
    return moved.transpose(1, 0, 2)


def solution(mesh):
    placed = (
        P(None, "slab", "sub", None),
        P(("slab", "sub"), None, None),
        P(("slab", "sub"), None),
        P(("slab", "sub"), None),
        P(("slab", "sub")),
    )
    return jax.shard_map(
        body, mesh=mesh, in_specs=placed, out_specs=P(("slab", "sub"), None, None), check_vma=False
    )
```

```python
import functools

import jax
import jax.numpy as jnp
from jax import lax
from jax.experimental import pallas as pl
from jax.experimental.pallas import tpu as pltpu
from jax.sharding import PartitionSpec as P

SUBSTEPS = 4
STEP_SIZE = 0.2
LANES = 128
NODES = 16
GROUP = 8
TOP = 8
ANSWERS = 4
VMEM_LIMIT = 48 * 1024 * 1024


def rows_and_lanes():
    return lax.broadcasted_iota(jnp.int32, (8, LANES), 0), lax.broadcasted_iota(jnp.int32, (8, LANES), 1)


def gather_pair(planes, index, valid, nodes, first_row, first_z, slot):
    row, lane = rows_and_lanes()
    tiles = planes.shape[-3]
    tile, offset = first_z // LANES, first_z % LANES
    beside = (tile + 1) % tiles
    upper = row < 4
    first, second = index

    def load(at):
        return jnp.where(
            upper,
            planes[(*first, at, pl.ds(first_row, 8), slice(None))],
            planes[(*second, at, pl.ds(first_row - 4, 8), slice(None))],
        )

    rows = jnp.where(lane >= offset, load(tile), load(beside))
    rows = pltpu.roll(rows, (NODES * slot - first_z) & (LANES - 1), 1)
    wanted = jnp.where(upper, jnp.where(valid[0], 4 * slot, -1), jnp.where(valid[1], 4 * slot, -1))
    return rows, nodes & (lane // 4 == wanted)


def flatten_pair(parts):
    row, _ = rows_and_lanes()
    total = None
    for c, part in enumerate(parts):
        part = pltpu.roll(part, 0, 1, stride=4, stride_axis=0)
        part = part + pltpu.roll(part, 7, 0)
        part = part + pltpu.roll(part, 6, 0)
        part = jnp.where(row % 4 == 0, part, 0.0)
        part = pltpu.roll(part, c, 0) if c else part
        total = part if total is None else total + part
    return total


def align_pair(tile):
    row, _ = rows_and_lanes()
    return jnp.where(row < 4, tile, pltpu.roll(tile, LANES - NODES, 1))


def load_kernel(field, padded, near, far, sems):
    length, cells = field.shape[2:]
    even = lax.axis_index("sub") % 2 == 0

    def edge_copies(near_row, far_row):
        return [
            pltpu.make_async_copy(field.at[:, :, pl.ds(row, 2), :], into, sems.at[n])
            for n, (row, into) in enumerate(((near_row, near), (far_row, far)))
        ]

    @pl.when(even)
    def _():
        for copy in edge_copies(length - 2, 0):
            copy.start()

    @pl.when(jnp.logical_not(even))
    def _():
        for copy in edge_copies(0, length - 2):
            copy.start()

    copies = edge_copies(0, 0)
    for tile in range(cells // LANES):
        copy = pltpu.make_async_copy(
            field.at[:, :, :, pl.ds(tile * LANES, LANES)],
            padded.at[:, :, tile, pl.ds(TOP, length), :],
            sems.at[2 + tile],
        )
        copy.start()
        copies.append(copy)
    for copy in copies:
        copy.wait()


def fill_halo(halo, near, far, planes):
    even = lax.axis_index("sub") % 2 == 0
    near_row, far_row = jnp.where(even, 8, 6), jnp.where(even, 6, 8)
    for c in range(halo.shape[0]):
        for into, x in enumerate(planes):
            for tile in range(halo.shape[-3]):
                lanes = slice(tile * LANES, (tile + 1) * LANES)
                halo[c, into, tile, pl.ds(near_row, 2), :] = near[c, x, :, lanes]
                halo[c, into, tile, pl.ds(far_row, 2), :] = far[c, x, :, lanes]


def halo_row(first_y, length):
    return jnp.where(first_y < 0, 8 + first_y, 8 + first_y - length)


def own_nodes(first_y, length):
    row, _ = rows_and_lanes()
    node = row % 4 + first_y
    return (node >= 0) & (node < length)


def box_planes(first_x, pair, depth):
    x = [first_x + 2 * pair, first_x + 2 * pair + 1]
    return [jnp.clip(at, 0, depth - 1) for at in x], [(at >= 0) & (at < depth) for at in x]


def own_boxes_kernel(table, live, padded, box_table):
    comps, depth, _, rows, _ = padded.shape
    length = rows - 2 * TOP
    box_table[...] = jnp.zeros_like(box_table)

    def one_group(group, _):
        parts = [[jnp.zeros((8, LANES), jnp.float32)] * comps for _ in range(2)]
        for slot in range(GROUP):
            b = group * GROUP + slot
            first_x, first_y, first_z = table[0, b], table[1, b], table[2, b]
            nodes = own_nodes(first_y, length)
            for pair in range(2):
                x, valid = box_planes(first_x, pair, depth)
                for c in range(comps):
                    found, mask = gather_pair(
                        padded, ((c, x[0]), (c, x[1])), valid, nodes, TOP + first_y, first_z, slot
                    )
                    parts[pair][c] = jnp.where(mask, found, parts[pair][c])
        for pair in range(2):
            box_table[group, 8 * pair : 8 * pair + 8, :] = align_pair(flatten_pair(parts[pair]))
        return 0

    lax.fori_loop(0, (live[0] + GROUP - 1) // GROUP, one_group, 0)


def halo_boxes_kernel(table, live, far, near, partial, box_table, halo, hits, *, length):
    comps, depth = near.shape[:2]
    bins = table.shape[1]
    found = jnp.int32(0)
    for b in range(bins):
        hits[found] = b
        crossing = (table[1, b] < 0) | (table[1, b] > length - 4)
        found = found + (crossing & (b < live[0])).astype(jnp.int32)
    box_table[...] = partial[...]
    fill_halo(halo, near, far, range(depth))

    def one_bin(n, _):
        b = hits[n]
        first_x, first_y, first_z = table[0, b], table[1, b], table[2, b]
        nodes = jnp.logical_not(own_nodes(first_y, length))
        for pair in range(2):
            x, valid = box_planes(first_x, pair, depth)
            parts = []
            for c in range(comps):
                rows, mask = gather_pair(
                    halo,
                    ((c, x[0]), (c, x[1])),
                    valid,
                    nodes,
                    halo_row(first_y, length),
                    first_z,
                    b % GROUP,
                )
                parts.append(jnp.where(mask, rows, 0.0))
            box_table[b // GROUP, 8 * pair : 8 * pair + 8, :] += align_pair(flatten_pair(parts))
        return 0

    lax.fori_loop(0, found, one_bin, 0)


def answers_kernel(lower_table, upper_table, padded, far, near, upper_out, lower_out, halo, acc, hits, crossing_hits):
    comps, depth, _, rows, _ = padded.shape
    length = rows - 2 * TOP
    bins = upper_table.shape[1]
    groups = bins // GROUP
    acc[...] = jnp.zeros_like(acc)
    edge = [0, 1, depth - 2, depth - 1]
    found, crossing_found = jnp.int32(0), jnp.int32(0)
    for side, table in enumerate((upper_table, lower_table)):
        for b in range(bins):
            first_x, first_y = table[0, b], table[1, b]
            wanted = first_x > depth - 4 if side else first_x < 0
            crossing = wanted & ((first_y < 0) | (first_y > length - 4))
            hits[found] = side * bins + b
            crossing_hits[crossing_found] = side * bins + b
            found = found + wanted.astype(jnp.int32)
            crossing_found = crossing_found + crossing.astype(jnp.int32)
    fill_halo(halo, near, far, edge)

    def one_bin(entry, used, planes, in_halo):
        side, b = entry // bins, entry % bins
        first_x, first_y, first_z = [jnp.where(side == 0, upper_table[d, b], lower_table[d, b]) for d in range(3)]
        x = first_x + jnp.where(side == 0, depth, 2 - depth)
        x = [x, x + 1]
        valid = [used & (at >= 0) & (at < depth) for at in x]
        x = [jnp.clip(at, 0, depth - 1) for at in x]
        nodes = own_nodes(first_y, length)
        first_row = TOP + first_y
        if in_halo:
            x = [jnp.where(at < 2, at, jnp.maximum(at - (depth - 4), 2)) for at in x]
            nodes = jnp.logical_not(nodes)
            first_row = halo_row(first_y, length)
        parts = []
        for c in range(comps):
            gathered, mask = gather_pair(planes, ((c, x[0]), (c, x[1])), valid, nodes, first_row, first_z, b % GROUP)
            parts.append(jnp.where(mask, gathered, 0.0))
        acc[side * groups + b // GROUP] += flatten_pair(parts)

    def some_bins(n, _):
        for k in range(ANSWERS):
            at = n * ANSWERS + k
            one_bin(hits[jnp.minimum(at, found - 1)], at < found, padded, False)
        return 0

    def crossing_bin(n, _):
        one_bin(crossing_hits[n], True, halo, True)
        return 0

    lax.fori_loop(0, (found + ANSWERS - 1) // ANSWERS, some_bins, 0)
    lax.fori_loop(0, crossing_found, crossing_bin, 0)
    for g in range(groups):
        upper_out[g] = align_pair(acc[g])
        lower_out[g] = align_pair(acc[groups + g])


def unscaled_weights(t):
    plus, minus, minus_two = t + 1.0, t - 1.0, t - 2.0
    inner, outer = t * minus, plus * minus_two
    return inner * minus_two, outer * minus, outer * t, inner * plus


def node_factor(node):
    return jnp.where(node == 0, -1.0 / 6.0, jnp.where(node == 1, 0.5, jnp.where(node == 2, -0.5, 1.0 / 6.0)))


def split(x):
    head = x.astype(jnp.bfloat16)
    return head, (x - head.astype(jnp.float32)).astype(jnp.bfloat16)


def group_matrix(box):
    row = lax.broadcasted_iota(jnp.int32, box.shape, 0)
    lane = lax.broadcasted_iota(jnp.int32, box.shape, 1)
    box = box * (node_factor(row // 4) * node_factor(lane // 4 % 4) * node_factor(lane % 4))
    box = jnp.take_along_axis(box, lane % GROUP * NODES + lane // GROUP, axis=1)
    head = box.astype(jnp.bfloat16).astype(jnp.float32)
    own = lax.broadcasted_iota(jnp.int32, (GROUP, LANES), 1) % GROUP == lax.broadcasted_iota(
        jnp.int32, (GROUP, LANES), 0
    )

    def spread(part):
        rows = [
            jnp.where(own, jnp.broadcast_to(part[4 * i + c : 4 * i + c + 1], (GROUP, LANES)), 0.0)
            for i in range(4)
            for c in range(3)
        ]
        return jnp.concatenate(rows, axis=0).astype(jnp.bfloat16)

    heads, tails = spread(head), spread(box - head)
    return jnp.concatenate([heads, heads, tails], axis=1)


def sample(matrix, position):
    along_x, along_y, along_z = (unscaled_weights(t) for t in position)
    weights = jnp.concatenate([y * z for y in along_y for z in along_z], axis=0)
    head, tail = split(weights)
    planes = jnp.dot(
        matrix, jnp.concatenate([head, tail, head], axis=0), preferred_element_type=jnp.float32
    )
    result = []
    for c in range(3):
        plane = [planes[8 * (3 * i + c) : 8 * (3 * i + c) + 8] for i in range(4)]
        result.append(
            (plane[0] * along_x[0] + plane[1] * along_x[1]) + (plane[2] * along_x[2] + plane[3] * along_x[3])
        )
    return result


def move_kernel(live, box_table, from_lower, from_upper, state, stokes, out):
    groups = box_table.shape[0]
    count = live[0]
    matrices, carry, rates, alive = [], [], [], []
    for g in range(groups):
        rows = slice(g * GROUP, (g + 1) * GROUP)
        answers = jnp.concatenate([from_lower[g], from_upper[g]], axis=0)
        matrices.append(group_matrix(box_table[g] + answers))
        rates.append(1.0 / stokes[rows, :])
        kept = g * GROUP + lax.broadcasted_iota(jnp.int32, rates[g].shape, 0) < count
        alive.append(kept)
        start = [jnp.where(kept, state[c, rows, :], 0.0) for c in range(6)]
        carry.append((start[:3], start[3:]))

    for _ in range(SUBSTEPS):
        moved = []
        for g in range(groups):
            position, velocity = carry[g]
            rate = rates[g]
            middle_pos = [x + 0.5 * STEP_SIZE * v for x, v in zip(position, velocity)]
            here = sample(matrices[g], position)
            there = sample(matrices[g], middle_pos)
            middle_vel = [v + 0.5 * STEP_SIZE * ((u - v) * rate) for u, v in zip(here, velocity)]
            moved.append(
                (
                    [x + STEP_SIZE * m for x, m in zip(position, middle_vel)],
                    [v + STEP_SIZE * (u - m) * rate for v, u, m in zip(velocity, there, middle_vel)],
                )
            )
        carry = moved
    for g in range(groups):
        rows = slice(g * GROUP, (g + 1) * GROUP)
        for c, value in enumerate([*carry[g][0], *carry[g][1]]):
            out[c, rows, :] = jnp.where(alive[g], value, state[c, rows, :])


def in_smem():
    return pl.BlockSpec(memory_space=pltpu.SMEM)


def in_vmem():
    return pl.BlockSpec(memory_space=pltpu.VMEM)


def exchange(near, far, axis):
    devices = lax.axis_size(axis)
    near_pairs = [(i, i ^ 1) for i in range(devices)]
    far_pairs = [(i, (i + 1 if i % 2 else i - 1) % devices) for i in range(devices)]
    far = lax.ppermute(far, axis, far_pairs)
    return lax.ppermute(near, axis, near_pairs), far


def shift(array, axis, step):
    devices = lax.axis_size(axis)
    return lax.ppermute(array, axis, [(i, (i + step) % devices) for i in range(devices)])


def body(velocity_field, particle_state, stokes_time, box_base, live_bins):
    comps, depth, length, cells = velocity_field.shape
    bins = box_base.shape[0]
    tiles = cells // LANES
    groups = bins // GROUP
    table = box_base.T
    state = particle_state.transpose(1, 0, 2)
    block = pltpu.with_memory_space_constraint(velocity_field, pltpu.HBM)
    params = pltpu.CompilerParams(vmem_limit_bytes=VMEM_LIMIT)

    lower_table, upper_table = shift(table, "slab", 1), shift(table, "slab", -1)
    edge_rows = jax.ShapeDtypeStruct((comps, depth, 2, cells), jnp.float32)
    padded, near, far = pl.pallas_call(
        load_kernel,
        out_shape=(pltpu.VMEM((comps, depth, tiles, length + 2 * TOP, LANES), jnp.float32), edge_rows, edge_rows),
        in_specs=[pl.BlockSpec(memory_space=pl.ANY)],
        out_specs=(in_vmem(), in_vmem(), in_vmem()),
        scratch_shapes=[pltpu.SemaphoreType.DMA((2 + tiles,))],
        compiler_params=params,
        cost_estimate=pl.CostEstimate(flops=1_000_000, bytes_accessed=4_000_000, transcendentals=0),
        name="load",
    )(block)
    near, far = exchange(near, far, "sub")

    box_tables = jax.ShapeDtypeStruct((groups, NODES, LANES), jnp.float32)
    box_table = pl.pallas_call(
        own_boxes_kernel,
        out_shape=box_tables,
        in_specs=[in_smem(), in_smem(), in_vmem()],
        out_specs=in_vmem(),
        compiler_params=params,
        cost_estimate=pl.CostEstimate(flops=1_000_000, bytes_accessed=8_000_000, transcendentals=0),
        name="own_boxes",
    )(table, live_bins, padded)

    answer = jax.ShapeDtypeStruct((groups, 8, LANES), jnp.float32)
    for_upper, for_lower = pl.pallas_call(
        answers_kernel,
        out_shape=(answer, answer),
        in_specs=[in_smem(), in_smem(), in_vmem(), in_vmem(), in_vmem()],
        out_specs=(in_vmem(), in_vmem()),
        scratch_shapes=[
            pltpu.VMEM((comps, 4, tiles, 16, LANES), jnp.float32),
            pltpu.VMEM((2 * groups, 8, LANES), jnp.float32),
            pltpu.SMEM((2 * bins + 1,), jnp.int32),
            pltpu.SMEM((2 * bins + 1,), jnp.int32),
        ],
        compiler_params=params,
        name="answers",
    )(lower_table, upper_table, padded, far, near)
    from_lower, from_upper = shift(for_upper, "slab", 1), shift(for_lower, "slab", -1)

    box_table = pl.pallas_call(
        functools.partial(halo_boxes_kernel, length=length),
        out_shape=box_tables,
        in_specs=[in_smem(), in_smem(), in_vmem(), in_vmem(), in_vmem()],
        out_specs=in_vmem(),
        scratch_shapes=[
            pltpu.VMEM((comps, depth, tiles, 16, LANES), jnp.float32),
            pltpu.SMEM((bins + 1,), jnp.int32),
        ],
        compiler_params=params,
        cost_estimate=pl.CostEstimate(flops=1_000_000, bytes_accessed=4_000_000, transcendentals=0),
        name="halo_boxes",
    )(table, live_bins, far, near, box_table)

    moved = pl.pallas_call(
        move_kernel,
        out_shape=jax.ShapeDtypeStruct(state.shape, jnp.float32),
        in_specs=[in_smem()] + [in_vmem()] * 5,
        out_specs=in_vmem(),
        compiler_params=params,
        name="move",
    )(live_bins, box_table, from_lower, from_upper, state, stokes_time)
    return moved.transpose(1, 0, 2)


def solution(mesh):
    placed = (
        P(None, "slab", "sub", None),
        P(("slab", "sub"), None, None),
        P(("slab", "sub"), None),
        P(("slab", "sub"), None),
        P(("slab", "sub")),
    )
    return jax.shard_map(
        body, mesh=mesh, in_specs=placed, out_specs=P(("slab", "sub"), None, None), check_vma=False
    )
```

```python
import functools

import jax
import jax.numpy as jnp
from jax import lax
from jax.experimental import pallas as pl
from jax.experimental.pallas import tpu as pltpu
from jax.sharding import PartitionSpec as P

SUBSTEPS = 4
STEP_SIZE = 0.2
LANES = 128
NODES = 16
GROUP = 8
TOP = 8
UNROLL = 4
VMEM_LIMIT = 48 * 1024 * 1024


def rows_and_lanes():
    return lax.broadcasted_iota(jnp.int32, (8, LANES), 0), lax.broadcasted_iota(jnp.int32, (8, LANES), 1)


def gather_pair(planes, index, valid, nodes, first_row, first_z, slot):
    row, lane = rows_and_lanes()
    tiles = planes.shape[-3]
    tile, offset = first_z // LANES, first_z % LANES
    beside = (tile + 1) % tiles
    upper = row < 4
    first, second = index

    def load(at):
        return jnp.where(
            upper,
            planes[(*first, at, pl.ds(first_row, 8), slice(None))],
            planes[(*second, at, pl.ds(first_row - 4, 8), slice(None))],
        )

    rows = jnp.where(lane >= offset, load(tile), load(beside))
    rows = pltpu.roll(rows, (NODES * slot - first_z) & (LANES - 1), 1)
    wanted = jnp.where(upper, jnp.where(valid[0], 4 * slot, -1), jnp.where(valid[1], 4 * slot, -1))
    return rows, nodes & (lane // 4 == wanted)


def flatten_pair(parts):
    row, _ = rows_and_lanes()
    total = None
    for c, part in enumerate(parts):
        part = pltpu.roll(part, 0, 1, stride=4, stride_axis=0)
        part = part + pltpu.roll(part, 7, 0)
        part = part + pltpu.roll(part, 6, 0)
        part = jnp.where(row % 4 == 0, part, 0.0)
        part = pltpu.roll(part, c, 0) if c else part
        total = part if total is None else total + part
    return total


def align_pair(tile):
    row, _ = rows_and_lanes()
    return jnp.where(row < 4, tile, pltpu.roll(tile, LANES - NODES, 1))


def load_kernel(field, base, padded, near, far, table, sems):
    length, cells = field.shape[2:]
    even = lax.axis_index("sub") % 2 == 0

    def edge_copies(near_row, far_row):
        return [
            pltpu.make_async_copy(field.at[:, :, pl.ds(row, 2), :], into, sems.at[n])
            for n, (row, into) in enumerate(((near_row, near), (far_row, far)))
        ]

    @pl.when(even)
    def _():
        for copy in edge_copies(length - 2, 0):
            copy.start()

    @pl.when(jnp.logical_not(even))
    def _():
        for copy in edge_copies(0, length - 2):
            copy.start()

    copies = edge_copies(0, 0)
    copy = pltpu.make_async_copy(base, table, sems.at[2])
    copy.start()
    copies.append(copy)
    for tile in range(cells // LANES):
        copy = pltpu.make_async_copy(
            field.at[:, :, :, pl.ds(tile * LANES, LANES)],
            padded.at[:, :, tile, pl.ds(TOP, length), :],
            sems.at[3 + tile],
        )
        copy.start()
        copies.append(copy)
    for copy in copies:
        copy.wait()


def fill_halo(padded, far, near, planes):
    comps, _, tiles, rows, _ = padded.shape
    even = lax.axis_index("sub") % 2 == 0
    below, above = TOP - 2, rows - TOP
    near_row, far_row = jnp.where(even, above, below), jnp.where(even, below, above)
    for c in range(comps):
        for x in planes:
            for tile in range(tiles):
                lanes = slice(tile * LANES, (tile + 1) * LANES)
                padded[c, x, tile, pl.ds(near_row, 2), :] = near[c, x, :, lanes]
                padded[c, x, tile, pl.ds(far_row, 2), :] = far[c, x, :, lanes]


def own_nodes(first_y, length):
    row, _ = rows_and_lanes()
    node = row % 4 + first_y
    return (node >= 0) & (node < length)


def box_planes(first_x, pair, depth):
    x = [first_x + 2 * pair, first_x + 2 * pair + 1]
    return [jnp.clip(at, 0, depth - 1) for at in x], [(at >= 0) & (at < depth) for at in x]


def own_boxes_kernel(table, live, padded, box_table):
    comps, depth, _, rows, _ = padded.shape
    length = rows - 2 * TOP
    box_table[...] = jnp.zeros_like(box_table)

    def one_group(group, _):
        parts = [[jnp.zeros((8, LANES), jnp.float32)] * comps for _ in range(2)]
        for slot in range(GROUP):
            b = group * GROUP + slot
            first_x, first_y, first_z = table[0, b], table[1, b], table[2, b]
            nodes = own_nodes(first_y, length)
            for pair in range(2):
                x, valid = box_planes(first_x, pair, depth)
                for c in range(comps):
                    found, mask = gather_pair(
                        padded, ((c, x[0]), (c, x[1])), valid, nodes, TOP + first_y, first_z, slot
                    )
                    parts[pair][c] = jnp.where(mask, found, parts[pair][c])
        for pair in range(2):
            box_table[group, 8 * pair : 8 * pair + 8, :] = align_pair(flatten_pair(parts[pair]))
        return 0

    lax.fori_loop(0, (live[0] + GROUP - 1) // GROUP, one_group, 0)


def halo_boxes_kernel(table, live, far, near, partial, padded_in, box_table, padded, hits):
    comps, depth, _, rows, _ = padded.shape
    length = rows - 2 * TOP
    bins = table.shape[1]
    found = jnp.int32(0)
    for b in range(bins):
        hits[found] = b
        crossing = (table[1, b] < 0) | (table[1, b] > length - 4)
        found = found + (crossing & (b < live[0])).astype(jnp.int32)
    box_table[...] = partial[...]
    fill_halo(padded, far, near, range(2, depth - 2))

    def some_bins(n, _):
        for k in range(UNROLL):
            at = n * UNROLL + k
            b = hits[jnp.minimum(at, found - 1)]
            first_x, first_y, first_z = table[0, b], table[1, b], table[2, b]
            nodes = jnp.logical_not(own_nodes(first_y, length))
            for pair in range(2):
                x, valid = box_planes(first_x, pair, depth)
                valid = [v & (at < found) for v in valid]
                parts = []
                for c in range(comps):
                    gathered, mask = gather_pair(
                        padded, ((c, x[0]), (c, x[1])), valid, nodes, TOP + first_y, first_z, b % GROUP
                    )
                    parts.append(jnp.where(mask, gathered, 0.0))
                box_table[b // GROUP, 8 * pair : 8 * pair + 8, :] += align_pair(flatten_pair(parts))
        return 0

    lax.fori_loop(0, (found + UNROLL - 1) // UNROLL, some_bins, 0)


def answers_kernel(upper_table, lower_table, padded_in, far, near, before, upper_out, lower_out, padded, acc, hits):
    comps, depth, _, rows, _ = padded.shape
    bins = lower_table.shape[1]
    groups = bins // GROUP
    fill_halo(padded, far, near, [0, 1, depth - 2, depth - 1])
    acc[...] = jnp.zeros_like(acc)
    found = jnp.int32(0)
    for side, table in enumerate((upper_table, lower_table)):
        for b in range(bins):
            hits[found] = side * bins + b
            wanted = table[0, b] > depth - 4 if side else table[0, b] < 0
            found = found + wanted.astype(jnp.int32)

    def some_bins(n, _):
        for k in range(UNROLL):
            at = n * UNROLL + k
            entry = hits[jnp.minimum(at, found - 1)]
            side, b = entry // bins, entry % bins
            first_x, first_y, first_z = [jnp.where(side == 0, upper_table[d, b], lower_table[d, b]) for d in range(3)]
            x = first_x + jnp.where(side == 0, depth, 2 - depth)
            x = [x, x + 1]
            valid = [(at < found) & (cell >= 0) & (cell < depth) for cell in x]
            x = [jnp.clip(cell, 0, depth - 1) for cell in x]
            parts = []
            for c in range(comps):
                gathered, mask = gather_pair(
                    padded, ((c, x[0]), (c, x[1])), valid, True, TOP + first_y, first_z, b % GROUP
                )
                parts.append(jnp.where(mask, gathered, 0.0))
            acc[side * groups + b // GROUP] += flatten_pair(parts)
        return 0

    lax.fori_loop(0, (found + UNROLL - 1) // UNROLL, some_bins, 0)
    for g in range(groups):
        upper_out[g] = align_pair(acc[g])
        lower_out[g] = align_pair(acc[groups + g])


def unscaled_weights(t):
    plus, minus, minus_two = t + 1.0, t - 1.0, t - 2.0
    inner, outer = t * minus, plus * minus_two
    return inner * minus_two, outer * minus, outer * t, inner * plus


def node_factor(node):
    return jnp.where(node == 0, -1.0 / 6.0, jnp.where(node == 1, 0.5, jnp.where(node == 2, -0.5, 1.0 / 6.0)))


def split(x):
    head = x.astype(jnp.bfloat16)
    return head, (x - head.astype(jnp.float32)).astype(jnp.bfloat16)


def group_matrix(box):
    row = lax.broadcasted_iota(jnp.int32, box.shape, 0)
    lane = lax.broadcasted_iota(jnp.int32, box.shape, 1)
    box = box * (node_factor(row // 4) * node_factor(lane // 4 % 4) * node_factor(lane % 4))
    box = jnp.take_along_axis(box, lane % GROUP * NODES + lane // GROUP, axis=1)
    head = box.astype(jnp.bfloat16).astype(jnp.float32)
    own = lax.broadcasted_iota(jnp.int32, (GROUP, LANES), 1) % GROUP == lax.broadcasted_iota(
        jnp.int32, (GROUP, LANES), 0
    )

    def spread(part):
        rows = [
            jnp.where(own, jnp.broadcast_to(part[4 * i + c : 4 * i + c + 1], (GROUP, LANES)), 0.0)
            for i in range(4)
            for c in range(3)
        ]
        return jnp.concatenate(rows, axis=0).astype(jnp.bfloat16)

    heads, tails = spread(head), spread(box - head)
    return jnp.concatenate([heads, heads, tails], axis=1)


def sample(matrix, position):
    along_x, along_y, along_z = (unscaled_weights(t) for t in position)
    weights = jnp.concatenate([y * z for y in along_y for z in along_z], axis=0)
    head, tail = split(weights)
    planes = jnp.dot(
        matrix, jnp.concatenate([head, tail, head], axis=0), preferred_element_type=jnp.float32
    )
    result = []
    for c in range(3):
        plane = [planes[8 * (3 * i + c) : 8 * (3 * i + c) + 8] for i in range(4)]
        result.append(
            (plane[0] * along_x[0] + plane[1] * along_x[1]) + (plane[2] * along_x[2] + plane[3] * along_x[3])
        )
    return result


def move_kernel(live, box_table, from_lower, from_upper, state, stokes, out):
    groups = box_table.shape[0]
    count = live[0]
    matrices, carry, rates, alive = [], [], [], []
    for g in range(groups):
        rows = slice(g * GROUP, (g + 1) * GROUP)
        answers = jnp.concatenate([from_lower[g], from_upper[g]], axis=0)
        matrices.append(group_matrix(box_table[g] + answers))
        rates.append(1.0 / stokes[rows, :])
        kept = g * GROUP + lax.broadcasted_iota(jnp.int32, rates[g].shape, 0) < count
        alive.append(kept)
        start = [jnp.where(kept, state[c, rows, :], 0.0) for c in range(6)]
        carry.append((start[:3], start[3:]))

    for _ in range(SUBSTEPS):
        moved = []
        for g in range(groups):
            position, velocity = carry[g]
            rate = rates[g]
            middle_pos = [x + 0.5 * STEP_SIZE * v for x, v in zip(position, velocity)]
            here = sample(matrices[g], position)
            there = sample(matrices[g], middle_pos)
            middle_vel = [v + 0.5 * STEP_SIZE * ((u - v) * rate) for u, v in zip(here, velocity)]
            moved.append(
                (
                    [x + STEP_SIZE * m for x, m in zip(position, middle_vel)],
                    [v + STEP_SIZE * (u - m) * rate for v, u, m in zip(velocity, there, middle_vel)],
                )
            )
        carry = moved
    for g in range(groups):
        rows = slice(g * GROUP, (g + 1) * GROUP)
        for c, value in enumerate([*carry[g][0], *carry[g][1]]):
            out[c, rows, :] = jnp.where(alive[g], value, state[c, rows, :])


def in_smem():
    return pl.BlockSpec(memory_space=pltpu.SMEM)


def in_vmem():
    return pl.BlockSpec(memory_space=pltpu.VMEM)


def exchange(near, far, axis):
    devices = lax.axis_size(axis)
    near_pairs = [(i, i ^ 1) for i in range(devices)]
    far_pairs = [(i, (i + 1 if i % 2 else i - 1) % devices) for i in range(devices)]
    far = lax.ppermute(far, axis, far_pairs)
    return lax.ppermute(near, axis, near_pairs), far


def shift(array, axis, step):
    devices = lax.axis_size(axis)
    return lax.ppermute(array, axis, [(i, (i + step) % devices) for i in range(devices)])


def body(velocity_field, particle_state, stokes_time, box_base, live_bins):
    comps, depth, length, cells = velocity_field.shape
    bins = box_base.shape[0]
    tiles = cells // LANES
    groups = bins // GROUP
    table = box_base.T
    state = particle_state.transpose(1, 0, 2)
    block = pltpu.with_memory_space_constraint(velocity_field, pltpu.HBM)
    params = pltpu.CompilerParams(vmem_limit_bytes=VMEM_LIMIT)

    lower_table, upper_table = shift(table, "slab", 1), shift(table, "slab", -1)
    padded_block = pltpu.VMEM((comps, depth, tiles, length + 2 * TOP, LANES), jnp.float32)
    edge_rows = jax.ShapeDtypeStruct((comps, depth, 2, cells), jnp.float32)
    padded, near, far, own_table = pl.pallas_call(
        load_kernel,
        out_shape=(
            padded_block,
            edge_rows,
            edge_rows,
            pltpu.SMEM(table.shape, jnp.int32),
        ),
        in_specs=[pl.BlockSpec(memory_space=pl.ANY)] * 2,
        out_specs=(in_vmem(), in_vmem(), in_vmem(), in_smem()),
        scratch_shapes=[pltpu.SemaphoreType.DMA((3 + tiles,))],
        compiler_params=params,
        name="load",
    )(block, pltpu.with_memory_space_constraint(table, pltpu.HBM))
    near, far = exchange(near, far, "sub")

    box_tables = jax.ShapeDtypeStruct((groups, NODES, LANES), jnp.float32)
    box_table = pl.pallas_call(
        own_boxes_kernel,
        out_shape=box_tables,
        in_specs=[in_smem(), in_smem(), in_vmem()],
        out_specs=in_vmem(),
        compiler_params=params,
        cost_estimate=pl.CostEstimate(flops=1_000_000, bytes_accessed=8_000_000, transcendentals=0),
        name="own_boxes",
    )(own_table, live_bins, padded)

    answer = jax.ShapeDtypeStruct((groups, 8, LANES), jnp.float32)
    for_upper, for_lower, padded = pl.pallas_call(
        answers_kernel,
        out_shape=(answer, answer, padded_block),
        in_specs=[in_smem(), in_smem(), in_vmem(), in_vmem(), in_vmem(), pl.BlockSpec(memory_space=pl.ANY)],
        out_specs=(in_vmem(), in_vmem(), in_vmem()),
        scratch_shapes=[pltpu.VMEM((2 * groups, 8, LANES), jnp.float32), pltpu.SMEM((2 * bins + 1,), jnp.int32)],
        input_output_aliases={2: 2},
        compiler_params=params,
        name="answers",
    )(upper_table, lower_table, padded, far, near, box_table)
    from_lower, from_upper = shift(for_upper, "slab", 1), shift(for_lower, "slab", -1)

    box_table, _ = pl.pallas_call(
        halo_boxes_kernel,
        out_shape=(box_tables, padded_block),
        in_specs=[in_smem(), in_smem(), in_vmem(), in_vmem(), in_vmem(), in_vmem()],
        out_specs=(in_vmem(), in_vmem()),
        scratch_shapes=[pltpu.SMEM((bins + 1,), jnp.int32)],
        input_output_aliases={5: 1},
        compiler_params=params,
        cost_estimate=pl.CostEstimate(flops=1_000_000, bytes_accessed=4_000_000, transcendentals=0),
        name="halo_boxes",
    )(own_table, live_bins, far, near, box_table, padded)

    moved = pl.pallas_call(
        move_kernel,
        out_shape=jax.ShapeDtypeStruct(state.shape, jnp.float32),
        in_specs=[in_smem()] + [in_vmem()] * 5,
        out_specs=in_vmem(),
        compiler_params=params,
        name="move",
    )(live_bins, box_table, from_lower, from_upper, state, stokes_time)
    return moved.transpose(1, 0, 2)


def solution(mesh):
    placed = (
        P(None, "slab", "sub", None),
        P(("slab", "sub"), None, None),
        P(("slab", "sub"), None),
        P(("slab", "sub"), None),
        P(("slab", "sub")),
    )
    return jax.shard_map(
        body, mesh=mesh, in_specs=placed, out_specs=P(("slab", "sub"), None, None), check_vma=False
    )
```

```python
import functools

import jax
import jax.numpy as jnp
from jax import lax
from jax.experimental import pallas as pl
from jax.experimental.pallas import tpu as pltpu
from jax.sharding import PartitionSpec as P

SUBSTEPS = 4
STEP_SIZE = 0.2
LANES = 128
LANE_BITS = 7
NODES = 16
GROUP = 8
GROUP_BITS = 3
TOP = 8
UNROLL = 4
VMEM_LIMIT = 48 * 1024 * 1024


def rows_and_lanes():
    return lax.broadcasted_iota(jnp.int32, (8, LANES), 0), lax.broadcasted_iota(jnp.int32, (8, LANES), 1)


def gather_pair(planes, index, valid, nodes, first_row, first_z, slot):
    row, lane = rows_and_lanes()
    tiles = planes.shape[-3]
    tile, offset = lax.shift_right_logical(first_z, LANE_BITS), first_z & (LANES - 1)
    beside = jnp.where(tile == tiles - 1, 0, tile + 1)
    upper = row < 4
    first, second = index

    def load(at):
        return jnp.where(
            upper,
            planes[(*first, at, pl.ds(first_row, 8), slice(None))],
            planes[(*second, at, pl.ds(first_row - 4, 8), slice(None))],
        )

    rows = jnp.where(lane >= offset, load(tile), load(beside))
    rows = pltpu.roll(rows, (NODES * slot - first_z) & (LANES - 1), 1)
    wanted = jnp.where(upper, jnp.where(valid[0], 4 * slot, -1), jnp.where(valid[1], 4 * slot, -1))
    return rows, nodes & (lax.shift_right_logical(lane, 2) == wanted)


def flatten_pair(parts):
    row, _ = rows_and_lanes()
    total = None
    for c, part in enumerate(parts):
        part = pltpu.roll(part, 0, 1, stride=4, stride_axis=0)
        part = part + pltpu.roll(part, 7, 0)
        part = part + pltpu.roll(part, 6, 0)
        part = jnp.where((row & 3) == 0, part, 0.0)
        part = pltpu.roll(part, c, 0) if c else part
        total = part if total is None else total + part
    return total


def align_pair(tile):
    row, _ = rows_and_lanes()
    return jnp.where(row < 4, tile, pltpu.roll(tile, LANES - NODES, 1))


def load_kernel(field, base, padded, near, far, table, sems):
    length, cells = field.shape[2:]
    even = lax.axis_index("sub") % 2 == 0

    def edge_copies(near_row, far_row):
        return [
            pltpu.make_async_copy(field.at[:, :, pl.ds(row, 2), :], into, sems.at[n])
            for n, (row, into) in enumerate(((near_row, near), (far_row, far)))
        ]

    @pl.when(even)
    def _():
        for copy in edge_copies(length - 2, 0):
            copy.start()

    @pl.when(jnp.logical_not(even))
    def _():
        for copy in edge_copies(0, length - 2):
            copy.start()

    copies = edge_copies(0, 0)
    copy = pltpu.make_async_copy(base, table, sems.at[2])
    copy.start()
    copies.append(copy)
    for tile in range(cells // LANES):
        copy = pltpu.make_async_copy(
            field.at[:, :, :, pl.ds(tile * LANES, LANES)],
            padded.at[:, :, tile, pl.ds(TOP, length), :],
            sems.at[3 + tile],
        )
        copy.start()
        copies.append(copy)
    for copy in copies:
        copy.wait()


def fill_halo(padded, far, near, planes):
    comps, _, tiles, rows, _ = padded.shape
    even = lax.axis_index("sub") % 2 == 0
    below, above = TOP - 2, rows - TOP
    near_row, far_row = jnp.where(even, above, below), jnp.where(even, below, above)
    for c in range(comps):
        for x in planes:
            for tile in range(tiles):
                lanes = slice(tile * LANES, (tile + 1) * LANES)
                padded[c, x, tile, pl.ds(near_row, 2), :] = near[c, x, :, lanes]
                padded[c, x, tile, pl.ds(far_row, 2), :] = far[c, x, :, lanes]


def own_nodes(first_y, length):
    row, _ = rows_and_lanes()
    node = (row & 3) + first_y
    return (node >= 0) & (node < length)


def box_planes(first_x, pair, depth):
    x = [first_x + 2 * pair, first_x + 2 * pair + 1]
    return [jnp.clip(at, 0, depth - 1) for at in x], [(at >= 0) & (at < depth) for at in x]


def own_boxes_kernel(table, live, padded, box_table):
    comps, depth, _, rows, _ = padded.shape
    length = rows - 2 * TOP
    box_table[...] = jnp.zeros_like(box_table)

    def one_group(group, _):
        parts = [[jnp.zeros((8, LANES), jnp.float32)] * comps for _ in range(2)]
        for slot in range(GROUP):
            b = group * GROUP + slot
            first_x, first_y, first_z = table[0, b], table[1, b], table[2, b]
            nodes = own_nodes(first_y, length)
            for pair in range(2):
                x, valid = box_planes(first_x, pair, depth)
                for c in range(comps):
                    found, mask = gather_pair(
                        padded, ((c, x[0]), (c, x[1])), valid, nodes, TOP + first_y, first_z, slot
                    )
                    parts[pair][c] = jnp.where(mask, found, parts[pair][c])
        for pair in range(2):
            box_table[group, 8 * pair : 8 * pair + 8, :] = align_pair(flatten_pair(parts[pair]))
        return 0

    lax.fori_loop(0, (live[0] + GROUP - 1) // GROUP, one_group, 0)


def halo_boxes_kernel(table, live, far, near, partial, padded_in, box_table, padded, hits):
    comps, depth, _, rows, _ = padded.shape
    length = rows - 2 * TOP
    bins = table.shape[1]
    found = jnp.int32(0)
    for b in range(bins):
        hits[found] = b
        crossing = (table[1, b] < 0) | (table[1, b] > length - 4)
        found = found + (crossing & (b < live[0])).astype(jnp.int32)
    box_table[...] = partial[...]
    fill_halo(padded, far, near, range(2, depth - 2))

    def some_bins(n, _):
        for k in range(UNROLL):
            at = n * UNROLL + k
            b = hits[jnp.minimum(at, found - 1)]
            first_x, first_y, first_z = table[0, b], table[1, b], table[2, b]
            nodes = jnp.logical_not(own_nodes(first_y, length))
            for pair in range(2):
                x, valid = box_planes(first_x, pair, depth)
                valid = [v & (at < found) for v in valid]
                parts = []
                for c in range(comps):
                    gathered, mask = gather_pair(
                        padded, ((c, x[0]), (c, x[1])), valid, nodes, TOP + first_y, first_z, b & (GROUP - 1)
                    )
                    parts.append(jnp.where(mask, gathered, 0.0))
                box_table[lax.shift_right_logical(b, GROUP_BITS), 8 * pair : 8 * pair + 8, :] += align_pair(flatten_pair(parts))
        return 0

    lax.fori_loop(0, (found + UNROLL - 1) // UNROLL, some_bins, 0)


def answers_kernel(upper_table, lower_table, padded_in, far, near, before, upper_out, lower_out, padded, acc, hits):
    comps, depth, _, rows, _ = padded.shape
    bins = lower_table.shape[1]
    groups = bins // GROUP
    fill_halo(padded, far, near, [0, 1, depth - 2, depth - 1])
    acc[...] = jnp.zeros_like(acc)
    found = jnp.int32(0)
    for side, table in enumerate((upper_table, lower_table)):
        for b in range(bins):
            hits[found] = side * bins + b
            wanted = table[0, b] > depth - 4 if side else table[0, b] < 0
            found = found + wanted.astype(jnp.int32)

    def some_bins(n, _):
        for k in range(UNROLL):
            at = n * UNROLL + k
            entry = hits[jnp.minimum(at, found - 1)]
            from_upper = entry < bins
            b = jnp.where(from_upper, entry, entry - bins)
            first_x, first_y, first_z = [jnp.where(from_upper, upper_table[d, b], lower_table[d, b]) for d in range(3)]
            x = first_x + jnp.where(from_upper, depth, 2 - depth)
            x = [x, x + 1]
            valid = [(at < found) & (cell >= 0) & (cell < depth) for cell in x]
            x = [jnp.clip(cell, 0, depth - 1) for cell in x]
            parts = []
            for c in range(comps):
                gathered, mask = gather_pair(
                    padded, ((c, x[0]), (c, x[1])), valid, True, TOP + first_y, first_z, b & (GROUP - 1)
                )
                parts.append(jnp.where(mask, gathered, 0.0))
            group = lax.shift_right_logical(entry, GROUP_BITS)
            for c in range(comps):
                acc[group, c] += parts[c]
        return 0

    lax.fori_loop(0, (found + UNROLL - 1) // UNROLL, some_bins, 0)
    for g in range(groups):
        upper_out[g] = align_pair(flatten_pair([acc[g, c] for c in range(comps)]))
        lower_out[g] = align_pair(flatten_pair([acc[groups + g, c] for c in range(comps)]))


def unscaled_weights(t):
    plus, minus, minus_two = t + 1.0, t - 1.0, t - 2.0
    inner, outer = t * minus, plus * minus_two
    return inner * minus_two, outer * minus, outer * t, inner * plus


def node_factor(node):
    return jnp.where(node == 0, -1.0 / 6.0, jnp.where(node == 1, 0.5, jnp.where(node == 2, -0.5, 1.0 / 6.0)))


def split(x):
    head = x.astype(jnp.bfloat16)
    return head, (x - head.astype(jnp.float32)).astype(jnp.bfloat16)


def group_matrix(box):
    row = lax.broadcasted_iota(jnp.int32, box.shape, 0)
    lane = lax.broadcasted_iota(jnp.int32, box.shape, 1)
    box = box * (node_factor(row // 4) * node_factor(lane // 4 % 4) * node_factor(lane % 4))
    box = jnp.take_along_axis(box, lane % GROUP * NODES + lane // GROUP, axis=1)
    head = box.astype(jnp.bfloat16).astype(jnp.float32)
    own = lax.broadcasted_iota(jnp.int32, (GROUP, LANES), 1) % GROUP == lax.broadcasted_iota(
        jnp.int32, (GROUP, LANES), 0
    )

    def spread(part):
        rows = [
            jnp.where(own, jnp.broadcast_to(part[4 * i + c : 4 * i + c + 1], (GROUP, LANES)), 0.0)
            for i in range(4)
            for c in range(3)
        ]
        return jnp.concatenate(rows, axis=0).astype(jnp.bfloat16)

    heads, tails = spread(head), spread(box - head)
    return jnp.concatenate([heads, heads, tails], axis=1)


def sample(matrix, position):
    along_x, along_y, along_z = (unscaled_weights(t) for t in position)
    weights = jnp.concatenate([y * z for y in along_y for z in along_z], axis=0)
    head, tail = split(weights)
    planes = jnp.dot(
        matrix, jnp.concatenate([head, tail, head], axis=0), preferred_element_type=jnp.float32
    )
    result = []
    for c in range(3):
        plane = [planes[8 * (3 * i + c) : 8 * (3 * i + c) + 8] for i in range(4)]
        result.append(
            (plane[0] * along_x[0] + plane[1] * along_x[1]) + (plane[2] * along_x[2] + plane[3] * along_x[3])
        )
    return result


def move_groups(groups, count, box_table, from_lower, from_upper, state, stokes, out):
    matrices, carry, rates, alive = [], [], [], []
    for g in range(groups):
        rows = slice(g * GROUP, (g + 1) * GROUP)
        answers = jnp.concatenate([from_lower[g], from_upper[g]], axis=0)
        matrices.append(group_matrix(box_table[g] + answers))
        rates.append(1.0 / stokes[rows, :])
        kept = g * GROUP + lax.broadcasted_iota(jnp.int32, rates[g].shape, 0) < count
        alive.append(kept)
        start = [jnp.where(kept, state[c, rows, :], 0.0) for c in range(6)]
        carry.append((start[:3], start[3:]))
    for _ in range(SUBSTEPS):
        moved = []
        for g in range(groups):
            position, velocity = carry[g]
            rate = rates[g]
            middle_pos = [x + 0.5 * STEP_SIZE * v for x, v in zip(position, velocity)]
            here = sample(matrices[g], position)
            there = sample(matrices[g], middle_pos)
            middle_vel = [v + 0.5 * STEP_SIZE * ((u - v) * rate) for u, v in zip(here, velocity)]
            moved.append(
                (
                    [x + STEP_SIZE * m for x, m in zip(position, middle_vel)],
                    [v + STEP_SIZE * (u - m) * rate for v, u, m in zip(velocity, there, middle_vel)],
                )
            )
        carry = moved
    for g in range(groups):
        rows = slice(g * GROUP, (g + 1) * GROUP)
        for c, value in enumerate([*carry[g][0], *carry[g][1]]):
            out[c, rows, :] = jnp.where(alive[g], value, state[c, rows, :])
    if groups < box_table.shape[0]:
        out[:, groups * GROUP :, :] = state[:, groups * GROUP :, :]


def move_kernel(live, box_table, from_lower, from_upper, state, stokes, out):
    count = live[0]
    groups = box_table.shape[0]
    fewer = 0
    for some in sorted({1, max(1, groups // 2), groups}):

        @pl.when((count > fewer * GROUP) & (count <= some * GROUP))
        def _(some=some):
            move_groups(some, count, box_table, from_lower, from_upper, state, stokes, out)

        fewer = some


def in_smem():
    return pl.BlockSpec(memory_space=pltpu.SMEM)


def in_vmem():
    return pl.BlockSpec(memory_space=pltpu.VMEM)


def exchange(near, far, axis):
    devices = lax.axis_size(axis)
    near_pairs = [(i, i ^ 1) for i in range(devices)]
    far_pairs = [(i, (i + 1 if i % 2 else i - 1) % devices) for i in range(devices)]
    far = lax.ppermute(far, axis, far_pairs)
    return lax.ppermute(near, axis, near_pairs), far


def shift(array, axis, step):
    devices = lax.axis_size(axis)
    return lax.ppermute(array, axis, [(i, (i + step) % devices) for i in range(devices)])


def body(velocity_field, particle_state, stokes_time, box_base, live_bins):
    comps, depth, length, cells = velocity_field.shape
    bins = box_base.shape[0]
    tiles = cells // LANES
    groups = bins // GROUP
    table = box_base.T
    state = particle_state.transpose(1, 0, 2)
    block = pltpu.with_memory_space_constraint(velocity_field, pltpu.HBM)
    params = pltpu.CompilerParams(vmem_limit_bytes=VMEM_LIMIT)

    lower_table, upper_table = shift(table, "slab", 1), shift(table, "slab", -1)
    padded_block = pltpu.VMEM((comps, depth, tiles, length + 2 * TOP, LANES), jnp.float32)
    edge_rows = jax.ShapeDtypeStruct((comps, depth, 2, cells), jnp.float32)
    padded, near, far, own_table = pl.pallas_call(
        load_kernel,
        out_shape=(
            padded_block,
            edge_rows,
            edge_rows,
            pltpu.SMEM(table.shape, jnp.int32),
        ),
        in_specs=[pl.BlockSpec(memory_space=pl.ANY)] * 2,
        out_specs=(in_vmem(), in_vmem(), in_vmem(), in_smem()),
        scratch_shapes=[pltpu.SemaphoreType.DMA((3 + tiles,))],
        compiler_params=params,
        name="load",
    )(block, pltpu.with_memory_space_constraint(table, pltpu.HBM))
    near, far = exchange(near, far, "sub")

    box_tables = jax.ShapeDtypeStruct((groups, NODES, LANES), jnp.float32)
    box_table = pl.pallas_call(
        own_boxes_kernel,
        out_shape=box_tables,
        in_specs=[in_smem(), in_smem(), in_vmem()],
        out_specs=in_vmem(),
        compiler_params=params,
        cost_estimate=pl.CostEstimate(flops=1_000_000, bytes_accessed=8_000_000, transcendentals=0),
        name="own_boxes",
    )(own_table, live_bins, padded)

    answer = jax.ShapeDtypeStruct((groups, 8, LANES), jnp.float32)
    for_upper, for_lower, padded = pl.pallas_call(
        answers_kernel,
        out_shape=(answer, answer, padded_block),
        in_specs=[in_smem(), in_smem(), in_vmem(), in_vmem(), in_vmem(), pl.BlockSpec(memory_space=pl.ANY)],
        out_specs=(in_vmem(), in_vmem(), in_vmem()),
        scratch_shapes=[
            pltpu.VMEM((2 * groups, comps, 8, LANES), jnp.float32),
            pltpu.SMEM((2 * bins + 1,), jnp.int32),
        ],
        input_output_aliases={2: 2},
        compiler_params=params,
        name="answers",
    )(upper_table, lower_table, padded, far, near, box_table)
    from_lower, from_upper = shift(for_upper, "slab", 1), shift(for_lower, "slab", -1)

    box_table, _ = pl.pallas_call(
        halo_boxes_kernel,
        out_shape=(box_tables, padded_block),
        in_specs=[in_smem(), in_smem(), in_vmem(), in_vmem(), in_vmem(), in_vmem()],
        out_specs=(in_vmem(), in_vmem()),
        scratch_shapes=[pltpu.SMEM((bins + 1,), jnp.int32)],
        input_output_aliases={5: 1},
        compiler_params=params,
        cost_estimate=pl.CostEstimate(flops=1_000_000, bytes_accessed=4_000_000, transcendentals=0),
        name="halo_boxes",
    )(own_table, live_bins, far, near, box_table, padded)

    moved = pl.pallas_call(
        move_kernel,
        out_shape=jax.ShapeDtypeStruct(state.shape, jnp.float32),
        in_specs=[in_smem()] + [in_vmem()] * 5,
        out_specs=in_vmem(),
        compiler_params=params,
        name="move",
    )(live_bins, box_table, from_lower, from_upper, state, stokes_time)
    return moved.transpose(1, 0, 2)


def solution(mesh):
    placed = (
        P(None, "slab", "sub", None),
        P(("slab", "sub"), None, None),
        P(("slab", "sub"), None),
        P(("slab", "sub"), None),
        P(("slab", "sub")),
    )
    return jax.shard_map(
        body, mesh=mesh, in_specs=placed, out_specs=P(("slab", "sub"), None, None), check_vma=False
    )
```

```python
import functools

import jax
import jax.numpy as jnp
from jax import lax
from jax.experimental import pallas as pl
from jax.experimental.pallas import tpu as pltpu
from jax.sharding import PartitionSpec as P

SUBSTEPS = 4
STEP_SIZE = 0.2
LANES = 128
LANE_BITS = 7
NODES = 16
GROUP = 8
GROUP_BITS = 3
TOP = 8
UNROLL = 4
VMEM_LIMIT = 48 * 1024 * 1024


def rows_and_lanes():
    return lax.broadcasted_iota(jnp.int32, (8, LANES), 0), lax.broadcasted_iota(jnp.int32, (8, LANES), 1)


def gather_pair(planes, index, valid, first_row, first_z, slot):
    row, lane = rows_and_lanes()
    tiles = planes.shape[-3]
    tile, offset = lax.shift_right_logical(first_z, LANE_BITS), first_z & (LANES - 1)
    beside = jnp.where(tile == tiles - 1, 0, tile + 1)
    upper = row < 4
    first, second = index

    def load(at):
        return jnp.where(
            upper,
            planes[(*first, at, pl.ds(first_row, 8), slice(None))],
            planes[(*second, at, pl.ds(first_row - 4, 8), slice(None))],
        )

    rows = jnp.where(lane >= offset, load(tile), load(beside))
    rows = pltpu.roll(rows, (NODES * slot - first_z) & (LANES - 1), 1)
    wanted = jnp.where(upper, jnp.where(valid[0], 4 * slot, -1), jnp.where(valid[1], 4 * slot, -1))
    return rows, (lax.shift_right_logical(lane, 2) == wanted)


def flatten_pair(parts):
    row, _ = rows_and_lanes()
    total = None
    for c, part in enumerate(parts):
        part = pltpu.roll(part, 0, 1, stride=4, stride_axis=0)
        part = part + pltpu.roll(part, 7, 0)
        part = part + pltpu.roll(part, 6, 0)
        part = jnp.where((row & 3) == 0, part, 0.0)
        part = pltpu.roll(part, c, 0) if c else part
        total = part if total is None else total + part
    return total


def align_pair(tile):
    row, _ = rows_and_lanes()
    return jnp.where(row < 4, tile, pltpu.roll(tile, LANES - NODES, 1))


def edges_kernel(field, near, far, sems):
    length = field.shape[2]
    even = lax.axis_index("sub") % 2 == 0

    def edge_copies(near_row, far_row):
        return [
            pltpu.make_async_copy(field.at[:, :, pl.ds(row, 2), :], into, sems.at[n])
            for n, (row, into) in enumerate(((near_row, near), (far_row, far)))
        ]

    @pl.when(even)
    def _():
        for copy in edge_copies(length - 2, 0):
            copy.start()

    @pl.when(jnp.logical_not(even))
    def _():
        for copy in edge_copies(0, length - 2):
            copy.start()

    for copy in edge_copies(0, 0):
        copy.wait()


def load_kernel(field, base, padded, table, sems):
    length, cells = field.shape[2:]
    copies = [pltpu.make_async_copy(base, table, sems.at[0])]
    for tile in range(cells // LANES):
        copies.append(
            pltpu.make_async_copy(
                field.at[:, :, :, pl.ds(tile * LANES, LANES)],
                padded.at[:, :, tile, pl.ds(TOP, length), :],
                sems.at[1 + tile],
            )
        )
    for copy in copies:
        copy.start()
    for copy in copies:
        copy.wait()


def fill_halo(padded, far, near, planes):
    comps, _, tiles, rows, _ = padded.shape
    even = lax.axis_index("sub") % 2 == 0
    below, above = TOP - 2, rows - TOP
    near_row, far_row = jnp.where(even, above, below), jnp.where(even, below, above)
    for c in range(comps):
        for x in planes:
            for tile in range(tiles):
                lanes = slice(tile * LANES, (tile + 1) * LANES)
                padded[c, x, tile, pl.ds(near_row, 2), :] = near[c, x, :, lanes]
                padded[c, x, tile, pl.ds(far_row, 2), :] = far[c, x, :, lanes]


def box_planes(first_x, pair, depth):
    x = [first_x + 2 * pair, first_x + 2 * pair + 1]
    return [jnp.clip(at, 0, depth - 1) for at in x], [(at >= 0) & (at < depth) for at in x]


def boxes_kernel(table, live, far, near, padded_in, box_table, padded):
    comps, depth, _, rows, _ = padded.shape
    fill_halo(padded, far, near, range(2, depth - 2))
    box_table[...] = jnp.zeros_like(box_table)

    def one_group(group, _):
        parts = [[jnp.zeros((8, LANES), jnp.float32)] * comps for _ in range(2)]
        for slot in range(GROUP):
            b = group * GROUP + slot
            first_x, first_y, first_z = table[0, b], table[1, b], table[2, b]
            for pair in range(2):
                x, valid = box_planes(first_x, pair, depth)
                for c in range(comps):
                    found, mask = gather_pair(padded, ((c, x[0]), (c, x[1])), valid, TOP + first_y, first_z, slot)
                    parts[pair][c] = jnp.where(mask, found, parts[pair][c])
        for pair in range(2):
            box_table[group, 8 * pair : 8 * pair + 8, :] = align_pair(flatten_pair(parts[pair]))
        return 0

    lax.fori_loop(0, (live[0] + GROUP - 1) // GROUP, one_group, 0)


def answers_kernel(upper_table, lower_table, padded_in, far, near, upper_out, lower_out, padded, acc, hits):
    comps, depth, _, rows, _ = padded.shape
    bins = lower_table.shape[1]
    groups = bins // GROUP
    fill_halo(padded, far, near, [0, 1, depth - 2, depth - 1])
    acc[...] = jnp.zeros_like(acc)
    found = jnp.int32(0)
    for side, table in enumerate((upper_table, lower_table)):
        for b in range(bins):
            hits[found] = side * bins + b
            wanted = table[0, b] > depth - 4 if side else table[0, b] < 0
            found = found + wanted.astype(jnp.int32)

    def some_bins(n, _):
        for k in range(UNROLL):
            at = n * UNROLL + k
            entry = hits[jnp.minimum(at, found - 1)]
            from_upper = entry < bins
            b = jnp.where(from_upper, entry, entry - bins)
            first_x, first_y, first_z = [jnp.where(from_upper, upper_table[d, b], lower_table[d, b]) for d in range(3)]
            x = first_x + jnp.where(from_upper, depth, 2 - depth)
            x = [x, x + 1]
            valid = [(at < found) & (cell >= 0) & (cell < depth) for cell in x]
            x = [jnp.clip(cell, 0, depth - 1) for cell in x]
            parts = []
            for c in range(comps):
                gathered, mask = gather_pair(
                    padded, ((c, x[0]), (c, x[1])), valid, TOP + first_y, first_z, b & (GROUP - 1)
                )
                parts.append(jnp.where(mask, gathered, 0.0))
            group = lax.shift_right_logical(entry, GROUP_BITS)
            for c in range(comps):
                acc[group, c] += parts[c]
        return 0

    lax.fori_loop(0, (found + UNROLL - 1) // UNROLL, some_bins, 0)
    for g in range(groups):
        upper_out[g] = align_pair(flatten_pair([acc[g, c] for c in range(comps)]))
        lower_out[g] = align_pair(flatten_pair([acc[groups + g, c] for c in range(comps)]))


def unscaled_weights(t):
    plus, minus, minus_two = t + 1.0, t - 1.0, t - 2.0
    inner, outer = t * minus, plus * minus_two
    return inner * minus_two, outer * minus, outer * t, inner * plus


def node_factor(node):
    return jnp.where(node == 0, -1.0 / 6.0, jnp.where(node == 1, 0.5, jnp.where(node == 2, -0.5, 1.0 / 6.0)))


def split(x):
    head = x.astype(jnp.bfloat16)
    return head, (x - head.astype(jnp.float32)).astype(jnp.bfloat16)


def group_matrix(box):
    row = lax.broadcasted_iota(jnp.int32, box.shape, 0)
    lane = lax.broadcasted_iota(jnp.int32, box.shape, 1)
    box = box * (node_factor(row // 4) * node_factor(lane // 4 % 4) * node_factor(lane % 4))
    box = jnp.take_along_axis(box, lane % GROUP * NODES + lane // GROUP, axis=1)
    head = box.astype(jnp.bfloat16).astype(jnp.float32)
    own = lax.broadcasted_iota(jnp.int32, (GROUP, LANES), 1) % GROUP == lax.broadcasted_iota(
        jnp.int32, (GROUP, LANES), 0
    )

    def spread(part):
        rows = [
            jnp.where(own, jnp.broadcast_to(part[4 * i + c : 4 * i + c + 1], (GROUP, LANES)), 0.0)
            for i in range(4)
            for c in range(3)
        ]
        return jnp.concatenate(rows, axis=0).astype(jnp.bfloat16)

    heads, tails = spread(head), spread(box - head)
    return jnp.concatenate([heads, heads, tails], axis=1)


def sample(matrix, position):
    along_x, along_y, along_z = (unscaled_weights(t) for t in position)
    weights = jnp.concatenate([y * z for y in along_y for z in along_z], axis=0)
    head, tail = split(weights)
    planes = jnp.dot(
        matrix, jnp.concatenate([head, tail, head], axis=0), preferred_element_type=jnp.float32
    )
    result = []
    for c in range(3):
        plane = [planes[8 * (3 * i + c) : 8 * (3 * i + c) + 8] for i in range(4)]
        result.append(
            (plane[0] * along_x[0] + plane[1] * along_x[1]) + (plane[2] * along_x[2] + plane[3] * along_x[3])
        )
    return result


def move_groups(groups, count, box_table, from_lower, from_upper, state, stokes, out):
    matrices, carry, rates, alive = [], [], [], []
    for g in range(groups):
        rows = slice(g * GROUP, (g + 1) * GROUP)
        answers = jnp.concatenate([from_lower[g], from_upper[g]], axis=0)
        matrices.append(group_matrix(box_table[g] + answers))
        rates.append(1.0 / stokes[rows, :])
        kept = g * GROUP + lax.broadcasted_iota(jnp.int32, rates[g].shape, 0) < count
        alive.append(kept)
        start = [jnp.where(kept, state[c, rows, :], 0.0) for c in range(6)]
        carry.append((start[:3], start[3:]))
    for _ in range(SUBSTEPS):
        moved = []
        for g in range(groups):
            position, velocity = carry[g]
            rate = rates[g]
            middle_pos = [x + 0.5 * STEP_SIZE * v for x, v in zip(position, velocity)]
            here = sample(matrices[g], position)
            there = sample(matrices[g], middle_pos)
            middle_vel = [v + 0.5 * STEP_SIZE * ((u - v) * rate) for u, v in zip(here, velocity)]
            moved.append(
                (
                    [x + STEP_SIZE * m for x, m in zip(position, middle_vel)],
                    [v + STEP_SIZE * (u - m) * rate for v, u, m in zip(velocity, there, middle_vel)],
                )
            )
        carry = moved
    for g in range(groups):
        rows = slice(g * GROUP, (g + 1) * GROUP)
        for c, value in enumerate([*carry[g][0], *carry[g][1]]):
            out[c, rows, :] = jnp.where(alive[g], value, state[c, rows, :])
    if groups < box_table.shape[0]:
        out[:, groups * GROUP :, :] = state[:, groups * GROUP :, :]


def move_kernel(live, box_table, from_lower, from_upper, state, stokes, out):
    count = live[0]
    groups = box_table.shape[0]
    fewer = 0
    for some in sorted({1, max(1, groups // 2), groups}):

        @pl.when((count > fewer * GROUP) & (count <= some * GROUP))
        def _(some=some):
            move_groups(some, count, box_table, from_lower, from_upper, state, stokes, out)

        fewer = some


def in_smem():
    return pl.BlockSpec(memory_space=pltpu.SMEM)


def in_vmem():
    return pl.BlockSpec(memory_space=pltpu.VMEM)


def exchange(near, far, axis):
    devices = lax.axis_size(axis)
    near_pairs = [(i, i ^ 1) for i in range(devices)]
    far_pairs = [(i, (i + 1 if i % 2 else i - 1) % devices) for i in range(devices)]
    far = lax.ppermute(far, axis, far_pairs)
    return lax.ppermute(near, axis, near_pairs), far


def shift(array, axis, step):
    devices = lax.axis_size(axis)
    return lax.ppermute(array, axis, [(i, (i + step) % devices) for i in range(devices)])


def body(velocity_field, particle_state, stokes_time, box_base, live_bins):
    comps, depth, length, cells = velocity_field.shape
    bins = box_base.shape[0]
    tiles = cells // LANES
    groups = bins // GROUP
    table = box_base.T
    state = particle_state.transpose(1, 0, 2)
    block = pltpu.with_memory_space_constraint(velocity_field, pltpu.HBM)
    params = pltpu.CompilerParams(vmem_limit_bytes=VMEM_LIMIT)

    lower_table, upper_table = shift(table, "slab", 1), shift(table, "slab", -1)
    padded_block = pltpu.VMEM((comps, depth, tiles, length + 2 * TOP, LANES), jnp.float32)
    edge_rows = jax.ShapeDtypeStruct((comps, depth, 2, cells), jnp.float32)
    near, far = pl.pallas_call(
        edges_kernel,
        out_shape=(edge_rows, edge_rows),
        in_specs=[pl.BlockSpec(memory_space=pl.ANY)],
        out_specs=(in_vmem(), in_vmem()),
        scratch_shapes=[pltpu.SemaphoreType.DMA((2,))],
        compiler_params=params,
        name="edges",
    )(block)
    near, far = exchange(near, far, "sub")

    padded, own_table = pl.pallas_call(
        load_kernel,
        out_shape=(padded_block, pltpu.SMEM(table.shape, jnp.int32)),
        in_specs=[pl.BlockSpec(memory_space=pl.ANY)] * 2,
        out_specs=(in_vmem(), in_smem()),
        scratch_shapes=[pltpu.SemaphoreType.DMA((1 + tiles,))],
        compiler_params=params,
        cost_estimate=pl.CostEstimate(flops=1_000_000, bytes_accessed=6_000_000, transcendentals=0),
        name="load",
    )(block, pltpu.with_memory_space_constraint(table, pltpu.HBM))

    answer = jax.ShapeDtypeStruct((groups, 8, LANES), jnp.float32)
    for_upper, for_lower, padded = pl.pallas_call(
        answers_kernel,
        out_shape=(answer, answer, padded_block),
        in_specs=[in_smem(), in_smem(), in_vmem(), in_vmem(), in_vmem()],
        out_specs=(in_vmem(), in_vmem(), in_vmem()),
        scratch_shapes=[
            pltpu.VMEM((2 * groups, comps, 8, LANES), jnp.float32),
            pltpu.SMEM((2 * bins + 1,), jnp.int32),
        ],
        input_output_aliases={2: 2},
        compiler_params=params,
        name="answers",
    )(upper_table, lower_table, padded, far, near)
    from_lower, from_upper = shift(for_upper, "slab", 1), shift(for_lower, "slab", -1)

    box_table, _ = pl.pallas_call(
        boxes_kernel,
        out_shape=(jax.ShapeDtypeStruct((groups, NODES, LANES), jnp.float32), padded_block),
        in_specs=[in_smem(), in_smem(), in_vmem(), in_vmem(), in_vmem()],
        out_specs=(in_vmem(), in_vmem()),
        input_output_aliases={4: 1},
        compiler_params=params,
        cost_estimate=pl.CostEstimate(flops=1_000_000, bytes_accessed=4_000_000, transcendentals=0),
        name="boxes",
    )(own_table, live_bins, far, near, padded)

    moved = pl.pallas_call(
        move_kernel,
        out_shape=jax.ShapeDtypeStruct(state.shape, jnp.float32),
        in_specs=[in_smem()] + [in_vmem()] * 5,
        out_specs=in_vmem(),
        compiler_params=params,
        name="move",
    )(live_bins, box_table, from_lower, from_upper, state, stokes_time)
    return moved.transpose(1, 0, 2)


def solution(mesh):
    placed = (
        P(None, "slab", "sub", None),
        P(("slab", "sub"), None, None),
        P(("slab", "sub"), None),
        P(("slab", "sub"), None),
        P(("slab", "sub")),
    )
    return jax.shard_map(
        body, mesh=mesh, in_specs=placed, out_specs=P(("slab", "sub"), None, None), check_vma=False
    )
```

```python
import functools

import jax
import jax.numpy as jnp
from jax import lax
from jax.experimental import pallas as pl
from jax.experimental.pallas import tpu as pltpu
from jax.sharding import PartitionSpec as P

SUBSTEPS = 4
STEP_SIZE = 0.2
LANES = 128
LANE_BITS = 7
NODES = 16
GROUP = 8
GROUP_BITS = 3
TOP = 8
UNROLL = 4
VMEM_LIMIT = 48 * 1024 * 1024


def rows_and_lanes():
    return lax.broadcasted_iota(jnp.int32, (8, LANES), 0), lax.broadcasted_iota(jnp.int32, (8, LANES), 1)


def gather_pair(planes, index, valid, first_row, first_z, slot):
    row, lane = rows_and_lanes()
    tiles = planes.shape[-3]
    tile, offset = lax.shift_right_logical(first_z, LANE_BITS), first_z & (LANES - 1)
    beside = jnp.where(tile == tiles - 1, 0, tile + 1)
    upper = row < 4
    first, second = index

    def load(at):
        return jnp.where(
            upper,
            planes[(*first, at, pl.ds(first_row, 8), slice(None))],
            planes[(*second, at, pl.ds(first_row - 4, 8), slice(None))],
        )

    rows = jnp.where(lane >= offset, load(tile), load(beside))
    rows = pltpu.roll(rows, (NODES * slot - first_z) & (LANES - 1), 1)
    wanted = jnp.where(upper, jnp.where(valid[0], 4 * slot, -1), jnp.where(valid[1], 4 * slot, -1))
    return rows, (lax.shift_right_logical(lane, 2) == wanted)


def flatten_pair(parts):
    row, _ = rows_and_lanes()
    total = None
    for c, part in enumerate(parts):
        part = pltpu.roll(part, 0, 1, stride=4, stride_axis=0)
        part = part + pltpu.roll(part, 7, 0)
        part = part + pltpu.roll(part, 6, 0)
        part = jnp.where((row & 3) == 0, part, 0.0)
        part = pltpu.roll(part, c, 0) if c else part
        total = part if total is None else total + part
    return total


def align_pair(tile):
    row, _ = rows_and_lanes()
    return jnp.where(row < 4, tile, pltpu.roll(tile, LANES - NODES, 1))


def edges_kernel(field, near, far, sems):
    length = field.shape[2]
    even = lax.axis_index("sub") % 2 == 0

    def edge_copies(near_row, far_row):
        return [
            pltpu.make_async_copy(field.at[:, :, pl.ds(row, 2), :], into, sems.at[n])
            for n, (row, into) in enumerate(((near_row, near), (far_row, far)))
        ]

    @pl.when(even)
    def _():
        for copy in edge_copies(length - 2, 0):
            copy.start()

    @pl.when(jnp.logical_not(even))
    def _():
        for copy in edge_copies(0, length - 2):
            copy.start()

    for copy in edge_copies(0, 0):
        copy.wait()


def load_kernel(field, base, padded, table, sems):
    length, cells = field.shape[2:]
    copies = [pltpu.make_async_copy(base, table, sems.at[0])]
    for tile in range(cells // LANES):
        copies.append(
            pltpu.make_async_copy(
                field.at[:, :, :, pl.ds(tile * LANES, LANES)],
                padded.at[:, :, tile, pl.ds(TOP, length), :],
                sems.at[1 + tile],
            )
        )
    for copy in copies:
        copy.start()
    for copy in copies:
        copy.wait()


def fill_halo(padded, far, near, planes):
    comps, _, tiles, rows, _ = padded.shape
    even = lax.axis_index("sub") % 2 == 0
    below, above = TOP - 2, rows - TOP
    near_row, far_row = jnp.where(even, above, below), jnp.where(even, below, above)
    for c in range(comps):
        for x in planes:
            for tile in range(tiles):
                lanes = slice(tile * LANES, (tile + 1) * LANES)
                padded[c, x, tile, pl.ds(near_row, 2), :] = near[c, x, :, lanes]
                padded[c, x, tile, pl.ds(far_row, 2), :] = far[c, x, :, lanes]


def box_planes(first_x, pair, depth):
    x = [first_x + 2 * pair, first_x + 2 * pair + 1]
    return [jnp.clip(at, 0, depth - 1) for at in x], [(at >= 0) & (at < depth) for at in x]


def boxes_kernel(table, live, far, near, padded_in, box_table, padded):
    comps, depth, _, rows, _ = padded.shape
    fill_halo(padded, far, near, range(2, depth - 2))
    box_table[...] = jnp.zeros_like(box_table)

    def one_group(group, _):
        parts = [[jnp.zeros((8, LANES), jnp.float32)] * comps for _ in range(2)]
        for slot in range(GROUP):
            b = group * GROUP + slot
            first_x, first_y, first_z = table[0, b], table[1, b], table[2, b]
            for pair in range(2):
                x, valid = box_planes(first_x, pair, depth)
                for c in range(comps):
                    found, mask = gather_pair(padded, ((c, x[0]), (c, x[1])), valid, TOP + first_y, first_z, slot)
                    parts[pair][c] = jnp.where(mask, found, parts[pair][c])
        for pair in range(2):
            box_table[group, 8 * pair : 8 * pair + 8, :] = align_pair(flatten_pair(parts[pair]))
        return 0

    lax.fori_loop(0, (live[0] + GROUP - 1) // GROUP, one_group, 0)


def hits_kernel(upper_base, lower_base, upper_table, lower_table, hits, sems, *, depth):
    copies = [
        pltpu.make_async_copy(source, into, sems.at[n])
        for n, (source, into) in enumerate(((upper_base, upper_table), (lower_base, lower_table)))
    ]
    for copy in copies:
        copy.start()
    for copy in copies:
        copy.wait()
    bins = upper_table.shape[1]
    found = jnp.int32(0)
    for side, table in enumerate((upper_table, lower_table)):
        for b in range(bins):
            hits[found] = side * bins + b
            wanted = table[0, b] > depth - 4 if side else table[0, b] < 0
            found = found + wanted.astype(jnp.int32)
    hits[2 * bins + 1] = found


def answers_kernel(hits, upper_table, lower_table, padded_in, far, near, upper_out, lower_out, padded, acc):
    comps, depth, _, rows, _ = padded.shape
    bins = lower_table.shape[1]
    groups = bins // GROUP
    fill_halo(padded, far, near, [0, 1, depth - 2, depth - 1])
    acc[...] = jnp.zeros_like(acc)
    found = hits[2 * bins + 1]

    def some_bins(n, _):
        for k in range(UNROLL):
            at = n * UNROLL + k
            entry = hits[jnp.minimum(at, found - 1)]
            from_upper = entry < bins
            b = jnp.where(from_upper, entry, entry - bins)
            first_x, first_y, first_z = [jnp.where(from_upper, upper_table[d, b], lower_table[d, b]) for d in range(3)]
            x = first_x + jnp.where(from_upper, depth, 2 - depth)
            x = [x, x + 1]
            valid = [(at < found) & (cell >= 0) & (cell < depth) for cell in x]
            x = [jnp.clip(cell, 0, depth - 1) for cell in x]
            parts = []
            for c in range(comps):
                gathered, mask = gather_pair(
                    padded, ((c, x[0]), (c, x[1])), valid, TOP + first_y, first_z, b & (GROUP - 1)
                )
                parts.append(jnp.where(mask, gathered, 0.0))
            group = lax.shift_right_logical(entry, GROUP_BITS)
            for c in range(comps):
                acc[group, c] += parts[c]
        return 0

    lax.fori_loop(0, (found + UNROLL - 1) // UNROLL, some_bins, 0)
    for g in range(groups):
        upper_out[g] = align_pair(flatten_pair([acc[g, c] for c in range(comps)]))
        lower_out[g] = align_pair(flatten_pair([acc[groups + g, c] for c in range(comps)]))


def unscaled_weights(t):
    plus, minus, minus_two = t + 1.0, t - 1.0, t - 2.0
    inner, outer = t * minus, plus * minus_two
    return inner * minus_two, outer * minus, outer * t, inner * plus


def node_factor(node):
    return jnp.where(node == 0, -1.0 / 6.0, jnp.where(node == 1, 0.5, jnp.where(node == 2, -0.5, 1.0 / 6.0)))


def split(x):
    head = x.astype(jnp.bfloat16)
    return head, (x - head.astype(jnp.float32)).astype(jnp.bfloat16)


def group_matrix(box):
    row = lax.broadcasted_iota(jnp.int32, box.shape, 0)
    lane = lax.broadcasted_iota(jnp.int32, box.shape, 1)
    box = box * (node_factor(row // 4) * node_factor(lane // 4 % 4) * node_factor(lane % 4))
    box = jnp.take_along_axis(box, lane % GROUP * NODES + lane // GROUP, axis=1)
    head = box.astype(jnp.bfloat16).astype(jnp.float32)
    own = lax.broadcasted_iota(jnp.int32, (GROUP, LANES), 1) % GROUP == lax.broadcasted_iota(
        jnp.int32, (GROUP, LANES), 0
    )

    def spread(part):
        rows = [
            jnp.where(own, jnp.broadcast_to(part[4 * i + c : 4 * i + c + 1], (GROUP, LANES)), 0.0)
            for i in range(4)
            for c in range(3)
        ]
        return jnp.concatenate(rows, axis=0).astype(jnp.bfloat16)

    heads, tails = spread(head), spread(box - head)
    return jnp.concatenate(
        [jnp.concatenate([heads, heads], axis=1), jnp.concatenate([tails, jnp.zeros_like(tails)], axis=1)], axis=0
    )


def sample(matrix, position):
    along_x, along_y, along_z = (unscaled_weights(t) for t in position)
    weights = jnp.concatenate([y * z for y in along_y for z in along_z], axis=0)
    head, tail = split(weights)
    planes = jnp.dot(matrix, jnp.concatenate([head, tail], axis=0), preferred_element_type=jnp.float32)
    half = planes.shape[0] // 2
    planes = planes[:half] + planes[half:]
    result = []
    for c in range(3):
        plane = [planes[8 * (3 * i + c) : 8 * (3 * i + c) + 8] for i in range(4)]
        result.append(
            (plane[0] * along_x[0] + plane[1] * along_x[1]) + (plane[2] * along_x[2] + plane[3] * along_x[3])
        )
    return result


def move_groups(groups, count, box_table, from_lower, from_upper, state, stokes, out):
    matrices, carry, rates, alive = [], [], [], []
    for g in range(groups):
        rows = slice(g * GROUP, (g + 1) * GROUP)
        answers = jnp.concatenate([from_lower[g], from_upper[g]], axis=0)
        matrices.append(group_matrix(box_table[g] + answers))
        rates.append(1.0 / stokes[rows, :])
        kept = g * GROUP + lax.broadcasted_iota(jnp.int32, rates[g].shape, 0) < count
        alive.append(kept)
        start = [jnp.where(kept, state[c, rows, :], 0.0) for c in range(6)]
        carry.append((start[:3], start[3:]))
    for _ in range(SUBSTEPS):
        moved = []
        for g in range(groups):
            position, velocity = carry[g]
            rate = rates[g]
            middle_pos = [x + 0.5 * STEP_SIZE * v for x, v in zip(position, velocity)]
            here = sample(matrices[g], position)
            there = sample(matrices[g], middle_pos)
            middle_vel = [v + 0.5 * STEP_SIZE * ((u - v) * rate) for u, v in zip(here, velocity)]
            moved.append(
                (
                    [x + STEP_SIZE * m for x, m in zip(position, middle_vel)],
                    [v + STEP_SIZE * (u - m) * rate for v, u, m in zip(velocity, there, middle_vel)],
                )
            )
        carry = moved
    for g in range(groups):
        rows = slice(g * GROUP, (g + 1) * GROUP)
        for c, value in enumerate([*carry[g][0], *carry[g][1]]):
            out[c, rows, :] = jnp.where(alive[g], value, state[c, rows, :])
    if groups < box_table.shape[0]:
        out[:, groups * GROUP :, :] = state[:, groups * GROUP :, :]


def move_kernel(live, box_table, from_lower, from_upper, state, stokes, out):
    count = live[0]
    groups = box_table.shape[0]
    fewer = 0
    for some in sorted({1, max(1, groups // 2), groups}):

        @pl.when((count > fewer * GROUP) & (count <= some * GROUP))
        def _(some=some):
            move_groups(some, count, box_table, from_lower, from_upper, state, stokes, out)

        fewer = some


def in_smem():
    return pl.BlockSpec(memory_space=pltpu.SMEM)


def in_vmem():
    return pl.BlockSpec(memory_space=pltpu.VMEM)


def exchange(near, far, axis):
    devices = lax.axis_size(axis)
    near_pairs = [(i, i ^ 1) for i in range(devices)]
    far_pairs = [(i, (i + 1 if i % 2 else i - 1) % devices) for i in range(devices)]
    far = lax.ppermute(far, axis, far_pairs)
    return lax.ppermute(near, axis, near_pairs), far


def shift(array, axis, step):
    devices = lax.axis_size(axis)
    return lax.ppermute(array, axis, [(i, (i + step) % devices) for i in range(devices)])


def body(velocity_field, particle_state, stokes_time, box_base, live_bins):
    comps, depth, length, cells = velocity_field.shape
    bins = box_base.shape[0]
    tiles = cells // LANES
    groups = bins // GROUP
    table = box_base.T
    state = particle_state.transpose(1, 0, 2)
    block = pltpu.with_memory_space_constraint(velocity_field, pltpu.HBM)
    params = pltpu.CompilerParams(vmem_limit_bytes=VMEM_LIMIT)

    lower_table, upper_table = shift(table, "slab", 1), shift(table, "slab", -1)
    padded_block = pltpu.VMEM((comps, depth, tiles, length + 2 * TOP, LANES), jnp.float32)
    edge_rows = jax.ShapeDtypeStruct((comps, depth, 2, cells), jnp.float32)
    near, far = pl.pallas_call(
        edges_kernel,
        out_shape=(edge_rows, edge_rows),
        in_specs=[pl.BlockSpec(memory_space=pl.ANY)],
        out_specs=(in_vmem(), in_vmem()),
        scratch_shapes=[pltpu.SemaphoreType.DMA((2,))],
        compiler_params=params,
        name="edges",
    )(block)
    near, far = exchange(near, far, "sub")

    smem_table = pltpu.SMEM(table.shape, jnp.int32)
    padded, own_table = pl.pallas_call(
        load_kernel,
        out_shape=(padded_block, smem_table),
        in_specs=[pl.BlockSpec(memory_space=pl.ANY)] * 2,
        out_specs=(in_vmem(), in_smem()),
        scratch_shapes=[pltpu.SemaphoreType.DMA((1 + tiles,))],
        compiler_params=params,
        cost_estimate=pl.CostEstimate(flops=1_000_000, bytes_accessed=6_000_000, transcendentals=0),
        name="load",
    )(block, pltpu.with_memory_space_constraint(table, pltpu.HBM))

    upper_cells, lower_cells, hits = pl.pallas_call(
        functools.partial(hits_kernel, depth=depth),
        out_shape=(smem_table, smem_table, pltpu.SMEM((2 * bins + 2,), jnp.int32)),
        in_specs=[in_vmem(), in_vmem()],
        out_specs=(in_smem(), in_smem(), in_smem()),
        scratch_shapes=[pltpu.SemaphoreType.DMA((2,))],
        compiler_params=params,
        name="hits",
    )(upper_table, lower_table)
    answer = jax.ShapeDtypeStruct((groups, 8, LANES), jnp.float32)
    for_upper, for_lower, padded = pl.pallas_call(
        answers_kernel,
        out_shape=(answer, answer, padded_block),
        in_specs=[in_smem(), in_smem(), in_smem(), in_vmem(), in_vmem(), in_vmem()],
        out_specs=(in_vmem(), in_vmem(), in_vmem()),
        scratch_shapes=[pltpu.VMEM((2 * groups, comps, 8, LANES), jnp.float32)],
        input_output_aliases={3: 2},
        compiler_params=params,
        name="answers",
    )(hits, upper_cells, lower_cells, padded, far, near)
    from_lower, from_upper = shift(for_upper, "slab", 1), shift(for_lower, "slab", -1)

    box_table, _ = pl.pallas_call(
        boxes_kernel,
        out_shape=(jax.ShapeDtypeStruct((groups, NODES, LANES), jnp.float32), padded_block),
        in_specs=[in_smem(), in_smem(), in_vmem(), in_vmem(), in_vmem()],
        out_specs=(in_vmem(), in_vmem()),
        input_output_aliases={4: 1},
        compiler_params=params,
        cost_estimate=pl.CostEstimate(flops=1_000_000, bytes_accessed=4_000_000, transcendentals=0),
        name="boxes",
    )(own_table, live_bins, far, near, padded)

    moved = pl.pallas_call(
        move_kernel,
        out_shape=jax.ShapeDtypeStruct(state.shape, jnp.float32),
        in_specs=[in_smem()] + [in_vmem()] * 5,
        out_specs=in_vmem(),
        compiler_params=params,
        name="move",
    )(live_bins, box_table, from_lower, from_upper, state, stokes_time)
    return moved.transpose(1, 0, 2)


def solution(mesh):
    placed = (
        P(None, "slab", "sub", None),
        P(("slab", "sub"), None, None),
        P(("slab", "sub"), None),
        P(("slab", "sub"), None),
        P(("slab", "sub")),
    )
    return jax.shard_map(
        body, mesh=mesh, in_specs=placed, out_specs=P(("slab", "sub"), None, None), check_vma=False
    )
```

```python
import functools

import jax
import jax.numpy as jnp
from jax import lax
from jax.experimental import pallas as pl
from jax.experimental.pallas import tpu as pltpu
from jax.sharding import PartitionSpec as P

SUBSTEPS = 4
STEP_SIZE = 0.2
LANES = 128
LANE_BITS = 7
NODES = 16
GROUP = 8
GROUP_BITS = 3
MARGIN = 2
TOP = 8
UNROLL = 4
VMEM_LIMIT = 32 * 1024 * 1024


def rows_and_lanes():
    return lax.broadcasted_iota(jnp.int32, (8, LANES), 0), lax.broadcasted_iota(jnp.int32, (8, LANES), 1)


def first_rows(shape, first_y, first_z):
    _, _, tiles, rows = shape
    tile = lax.shift_right_logical(first_z, LANE_BITS)
    beside = jnp.where(tile == tiles - 1, 0, tile + 1)
    start = MARGIN * tiles * rows + TOP + first_y
    return start + tile * rows, start + beside * rows, first_z & (LANES - 1)


def gather_pair(padded, shape, x, valid, starts, slot):
    comps, _, tiles, rows = shape
    row, lane = rows_and_lanes()
    here, there, offset = starts
    upper, left = row < 4, lane >= offset
    plane = x * (tiles * rows)
    shift = (NODES * slot - offset) & (LANES - 1)
    wanted = jnp.where(upper, jnp.where(valid[0], 4 * slot, -1), jnp.where(valid[1], 4 * slot, -1))
    found = []
    for c in range(comps):
        near, far = [
            jnp.where(
                upper, padded[c, pl.ds(plane + start, 8), :], padded[c, pl.ds(plane + start + (tiles * rows - 4), 8), :]
            )
            for start in (here, there)
        ]
        found.append(pltpu.roll(jnp.where(left, near, far), shift, 1))
    return found, lax.shift_right_logical(lane, 2) == wanted


def flatten_pair(parts):
    row, _ = rows_and_lanes()
    first, second, third = [pltpu.roll(part, 0, 1, stride=4, stride_axis=0) for part in parts]
    low = jnp.where((row & 1) == 0, first + pltpu.roll(first, 7, 0), second + pltpu.roll(second, 1, 0))
    high = jnp.where((row & 1) == 0, third + pltpu.roll(third, 7, 0), 0.0)
    return jnp.where((row & 2) == 0, low + pltpu.roll(low, 6, 0), high + pltpu.roll(high, 2, 0))


def align_pair(tile):
    row, _ = rows_and_lanes()
    return jnp.where(row < 4, tile, pltpu.roll(tile, LANES - NODES, 1))


def edges_kernel(field, near, far, sems):
    length = field.shape[2]
    even = lax.axis_index("sub") % 2 == 0

    def edge_copies(near_row, far_row):
        return [
            pltpu.make_async_copy(field.at[:, :, pl.ds(row, 2), :], into, sems.at[n])
            for n, (row, into) in enumerate(((near_row, near), (far_row, far)))
        ]

    @pl.when(even)
    def _():
        for copy in edge_copies(length - 2, 0):
            copy.start()

    @pl.when(jnp.logical_not(even))
    def _():
        for copy in edge_copies(0, length - 2):
            copy.start()

    for copy in edge_copies(0, 0):
        copy.wait()


def load_kernel(field, base, padded, table, sems):
    depth, length, cells = field.shape[1:]
    copies = [pltpu.make_async_copy(base, table, sems.at[0])]
    for tile in range(cells // LANES):
        copies.append(
            pltpu.make_async_copy(
                field.at[:, :, :, pl.ds(tile * LANES, LANES)],
                padded.at[:, pl.ds(MARGIN, depth), tile, pl.ds(TOP, length), :],
                sems.at[1 + tile],
            )
        )
    for copy in copies:
        copy.start()
    for copy in copies:
        copy.wait()


def fill_halo(padded, shape, far, near, planes):
    comps, _, tiles, rows = shape
    even = lax.axis_index("sub") % 2 == 0
    below, above = TOP - 2, rows - TOP
    near_row, far_row = jnp.where(even, above, below), jnp.where(even, below, above)
    for c in range(comps):
        for x in planes:
            for tile in range(tiles):
                lanes = slice(tile * LANES, (tile + 1) * LANES)
                start = ((MARGIN + x) * tiles + tile) * rows
                padded[c, pl.ds(start + near_row, 2), :] = near[c, x, :, lanes]
                padded[c, pl.ds(start + far_row, 2), :] = far[c, x, :, lanes]


def boxes_kernel(table, live, far, near, padded_in, box_table, padded, acc, *, shape):
    comps, depth = shape[:2]
    fill_halo(padded, shape, far, near, range(2, depth - 2))
    acc[...] = jnp.zeros_like(acc)

    def one_group(group, _):
        parts = [[jnp.zeros((8, LANES), jnp.float32)] * comps for _ in range(2)]
        for slot in range(GROUP):
            b = group * GROUP + slot
            x = table[0, b]
            starts = first_rows(shape, table[1, b], table[2, b])
            valid = ((x >= 0, x >= -1), (x < depth - 2, x < depth - 3))
            for pair in range(2):
                found, mask = gather_pair(padded, shape, x + 2 * pair, valid[pair], starts, slot)
                parts[pair] = [jnp.where(mask, new, old) for new, old in zip(found, parts[pair])]
        for pair in range(2):
            for c in range(comps):
                acc[group, pair, c] = parts[pair][c]
        return 0

    lax.fori_loop(0, (live[0] + GROUP - 1) // GROUP, one_group, 0)
    for group in range(box_table.shape[0]):
        for pair in range(2):
            rows = flatten_pair([acc[group, pair, c] for c in range(comps)])
            box_table[group, 8 * pair : 8 * pair + 8, :] = align_pair(rows)


def hits_kernel(upper_base, lower_base, upper_table, lower_table, hits, sems, *, depth):
    copies = [
        pltpu.make_async_copy(source, into, sems.at[n])
        for n, (source, into) in enumerate(((upper_base, upper_table), (lower_base, lower_table)))
    ]
    for copy in copies:
        copy.start()
    for copy in copies:
        copy.wait()
    bins = upper_table.shape[1]
    found = jnp.int32(0)
    for side, table in enumerate((upper_table, lower_table)):
        for b in range(bins):
            hits[found] = side * bins + b
            wanted = table[0, b] > depth - 4 if side else table[0, b] < 0
            found = found + wanted.astype(jnp.int32)
    hits[2 * bins + 1] = found


def answers_kernel(hits, upper_table, lower_table, padded_in, far, near, upper_out, lower_out, padded, acc, *, shape):
    comps, depth = shape[:2]
    bins = lower_table.shape[1]
    groups = bins // GROUP
    fill_halo(padded, shape, far, near, [0, 1, depth - 2, depth - 1])
    acc[...] = jnp.zeros_like(acc)
    found = hits[2 * bins + 1]

    def some_bins(n, _):
        for k in range(UNROLL):
            at = n * UNROLL + k
            entry = hits[jnp.minimum(at, found - 1)]
            from_upper = entry < bins
            b = jnp.where(from_upper, entry, entry - bins)
            first_x, first_y, first_z = [jnp.where(from_upper, upper_table[d, b], lower_table[d, b]) for d in range(3)]
            x = first_x + jnp.where(from_upper, depth, 2 - depth)
            valid = [(at < found) & (cell >= 0) & (cell < depth) for cell in (x, x + 1)]
            starts = first_rows(shape, first_y, first_z)
            gathered, mask = gather_pair(padded, shape, x, valid, starts, b & (GROUP - 1))
            group = lax.shift_right_logical(entry, GROUP_BITS)
            for c in range(comps):
                acc[group, c] += jnp.where(mask, gathered[c], 0.0)
        return 0

    lax.fori_loop(0, (found + UNROLL - 1) // UNROLL, some_bins, 0)
    for g in range(groups):
        upper_out[g] = align_pair(flatten_pair([acc[g, c] for c in range(comps)]))
        lower_out[g] = align_pair(flatten_pair([acc[groups + g, c] for c in range(comps)]))


def unscaled_weights(t):
    plus, minus, minus_two = t + 1.0, t - 1.0, t - 2.0
    inner, outer = t * minus, plus * minus_two
    return inner * minus_two, outer * minus, outer * t, inner * plus


def node_factor(node):
    return jnp.where(node == 0, -1.0 / 6.0, jnp.where(node == 1, 0.5, jnp.where(node == 2, -0.5, 1.0 / 6.0)))


def split(x):
    head = x.astype(jnp.bfloat16)
    return head, (x - head.astype(jnp.float32)).astype(jnp.bfloat16)


def group_matrix(box):
    row = lax.broadcasted_iota(jnp.int32, box.shape, 0)
    lane = lax.broadcasted_iota(jnp.int32, box.shape, 1)
    box = box * (node_factor(row // 4) * node_factor(lane // 4 % 4) * node_factor(lane % 4))
    box = jnp.take_along_axis(box, lane % GROUP * NODES + lane // GROUP, axis=1)
    head = box.astype(jnp.bfloat16).astype(jnp.float32)
    own = lax.broadcasted_iota(jnp.int32, (GROUP, LANES), 1) % GROUP == lax.broadcasted_iota(
        jnp.int32, (GROUP, LANES), 0
    )

    def spread(part):
        rows = [
            jnp.where(own, jnp.broadcast_to(part[4 * i + c : 4 * i + c + 1], (GROUP, LANES)), 0.0)
            for i in range(4)
            for c in range(3)
        ]
        return jnp.concatenate(rows, axis=0).astype(jnp.bfloat16)

    heads, tails = spread(head), spread(box - head)
    return jnp.concatenate(
        [jnp.concatenate([heads, heads], axis=1), jnp.concatenate([tails, jnp.zeros_like(tails)], axis=1)], axis=0
    )


def sample(matrix, position):
    along_x, along_y, along_z = (unscaled_weights(t) for t in position)
    weights = jnp.concatenate([y * z for y in along_y for z in along_z], axis=0)
    head, tail = split(weights)
    planes = jnp.dot(matrix, jnp.concatenate([head, tail], axis=0), preferred_element_type=jnp.float32)
    half = planes.shape[0] // 2
    planes = planes[:half] + planes[half:]
    result = []
    for c in range(3):
        plane = [planes[8 * (3 * i + c) : 8 * (3 * i + c) + 8] for i in range(4)]
        result.append(
            (plane[0] * along_x[0] + plane[1] * along_x[1]) + (plane[2] * along_x[2] + plane[3] * along_x[3])
        )
    return result


def move_groups(groups, count, box_table, from_lower, from_upper, state, stokes, out):
    matrices, carry, rates, alive = [], [], [], []
    for g in range(groups):
        rows = slice(g * GROUP, (g + 1) * GROUP)
        answers = jnp.concatenate([from_lower[g], from_upper[g]], axis=0)
        matrices.append(group_matrix(box_table[g] + answers))
        rates.append(1.0 / stokes[rows, :])
        kept = g * GROUP + lax.broadcasted_iota(jnp.int32, rates[g].shape, 0) < count
        alive.append(kept)
        start = [jnp.where(kept, state[c, rows, :], 0.0) for c in range(6)]
        carry.append((start[:3], start[3:]))
    for _ in range(SUBSTEPS):
        moved = []
        for g in range(groups):
            position, velocity = carry[g]
            rate = rates[g]
            middle_pos = [x + 0.5 * STEP_SIZE * v for x, v in zip(position, velocity)]
            here = sample(matrices[g], position)
            there = sample(matrices[g], middle_pos)
            middle_vel = [v + 0.5 * STEP_SIZE * ((u - v) * rate) for u, v in zip(here, velocity)]
            moved.append(
                (
                    [x + STEP_SIZE * m for x, m in zip(position, middle_vel)],
                    [v + STEP_SIZE * (u - m) * rate for v, u, m in zip(velocity, there, middle_vel)],
                )
            )
        carry = moved
    for g in range(groups):
        rows = slice(g * GROUP, (g + 1) * GROUP)
        for c, value in enumerate([*carry[g][0], *carry[g][1]]):
            out[c, rows, :] = jnp.where(alive[g], value, state[c, rows, :])
    if groups < box_table.shape[0]:
        out[:, groups * GROUP :, :] = state[:, groups * GROUP :, :]


def move_kernel(live, box_table, from_lower, from_upper, state, stokes, out):
    count = live[0]
    groups = box_table.shape[0]
    fewer = 0
    for some in sorted({1, max(1, groups // 2), groups}):

        @pl.when((count > fewer * GROUP) & (count <= some * GROUP))
        def _(some=some):
            move_groups(some, count, box_table, from_lower, from_upper, state, stokes, out)

        fewer = some


def in_smem():
    return pl.BlockSpec(memory_space=pltpu.SMEM)


def in_vmem():
    return pl.BlockSpec(memory_space=pltpu.VMEM)


def exchange(near, far, axis):
    devices = lax.axis_size(axis)
    near_pairs = [(i, i ^ 1) for i in range(devices)]
    far_pairs = [(i, (i + 1 if i % 2 else i - 1) % devices) for i in range(devices)]
    far = lax.ppermute(far, axis, far_pairs)
    return lax.ppermute(near, axis, near_pairs), far


def shift(array, axis, step):
    devices = lax.axis_size(axis)
    return lax.ppermute(array, axis, [(i, (i + step) % devices) for i in range(devices)])


def body(velocity_field, particle_state, stokes_time, box_base, live_bins):
    comps, depth, length, cells = velocity_field.shape
    bins = box_base.shape[0]
    tiles = cells // LANES
    groups = bins // GROUP
    table = box_base.T
    state = particle_state.transpose(1, 0, 2)
    block = pltpu.with_memory_space_constraint(velocity_field, pltpu.HBM)
    params = pltpu.CompilerParams(vmem_limit_bytes=VMEM_LIMIT)

    lower_table, upper_table = shift(table, "slab", 1), shift(table, "slab", -1)
    shape = (comps, depth, tiles, length + 2 * TOP)
    planes = depth + 2 * MARGIN
    rows_of_block = pltpu.VMEM((comps, planes * tiles * (length + 2 * TOP), LANES), jnp.float32)
    edge_rows = jax.ShapeDtypeStruct((comps, depth, 2, cells), jnp.float32)
    near, far = pl.pallas_call(
        edges_kernel,
        out_shape=(edge_rows, edge_rows),
        in_specs=[pl.BlockSpec(memory_space=pl.ANY)],
        out_specs=(in_vmem(), in_vmem()),
        scratch_shapes=[pltpu.SemaphoreType.DMA((2,))],
        compiler_params=params,
        name="edges",
    )(block)
    near, far = exchange(near, far, "sub")

    smem_table = pltpu.SMEM(table.shape, jnp.int32)
    padded, own_table = pl.pallas_call(
        load_kernel,
        out_shape=(pltpu.VMEM((comps, planes, tiles, length + 2 * TOP, LANES), jnp.float32), smem_table),
        in_specs=[pl.BlockSpec(memory_space=pl.ANY)] * 2,
        out_specs=(in_vmem(), in_smem()),
        scratch_shapes=[pltpu.SemaphoreType.DMA((1 + tiles,))],
        compiler_params=params,
        cost_estimate=pl.CostEstimate(flops=1_000_000, bytes_accessed=6_000_000, transcendentals=0),
        name="load",
    )(block, pltpu.with_memory_space_constraint(table, pltpu.HBM))

    padded = padded.reshape(rows_of_block.shape)
    upper_cells, lower_cells, hits = pl.pallas_call(
        functools.partial(hits_kernel, depth=depth),
        out_shape=(smem_table, smem_table, pltpu.SMEM((2 * bins + 2,), jnp.int32)),
        in_specs=[in_vmem(), in_vmem()],
        out_specs=(in_smem(), in_smem(), in_smem()),
        scratch_shapes=[pltpu.SemaphoreType.DMA((2,))],
        compiler_params=params,
        name="hits",
    )(upper_table, lower_table)
    answer = jax.ShapeDtypeStruct((groups, 8, LANES), jnp.float32)
    for_upper, for_lower, padded = pl.pallas_call(
        functools.partial(answers_kernel, shape=shape),
        out_shape=(answer, answer, rows_of_block),
        in_specs=[in_smem(), in_smem(), in_smem(), in_vmem(), in_vmem(), in_vmem()],
        out_specs=(in_vmem(), in_vmem(), in_vmem()),
        scratch_shapes=[pltpu.VMEM((2 * groups, comps, 8, LANES), jnp.float32)],
        input_output_aliases={3: 2},
        compiler_params=params,
        name="answers",
    )(hits, upper_cells, lower_cells, padded, far, near)
    from_lower, from_upper = shift(for_upper, "slab", 1), shift(for_lower, "slab", -1)

    box_table, _ = pl.pallas_call(
        functools.partial(boxes_kernel, shape=shape),
        out_shape=(jax.ShapeDtypeStruct((groups, NODES, LANES), jnp.float32), rows_of_block),
        in_specs=[in_smem(), in_smem(), in_vmem(), in_vmem(), in_vmem()],
        out_specs=(in_vmem(), in_vmem()),
        scratch_shapes=[pltpu.VMEM((groups, 2, comps, 8, LANES), jnp.float32)],
        input_output_aliases={4: 1},
        compiler_params=params,
        cost_estimate=pl.CostEstimate(flops=1_000_000, bytes_accessed=4_000_000, transcendentals=0),
        name="boxes",
    )(own_table, live_bins, far, near, padded)

    moved = pl.pallas_call(
        move_kernel,
        out_shape=jax.ShapeDtypeStruct(state.shape, jnp.float32),
        in_specs=[in_smem()] + [in_vmem()] * 5,
        out_specs=in_vmem(),
        compiler_params=params,
        name="move",
    )(live_bins, box_table, from_lower, from_upper, state, stokes_time)
    return moved.transpose(1, 0, 2)


def solution(mesh):
    placed = (
        P(None, "slab", "sub", None),
        P(("slab", "sub"), None, None),
        P(("slab", "sub"), None),
        P(("slab", "sub"), None),
        P(("slab", "sub")),
    )
    return jax.shard_map(
        body, mesh=mesh, in_specs=placed, out_specs=P(("slab", "sub"), None, None), check_vma=False
    )
```

```python
import functools

import jax
import jax.numpy as jnp
from jax import lax
from jax.experimental import pallas as pl
from jax.experimental.pallas import tpu as pltpu
from jax.sharding import PartitionSpec as P

SUBSTEPS = 4
STEP_SIZE = 0.2
LANES = 128
LANE_BITS = 7
NODES = 16
GROUP = 8
GROUP_BITS = 3
MARGIN = 2
TOP = 8
UNROLL = 4
VMEM_LIMIT = 32 * 1024 * 1024


def rows_and_lanes():
    return lax.broadcasted_iota(jnp.int32, (8, LANES), 0), lax.broadcasted_iota(jnp.int32, (8, LANES), 1)


def first_rows(shape, first_y, first_z):
    _, _, tiles, rows = shape
    tile = lax.shift_right_logical(first_z, LANE_BITS)
    beside = jnp.where(tile == tiles - 1, 0, tile + 1)
    start = MARGIN * tiles * rows + TOP + first_y
    return start + tile * rows, start + beside * rows, first_z & (LANES - 1)


def gather_pair(padded, shape, x, valid, starts, slot):
    comps, _, tiles, rows = shape
    row, lane = rows_and_lanes()
    here, there, offset = starts
    upper, left = row < 4, lane >= offset
    plane = x * (tiles * rows)
    shift = (NODES * slot - offset) & (LANES - 1)
    wanted = jnp.where(upper, jnp.where(valid[0], 4 * slot, -1), jnp.where(valid[1], 4 * slot, -1))
    found = []
    for c in range(comps):
        near, far = [
            jnp.where(
                upper, padded[c, pl.ds(plane + start, 8), :], padded[c, pl.ds(plane + start + (tiles * rows - 4), 8), :]
            )
            for start in (here, there)
        ]
        found.append(pltpu.roll(jnp.where(left, near, far), shift, 1))
    return found, lax.shift_right_logical(lane, 2) == wanted


def flatten_pair(parts):
    row, _ = rows_and_lanes()
    first, second, third = [pltpu.roll(part, 0, 1, stride=4, stride_axis=0) for part in parts]
    low = jnp.where((row & 1) == 0, first + pltpu.roll(first, 7, 0), second + pltpu.roll(second, 1, 0))
    high = jnp.where((row & 1) == 0, third + pltpu.roll(third, 7, 0), 0.0)
    return jnp.where((row & 2) == 0, low + pltpu.roll(low, 6, 0), high + pltpu.roll(high, 2, 0))


def align_pair(tile):
    row, _ = rows_and_lanes()
    return jnp.where(row < 4, tile, pltpu.roll(tile, LANES - NODES, 1))


def edges_kernel(field, near, far, sems):
    length = field.shape[2]
    even = lax.axis_index("sub") % 2 == 0

    def edge_copies(near_row, far_row):
        return [
            pltpu.make_async_copy(field.at[:, :, pl.ds(row, 2), :], into, sems.at[n])
            for n, (row, into) in enumerate(((near_row, near), (far_row, far)))
        ]

    @pl.when(even)
    def _():
        for copy in edge_copies(length - 2, 0):
            copy.start()

    @pl.when(jnp.logical_not(even))
    def _():
        for copy in edge_copies(0, length - 2):
            copy.start()

    for copy in edge_copies(0, 0):
        copy.wait()


def load_kernel(field, base, padded, table, sems):
    depth, length, cells = field.shape[1:]
    copies = [pltpu.make_async_copy(base, table, sems.at[0])]
    for tile in range(cells // LANES):
        copies.append(
            pltpu.make_async_copy(
                field.at[:, :, :, pl.ds(tile * LANES, LANES)],
                padded.at[:, pl.ds(MARGIN, depth), tile, pl.ds(TOP, length), :],
                sems.at[1 + tile],
            )
        )
    for copy in copies:
        copy.start()
    for copy in copies:
        copy.wait()


def fill_halo(padded, shape, far, near, planes):
    comps, _, tiles, rows = shape
    even = lax.axis_index("sub") % 2 == 0
    below, above = TOP - 2, rows - TOP
    near_row, far_row = jnp.where(even, above, below), jnp.where(even, below, above)
    for c in range(comps):
        for x in planes:
            for tile in range(tiles):
                lanes = slice(tile * LANES, (tile + 1) * LANES)
                start = ((MARGIN + x) * tiles + tile) * rows
                padded[c, pl.ds(start + near_row, 2), :] = near[c, x, :, lanes]
                padded[c, pl.ds(start + far_row, 2), :] = far[c, x, :, lanes]


def boxes_kernel(table, live, far, near, padded_in, box_table, padded, acc, *, shape):
    comps, depth = shape[:2]
    fill_halo(padded, shape, far, near, range(2, depth - 2))
    acc[...] = jnp.zeros_like(acc)

    def one_group(group, _):
        parts = [[jnp.zeros((8, LANES), jnp.float32)] * comps for _ in range(2)]
        for slot in range(GROUP):
            b = group * GROUP + slot
            x = table[0, b]
            starts = first_rows(shape, table[1, b], table[2, b])
            valid = ((x >= 0, x >= -1), (x < depth - 2, x < depth - 3))
            for pair in range(2):
                found, mask = gather_pair(padded, shape, x + 2 * pair, valid[pair], starts, slot)
                parts[pair] = [jnp.where(mask, new, old) for new, old in zip(found, parts[pair])]
        for pair in range(2):
            for c in range(comps):
                acc[group, pair, c] = parts[pair][c]
        return 0

    lax.fori_loop(0, (live[0] + GROUP - 1) // GROUP, one_group, 0)
    for group in range(box_table.shape[0]):
        for pair in range(2):
            rows = flatten_pair([acc[group, pair, c] for c in range(comps)])
            box_table[group, 8 * pair : 8 * pair + 8, :] = align_pair(rows)


def hits_kernel(upper_base, lower_base, hits, *, depth):
    bins = upper_base.shape[1]
    row = lax.broadcasted_iota(jnp.int32, (8, bins), 0)
    lane = lax.broadcasted_iota(jnp.int32, (8, bins), 1)
    x, y, z = [jnp.where(row == 0, upper_base[d : d + 1, :], lower_base[d : d + 1, :]) for d in range(3)]
    wanted = ((row == 0) & (x < 0)) | ((row == 1) & (x > depth - 4))
    marks = jnp.where(wanted, 1.0, 0.0)
    earlier = lax.broadcasted_iota(jnp.int32, (bins, bins), 0) < lax.broadcasted_iota(jnp.int32, (bins, bins), 1)
    rank = jnp.dot(
        marks.astype(jnp.bfloat16),
        jnp.where(earlier, 1.0, 0.0).astype(jnp.bfloat16),
        preferred_element_type=jnp.float32,
    )
    rank = jnp.where(row == 1, rank + jnp.sum(marks[0:1], axis=1, keepdims=True), rank)
    rank = jnp.where(wanted, rank, -1.0)
    places = ((row * bins + lane) * 64 + (x + 2)).astype(jnp.float32)
    cells = (z * 64 + (y + 2)).astype(jnp.float32)
    found = jnp.sum(marks).astype(jnp.int32)
    hits[4, 0] = found

    def some_hits(n, _):
        for k in range(2 * UNROLL):
            at = n * 2 * UNROLL + k
            chosen = rank == at.astype(jnp.float32)
            place = jnp.sum(jnp.where(chosen, places, 0.0)).astype(jnp.int32)
            cell = jnp.sum(jnp.where(chosen, cells, 0.0)).astype(jnp.int32)
            hits[0, at] = lax.shift_right_logical(place, 6)
            hits[1, at] = (place & 63) - 2
            hits[2, at] = (cell & 63) - 2
            hits[3, at] = lax.shift_right_logical(cell, 6)
        return 0

    lax.fori_loop(0, (found + 2 * UNROLL - 1) // (2 * UNROLL), some_hits, 0)


def answers_kernel(hits, padded_in, far, near, upper_out, lower_out, padded, acc, *, shape):
    comps, depth = shape[:2]
    groups = upper_out.shape[0]
    bins = groups * GROUP
    fill_halo(padded, shape, far, near, [0, 1, depth - 2, depth - 1])
    acc[...] = jnp.zeros_like(acc)
    found = hits[4, 0]

    def some_bins(n, _):
        for k in range(UNROLL):
            at = n * UNROLL + k
            n_th = jnp.minimum(at, found - 1)
            entry, first_x, first_y, first_z = [hits[d, n_th] for d in range(4)]
            from_upper = entry < bins
            x = first_x + jnp.where(from_upper, depth, 2 - depth)
            valid = [(at < found) & (cell >= 0) & (cell < depth) for cell in (x, x + 1)]
            starts = first_rows(shape, first_y, first_z)
            gathered, mask = gather_pair(padded, shape, x, valid, starts, entry & (GROUP - 1))
            group = lax.shift_right_logical(entry, GROUP_BITS)
            for c in range(comps):
                acc[group, c] += jnp.where(mask, gathered[c], 0.0)
        return 0

    lax.fori_loop(0, (found + UNROLL - 1) // UNROLL, some_bins, 0)
    for g in range(groups):
        upper_out[g] = align_pair(flatten_pair([acc[g, c] for c in range(comps)]))
        lower_out[g] = align_pair(flatten_pair([acc[groups + g, c] for c in range(comps)]))


def unscaled_weights(t):
    plus, minus, minus_two = t + 1.0, t - 1.0, t - 2.0
    inner, outer = t * minus, plus * minus_two
    return inner * minus_two, outer * minus, outer * t, inner * plus


def node_factor(node):
    return jnp.where(node == 0, -1.0 / 6.0, jnp.where(node == 1, 0.5, jnp.where(node == 2, -0.5, 1.0 / 6.0)))


def split(x):
    head = x.astype(jnp.bfloat16)
    return head, (x - head.astype(jnp.float32)).astype(jnp.bfloat16)


def group_matrix(box):
    row = lax.broadcasted_iota(jnp.int32, box.shape, 0)
    lane = lax.broadcasted_iota(jnp.int32, box.shape, 1)
    box = box * (node_factor(row // 4) * node_factor(lane // 4 % 4) * node_factor(lane % 4))
    box = jnp.take_along_axis(box, lane % GROUP * NODES + lane // GROUP, axis=1)
    head = box.astype(jnp.bfloat16).astype(jnp.float32)
    own = lax.broadcasted_iota(jnp.int32, (GROUP, LANES), 1) % GROUP == lax.broadcasted_iota(
        jnp.int32, (GROUP, LANES), 0
    )

    def spread(part):
        rows = [
            jnp.where(own, jnp.broadcast_to(part[4 * i + c : 4 * i + c + 1], (GROUP, LANES)), 0.0)
            for i in range(4)
            for c in range(3)
        ]
        return jnp.concatenate(rows, axis=0).astype(jnp.bfloat16)

    heads, tails = spread(head), spread(box - head)
    return jnp.concatenate(
        [jnp.concatenate([heads, heads], axis=1), jnp.concatenate([tails, jnp.zeros_like(tails)], axis=1)], axis=0
    )


def sample(matrix, position):
    along_x, along_y, along_z = (unscaled_weights(t) for t in position)
    weights = jnp.concatenate([y * z for y in along_y for z in along_z], axis=0)
    head, tail = split(weights)
    planes = jnp.dot(matrix, jnp.concatenate([head, tail], axis=0), preferred_element_type=jnp.float32)
    half = planes.shape[0] // 2
    planes = planes[:half] + planes[half:]
    result = []
    for c in range(3):
        plane = [planes[8 * (3 * i + c) : 8 * (3 * i + c) + 8] for i in range(4)]
        result.append(
            (plane[0] * along_x[0] + plane[1] * along_x[1]) + (plane[2] * along_x[2] + plane[3] * along_x[3])
        )
    return result


def move_groups(groups, count, box_table, from_lower, from_upper, state, stokes, out):
    matrices, carry, rates, alive = [], [], [], []
    for g in range(groups):
        rows = slice(g * GROUP, (g + 1) * GROUP)
        answers = jnp.concatenate([from_lower[g], from_upper[g]], axis=0)
        matrices.append(group_matrix(box_table[g] + answers))
        rates.append(1.0 / stokes[rows, :])
        kept = g * GROUP + lax.broadcasted_iota(jnp.int32, rates[g].shape, 0) < count
        alive.append(kept)
        start = [jnp.where(kept, state[c, rows, :], 0.0) for c in range(6)]
        carry.append((start[:3], start[3:]))
    for _ in range(SUBSTEPS):
        moved = []
        for g in range(groups):
            position, velocity = carry[g]
            rate = rates[g]
            middle_pos = [x + 0.5 * STEP_SIZE * v for x, v in zip(position, velocity)]
            here = sample(matrices[g], position)
            there = sample(matrices[g], middle_pos)
            middle_vel = [v + 0.5 * STEP_SIZE * ((u - v) * rate) for u, v in zip(here, velocity)]
            moved.append(
                (
                    [x + STEP_SIZE * m for x, m in zip(position, middle_vel)],
                    [v + STEP_SIZE * (u - m) * rate for v, u, m in zip(velocity, there, middle_vel)],
                )
            )
        carry = moved
    for g in range(groups):
        rows = slice(g * GROUP, (g + 1) * GROUP)
        for c, value in enumerate([*carry[g][0], *carry[g][1]]):
            out[c, rows, :] = jnp.where(alive[g], value, state[c, rows, :])
    if groups < box_table.shape[0]:
        out[:, groups * GROUP :, :] = state[:, groups * GROUP :, :]


def move_kernel(live, box_table, from_lower, from_upper, state, stokes, out):
    count = live[0]
    groups = box_table.shape[0]
    fewer = 0
    for some in sorted({1, max(1, groups // 2), groups}):

        @pl.when((count > fewer * GROUP) & (count <= some * GROUP))
        def _(some=some):
            move_groups(some, count, box_table, from_lower, from_upper, state, stokes, out)

        fewer = some


def in_smem():
    return pl.BlockSpec(memory_space=pltpu.SMEM)


def in_vmem():
    return pl.BlockSpec(memory_space=pltpu.VMEM)


def exchange(near, far, axis):
    devices = lax.axis_size(axis)
    near_pairs = [(i, i ^ 1) for i in range(devices)]
    far_pairs = [(i, (i + 1 if i % 2 else i - 1) % devices) for i in range(devices)]
    far = lax.ppermute(far, axis, far_pairs)
    return lax.ppermute(near, axis, near_pairs), far


def shift(array, axis, step):
    devices = lax.axis_size(axis)
    return lax.ppermute(array, axis, [(i, (i + step) % devices) for i in range(devices)])


def body(velocity_field, particle_state, stokes_time, box_base, live_bins):
    comps, depth, length, cells = velocity_field.shape
    bins = box_base.shape[0]
    tiles = cells // LANES
    groups = bins // GROUP
    table = box_base.T
    state = particle_state.transpose(1, 0, 2)
    block = pltpu.with_memory_space_constraint(velocity_field, pltpu.HBM)
    params = pltpu.CompilerParams(vmem_limit_bytes=VMEM_LIMIT)

    lower_table, upper_table = shift(table, "slab", 1), shift(table, "slab", -1)
    shape = (comps, depth, tiles, length + 2 * TOP)
    planes = depth + 2 * MARGIN
    rows_of_block = pltpu.VMEM((comps, planes * tiles * (length + 2 * TOP), LANES), jnp.float32)
    edge_rows = jax.ShapeDtypeStruct((comps, depth, 2, cells), jnp.float32)
    near, far = pl.pallas_call(
        edges_kernel,
        out_shape=(edge_rows, edge_rows),
        in_specs=[pl.BlockSpec(memory_space=pl.ANY)],
        out_specs=(in_vmem(), in_vmem()),
        scratch_shapes=[pltpu.SemaphoreType.DMA((2,))],
        compiler_params=params,
        name="edges",
    )(block)
    near, far = exchange(near, far, "sub")

    smem_table = pltpu.SMEM(table.shape, jnp.int32)
    padded, own_table = pl.pallas_call(
        load_kernel,
        out_shape=(pltpu.VMEM((comps, planes, tiles, length + 2 * TOP, LANES), jnp.float32), smem_table),
        in_specs=[pl.BlockSpec(memory_space=pl.ANY)] * 2,
        out_specs=(in_vmem(), in_smem()),
        scratch_shapes=[pltpu.SemaphoreType.DMA((1 + tiles,))],
        compiler_params=params,
        cost_estimate=pl.CostEstimate(flops=1_000_000, bytes_accessed=6_000_000, transcendentals=0),
        name="load",
    )(block, pltpu.with_memory_space_constraint(table, pltpu.HBM))

    padded = padded.reshape(rows_of_block.shape)
    hits = pl.pallas_call(
        functools.partial(hits_kernel, depth=depth),
        out_shape=pltpu.SMEM((5, 2 * bins), jnp.int32),
        in_specs=[in_vmem(), in_vmem()],
        out_specs=in_smem(),
        compiler_params=params,
        name="hits",
    )(upper_table, lower_table)
    answer = jax.ShapeDtypeStruct((groups, 8, LANES), jnp.float32)
    for_upper, for_lower, padded = pl.pallas_call(
        functools.partial(answers_kernel, shape=shape),
        out_shape=(answer, answer, rows_of_block),
        in_specs=[in_smem(), in_vmem(), in_vmem(), in_vmem()],
        out_specs=(in_vmem(), in_vmem(), in_vmem()),
        scratch_shapes=[pltpu.VMEM((2 * groups, comps, 8, LANES), jnp.float32)],
        input_output_aliases={1: 2},
        compiler_params=params,
        name="answers",
    )(hits, padded, far, near)
    from_lower, from_upper = shift(for_upper, "slab", 1), shift(for_lower, "slab", -1)

    box_table, _ = pl.pallas_call(
        functools.partial(boxes_kernel, shape=shape),
        out_shape=(jax.ShapeDtypeStruct((groups, NODES, LANES), jnp.float32), rows_of_block),
        in_specs=[in_smem(), in_smem(), in_vmem(), in_vmem(), in_vmem()],
        out_specs=(in_vmem(), in_vmem()),
        scratch_shapes=[pltpu.VMEM((groups, 2, comps, 8, LANES), jnp.float32)],
        input_output_aliases={4: 1},
        compiler_params=params,
        cost_estimate=pl.CostEstimate(flops=1_000_000, bytes_accessed=4_000_000, transcendentals=0),
        name="boxes",
    )(own_table, live_bins, far, near, padded)

    moved = pl.pallas_call(
        move_kernel,
        out_shape=jax.ShapeDtypeStruct(state.shape, jnp.float32),
        in_specs=[in_smem()] + [in_vmem()] * 5,
        out_specs=in_vmem(),
        compiler_params=params,
        name="move",
    )(live_bins, box_table, from_lower, from_upper, state, stokes_time)
    return moved.transpose(1, 0, 2)


def solution(mesh):
    placed = (
        P(None, "slab", "sub", None),
        P(("slab", "sub"), None, None),
        P(("slab", "sub"), None),
        P(("slab", "sub"), None),
        P(("slab", "sub")),
    )
    return jax.shard_map(
        body, mesh=mesh, in_specs=placed, out_specs=P(("slab", "sub"), None, None), check_vma=False
    )
```

```python
import functools

import jax
import jax.numpy as jnp
from jax import lax
from jax.experimental import pallas as pl
from jax.experimental.pallas import tpu as pltpu
from jax.sharding import PartitionSpec as P

SUBSTEPS = 4
STEP_SIZE = 0.2
LANES = 128
LANE_BITS = 7
NODES = 16
GROUP = 8
GROUP_BITS = 3
MARGIN = 2
TOP = 8
UNROLL = 8
VMEM_LIMIT = 32 * 1024 * 1024


def rows_and_lanes():
    return lax.broadcasted_iota(jnp.int32, (8, LANES), 0), lax.broadcasted_iota(jnp.int32, (8, LANES), 1)


def first_rows(shape, first_y, first_z):
    _, _, tiles, rows = shape
    tile = lax.shift_right_logical(first_z, LANE_BITS)
    beside = jnp.where(tile == tiles - 1, 0, tile + 1)
    start = MARGIN * tiles * rows + TOP + first_y
    return start + tile * rows, start + beside * rows, first_z & (LANES - 1)


def gather_pair(padded, shape, x, valid, starts, slot):
    comps, _, tiles, rows = shape
    row, lane = rows_and_lanes()
    here, there, offset = starts
    upper, left = row < 4, lane >= offset
    plane = x * (tiles * rows)
    shift = (NODES * slot - offset) & (LANES - 1)
    wanted = jnp.where(upper, jnp.where(valid[0], 4 * slot, -1), jnp.where(valid[1], 4 * slot, -1))
    found = []
    for c in range(comps):
        near, far = [
            jnp.where(
                upper, padded[c, pl.ds(plane + start, 8), :], padded[c, pl.ds(plane + start + (tiles * rows - 4), 8), :]
            )
            for start in (here, there)
        ]
        found.append(pltpu.roll(jnp.where(left, near, far), shift, 1))
    return found, lax.shift_right_logical(lane, 2) == wanted


def flatten_pair(parts):
    row, _ = rows_and_lanes()
    first, second, third = [pltpu.roll(part, 0, 1, stride=4, stride_axis=0) for part in parts]
    low = jnp.where((row & 1) == 0, first + pltpu.roll(first, 7, 0), second + pltpu.roll(second, 1, 0))
    high = jnp.where((row & 1) == 0, third + pltpu.roll(third, 7, 0), 0.0)
    return jnp.where((row & 2) == 0, low + pltpu.roll(low, 6, 0), high + pltpu.roll(high, 2, 0))


def align_pair(tile):
    row, _ = rows_and_lanes()
    return jnp.where(row < 4, tile, pltpu.roll(tile, LANES - NODES, 1))


def edges_kernel(field, near, far, sems):
    length = field.shape[2]
    even = lax.axis_index("sub") % 2 == 0

    def edge_copies(near_row, far_row):
        return [
            pltpu.make_async_copy(field.at[:, :, pl.ds(row, 2), :], into, sems.at[n])
            for n, (row, into) in enumerate(((near_row, near), (far_row, far)))
        ]

    @pl.when(even)
    def _():
        for copy in edge_copies(length - 2, 0):
            copy.start()

    @pl.when(jnp.logical_not(even))
    def _():
        for copy in edge_copies(0, length - 2):
            copy.start()

    for copy in edge_copies(0, 0):
        copy.wait()


def load_kernel(field, base, padded, table, sems):
    depth, length, cells = field.shape[1:]
    copies = [pltpu.make_async_copy(base, table, sems.at[0])]
    for tile in range(cells // LANES):
        copies.append(
            pltpu.make_async_copy(
                field.at[:, :, :, pl.ds(tile * LANES, LANES)],
                padded.at[:, pl.ds(MARGIN, depth), tile, pl.ds(TOP, length), :],
                sems.at[1 + tile],
            )
        )
    for copy in copies:
        copy.start()
    for copy in copies:
        copy.wait()


def fill_halo(padded, shape, far, near, planes):
    comps, _, tiles, rows = shape
    even = lax.axis_index("sub") % 2 == 0
    below, above = TOP - 2, rows - TOP
    near_row, far_row = jnp.where(even, above, below), jnp.where(even, below, above)
    for c in range(comps):
        for x in planes:
            for tile in range(tiles):
                lanes = slice(tile * LANES, (tile + 1) * LANES)
                start = ((MARGIN + x) * tiles + tile) * rows
                padded[c, pl.ds(start + near_row, 2), :] = near[c, x, :, lanes]
                padded[c, pl.ds(start + far_row, 2), :] = far[c, x, :, lanes]


def boxes_kernel(table, live, far, near, padded_in, box_table, padded, acc, *, shape):
    comps, depth = shape[:2]
    fill_halo(padded, shape, far, near, range(2, depth - 2))
    acc[...] = jnp.zeros_like(acc)

    def one_group(group, _):
        parts = [[jnp.zeros((8, LANES), jnp.float32)] * comps for _ in range(2)]
        for slot in range(GROUP):
            b = group * GROUP + slot
            x = table[0, b]
            starts = first_rows(shape, table[1, b], table[2, b])
            valid = ((x >= 0, x >= -1), (x < depth - 2, x < depth - 3))
            for pair in range(2):
                found, mask = gather_pair(padded, shape, x + 2 * pair, valid[pair], starts, slot)
                parts[pair] = [jnp.where(mask, new, old) for new, old in zip(found, parts[pair])]
        for pair in range(2):
            for c in range(comps):
                acc[group, pair, c] = parts[pair][c]
        return 0

    lax.fori_loop(0, (live[0] + GROUP - 1) // GROUP, one_group, 0)
    for group in range(box_table.shape[0]):
        for pair in range(2):
            rows = flatten_pair([acc[group, pair, c] for c in range(comps)])
            box_table[group, 8 * pair : 8 * pair + 8, :] = align_pair(rows)


def hits_kernel(upper_base, lower_base, hits, *, depth):
    bins = upper_base.shape[1]
    row = lax.broadcasted_iota(jnp.int32, (8, bins), 0)
    lane = lax.broadcasted_iota(jnp.int32, (8, bins), 1)
    x, y, z = [jnp.where(row == 0, upper_base[d : d + 1, :], lower_base[d : d + 1, :]) for d in range(3)]
    wanted = ((row == 0) & (x < 0)) | ((row == 1) & (x > depth - 4))
    marks = jnp.where(wanted, 1.0, 0.0)
    earlier = lax.broadcasted_iota(jnp.int32, (bins, bins), 0) < lax.broadcasted_iota(jnp.int32, (bins, bins), 1)
    rank = jnp.dot(marks, jnp.where(earlier, 1.0, 0.0), preferred_element_type=jnp.float32)
    rank = jnp.where(row == 1, rank + jnp.sum(marks[0:1], axis=1, keepdims=True), rank)
    rank = jnp.where(wanted, rank, -1.0)
    places = ((row * bins + lane) * 64 + (x + 2)).astype(jnp.float32)
    cells = (z * 64 + (y + 2)).astype(jnp.float32)
    found = jnp.sum(marks).astype(jnp.int32)
    hits[4, 0] = found

    def some_hits(n, _):
        for k in range(UNROLL):
            at = n * UNROLL + k
            chosen = rank == at.astype(jnp.float32)
            place = jnp.sum(jnp.where(chosen, places, 0.0)).astype(jnp.int32)
            cell = jnp.sum(jnp.where(chosen, cells, 0.0)).astype(jnp.int32)
            hits[0, at] = lax.shift_right_logical(place, 6)
            hits[1, at] = (place & 63) - 2
            hits[2, at] = (cell & 63) - 2
            hits[3, at] = lax.shift_right_logical(cell, 6)
        return 0

    lax.fori_loop(0, (found + UNROLL - 1) // UNROLL, some_hits, 0)


def answers_kernel(hits, padded_in, far, near, upper_out, lower_out, padded, acc, *, shape):
    comps, depth = shape[:2]
    groups = upper_out.shape[0]
    bins = groups * GROUP
    fill_halo(padded, shape, far, near, [0, 1, depth - 2, depth - 1])
    acc[...] = jnp.zeros_like(acc)
    found = hits[4, 0]

    def some_bins(n, _):
        for k in range(UNROLL):
            at = n * UNROLL + k
            n_th = jnp.minimum(at, found - 1)
            entry, first_x, first_y, first_z = [hits[d, n_th] for d in range(4)]
            from_upper = entry < bins
            x = first_x + jnp.where(from_upper, depth, 2 - depth)
            valid = [(at < found) & (cell >= 0) & (cell < depth) for cell in (x, x + 1)]
            starts = first_rows(shape, first_y, first_z)
            gathered, mask = gather_pair(padded, shape, x, valid, starts, entry & (GROUP - 1))
            group = lax.shift_right_logical(entry, GROUP_BITS)
            for c in range(comps):
                acc[group, c] += jnp.where(mask, gathered[c], 0.0)
        return 0

    lax.fori_loop(0, (found + UNROLL - 1) // UNROLL, some_bins, 0)
    for g in range(groups):
        upper_out[g] = align_pair(flatten_pair([acc[g, c] for c in range(comps)]))
        lower_out[g] = align_pair(flatten_pair([acc[groups + g, c] for c in range(comps)]))


def unscaled_weights(t):
    plus, minus, minus_two = t + 1.0, t - 1.0, t - 2.0
    inner, outer = t * minus, plus * minus_two
    return inner * minus_two, outer * minus, outer * t, inner * plus


def node_factor(node):
    return jnp.where(node == 0, -1.0 / 6.0, jnp.where(node == 1, 0.5, jnp.where(node == 2, -0.5, 1.0 / 6.0)))


def split(x):
    head = x.astype(jnp.bfloat16)
    return head, (x - head.astype(jnp.float32)).astype(jnp.bfloat16)


def group_matrix(box):
    row = lax.broadcasted_iota(jnp.int32, box.shape, 0)
    lane = lax.broadcasted_iota(jnp.int32, box.shape, 1)
    box = box * (node_factor(row // 4) * node_factor(lane // 4 % 4) * node_factor(lane % 4))
    box = jnp.take_along_axis(box, lane % GROUP * NODES + lane // GROUP, axis=1)
    head = box.astype(jnp.bfloat16).astype(jnp.float32)
    own = lax.broadcasted_iota(jnp.int32, (GROUP, LANES), 1) % GROUP == lax.broadcasted_iota(
        jnp.int32, (GROUP, LANES), 0
    )

    def spread(part):
        rows = [
            jnp.where(own, jnp.broadcast_to(part[4 * i + c : 4 * i + c + 1], (GROUP, LANES)), 0.0)
            for i in range(4)
            for c in range(3)
        ]
        return jnp.concatenate(rows, axis=0).astype(jnp.bfloat16)

    heads, tails = spread(head), spread(box - head)
    return jnp.concatenate(
        [jnp.concatenate([heads, heads], axis=1), jnp.concatenate([tails, jnp.zeros_like(tails)], axis=1)], axis=0
    )


def sample(matrix, position):
    along_x, along_y, along_z = (unscaled_weights(t) for t in position)
    weights = jnp.concatenate([y * z for y in along_y for z in along_z], axis=0)
    head, tail = split(weights)
    planes = jnp.dot(matrix, jnp.concatenate([head, tail], axis=0), preferred_element_type=jnp.float32)
    half = planes.shape[0] // 2
    planes = planes[:half] + planes[half:]
    result = []
    for c in range(3):
        plane = [planes[8 * (3 * i + c) : 8 * (3 * i + c) + 8] for i in range(4)]
        result.append(
            (plane[0] * along_x[0] + plane[1] * along_x[1]) + (plane[2] * along_x[2] + plane[3] * along_x[3])
        )
    return result


def move_groups(groups, count, box_table, from_lower, from_upper, state, stokes, out):
    matrices, carry, rates, alive = [], [], [], []
    for g in range(groups):
        rows = slice(g * GROUP, (g + 1) * GROUP)
        answers = jnp.concatenate([from_lower[g], from_upper[g]], axis=0)
        matrices.append(group_matrix(box_table[g] + answers))
        rates.append(1.0 / stokes[rows, :])
        kept = g * GROUP + lax.broadcasted_iota(jnp.int32, rates[g].shape, 0) < count
        alive.append(kept)
        start = [jnp.where(kept, state[c, rows, :], 0.0) for c in range(6)]
        carry.append((start[:3], start[3:]))
    for _ in range(SUBSTEPS):
        moved = []
        for g in range(groups):
            position, velocity = carry[g]
            rate = rates[g]
            middle_pos = [x + 0.5 * STEP_SIZE * v for x, v in zip(position, velocity)]
            here = sample(matrices[g], position)
            there = sample(matrices[g], middle_pos)
            middle_vel = [v + 0.5 * STEP_SIZE * ((u - v) * rate) for u, v in zip(here, velocity)]
            moved.append(
                (
                    [x + STEP_SIZE * m for x, m in zip(position, middle_vel)],
                    [v + STEP_SIZE * (u - m) * rate for v, u, m in zip(velocity, there, middle_vel)],
                )
            )
        carry = moved
    for g in range(groups):
        rows = slice(g * GROUP, (g + 1) * GROUP)
        for c, value in enumerate([*carry[g][0], *carry[g][1]]):
            out[c, rows, :] = jnp.where(alive[g], value, state[c, rows, :])
    if groups < box_table.shape[0]:
        out[:, groups * GROUP :, :] = state[:, groups * GROUP :, :]


def move_kernel(live, box_table, from_lower, from_upper, state, stokes, out):
    count = live[0]
    groups = box_table.shape[0]
    fewer = 0
    for some in sorted({1, max(1, groups // 2), groups}):

        @pl.when((count > fewer * GROUP) & (count <= some * GROUP))
        def _(some=some):
            move_groups(some, count, box_table, from_lower, from_upper, state, stokes, out)

        fewer = some


def in_smem():
    return pl.BlockSpec(memory_space=pltpu.SMEM)


def in_vmem():
    return pl.BlockSpec(memory_space=pltpu.VMEM)


def exchange(near, far, axis):
    devices = lax.axis_size(axis)
    near_pairs = [(i, i ^ 1) for i in range(devices)]
    far_pairs = [(i, (i + 1 if i % 2 else i - 1) % devices) for i in range(devices)]
    far = lax.ppermute(far, axis, far_pairs)
    return lax.ppermute(near, axis, near_pairs), far


def shift(array, axis, step):
    devices = lax.axis_size(axis)
    return lax.ppermute(array, axis, [(i, (i + step) % devices) for i in range(devices)])


def body(velocity_field, particle_state, stokes_time, box_base, live_bins):
    comps, depth, length, cells = velocity_field.shape
    bins = box_base.shape[0]
    tiles = cells // LANES
    groups = bins // GROUP
    table = box_base.T
    state = particle_state.transpose(1, 0, 2)
    block = pltpu.with_memory_space_constraint(velocity_field, pltpu.HBM)
    params = pltpu.CompilerParams(vmem_limit_bytes=VMEM_LIMIT)

    lower_table, upper_table = shift(table, "slab", 1), shift(table, "slab", -1)
    shape = (comps, depth, tiles, length + 2 * TOP)
    planes = depth + 2 * MARGIN
    rows_of_block = pltpu.VMEM((comps, planes * tiles * (length + 2 * TOP), LANES), jnp.float32)
    edge_rows = jax.ShapeDtypeStruct((comps, depth, 2, cells), jnp.float32)
    near, far = pl.pallas_call(
        edges_kernel,
        out_shape=(edge_rows, edge_rows),
        in_specs=[pl.BlockSpec(memory_space=pl.ANY)],
        out_specs=(in_vmem(), in_vmem()),
        scratch_shapes=[pltpu.SemaphoreType.DMA((2,))],
        compiler_params=params,
        name="edges",
    )(block)
    near, far = exchange(near, far, "sub")

    smem_table = pltpu.SMEM(table.shape, jnp.int32)
    padded, own_table = pl.pallas_call(
        load_kernel,
        out_shape=(pltpu.VMEM((comps, planes, tiles, length + 2 * TOP, LANES), jnp.float32), smem_table),
        in_specs=[pl.BlockSpec(memory_space=pl.ANY)] * 2,
        out_specs=(in_vmem(), in_smem()),
        scratch_shapes=[pltpu.SemaphoreType.DMA((1 + tiles,))],
        compiler_params=params,
        cost_estimate=pl.CostEstimate(flops=1_000_000, bytes_accessed=6_000_000, transcendentals=0),
        name="load",
    )(block, pltpu.with_memory_space_constraint(table, pltpu.HBM))

    padded = padded.reshape(rows_of_block.shape)
    hits = pl.pallas_call(
        functools.partial(hits_kernel, depth=depth),
        out_shape=pltpu.SMEM((5, 2 * bins), jnp.int32),
        in_specs=[in_vmem(), in_vmem()],
        out_specs=in_smem(),
        compiler_params=params,
        name="hits",
    )(upper_table, lower_table)
    answer = jax.ShapeDtypeStruct((groups, 8, LANES), jnp.float32)
    for_upper, for_lower, padded = pl.pallas_call(
        functools.partial(answers_kernel, shape=shape),
        out_shape=(answer, answer, rows_of_block),
        in_specs=[in_smem(), in_vmem(), in_vmem(), in_vmem()],
        out_specs=(in_vmem(), in_vmem(), in_vmem()),
        scratch_shapes=[pltpu.VMEM((2 * groups, comps, 8, LANES), jnp.float32)],
        input_output_aliases={1: 2},
        compiler_params=params,
        name="answers",
    )(hits, padded, far, near)
    from_lower, from_upper = shift(for_upper, "slab", 1), shift(for_lower, "slab", -1)

    box_table, _ = pl.pallas_call(
        functools.partial(boxes_kernel, shape=shape),
        out_shape=(jax.ShapeDtypeStruct((groups, NODES, LANES), jnp.float32), rows_of_block),
        in_specs=[in_smem(), in_smem(), in_vmem(), in_vmem(), in_vmem()],
        out_specs=(in_vmem(), in_vmem()),
        scratch_shapes=[pltpu.VMEM((groups, 2, comps, 8, LANES), jnp.float32)],
        input_output_aliases={4: 1},
        compiler_params=params,
        cost_estimate=pl.CostEstimate(flops=1_000_000, bytes_accessed=4_000_000, transcendentals=0),
        name="boxes",
    )(own_table, live_bins, far, near, padded)

    moved = pl.pallas_call(
        move_kernel,
        out_shape=jax.ShapeDtypeStruct(state.shape, jnp.float32),
        in_specs=[in_smem()] + [in_vmem()] * 5,
        out_specs=in_vmem(),
        compiler_params=params,
        name="move",
    )(live_bins, box_table, from_lower, from_upper, state, stokes_time)
    return moved.transpose(1, 0, 2)


def solution(mesh):
    placed = (
        P(None, "slab", "sub", None),
        P(("slab", "sub"), None, None),
        P(("slab", "sub"), None),
        P(("slab", "sub"), None),
        P(("slab", "sub")),
    )
    return jax.shard_map(
        body, mesh=mesh, in_specs=placed, out_specs=P(("slab", "sub"), None, None), check_vma=False
    )
```

```python
import functools

import jax
import jax.numpy as jnp
from jax import lax
from jax.experimental import pallas as pl
from jax.experimental.pallas import tpu as pltpu
from jax.sharding import PartitionSpec as P

SUBSTEPS = 4
STEP_SIZE = 0.2
LANES = 128
LANE_BITS = 7
NODES = 16
GROUP = 8
GROUP_BITS = 3
MARGIN = 2
TOP = 8
UNROLL = 8
ALWAYS = 16
VMEM_LIMIT = 32 * 1024 * 1024


def rows_and_lanes():
    return lax.broadcasted_iota(jnp.int32, (8, LANES), 0), lax.broadcasted_iota(jnp.int32, (8, LANES), 1)


def first_rows(shape, first_y, first_z):
    _, _, tiles, rows = shape
    tile = lax.shift_right_logical(first_z, LANE_BITS)
    beside = jnp.where(tile == tiles - 1, 0, tile + 1)
    start = MARGIN * tiles * rows + TOP + first_y
    return start + tile * rows, start + beside * rows, first_z & (LANES - 1)


def gather_pair(padded, shape, x, valid, starts, slot):
    comps, _, tiles, rows = shape
    row, lane = rows_and_lanes()
    here, there, offset = starts
    upper, left = row < 4, lane >= offset
    plane = x * (tiles * rows)
    shift = (NODES * slot - offset) & (LANES - 1)
    wanted = jnp.where(upper, jnp.where(valid[0], 4 * slot, -1), jnp.where(valid[1], 4 * slot, -1))
    found = []
    for c in range(comps):
        near, far = [
            jnp.where(
                upper, padded[c, pl.ds(plane + start, 8), :], padded[c, pl.ds(plane + start + (tiles * rows - 4), 8), :]
            )
            for start in (here, there)
        ]
        found.append(pltpu.roll(jnp.where(left, near, far), shift, 1))
    return found, lax.shift_right_logical(lane, 2) == wanted


def flatten_pair(parts):
    row, _ = rows_and_lanes()
    first, second, third = [pltpu.roll(part, 0, 1, stride=4, stride_axis=0) for part in parts]
    low = jnp.where((row & 1) == 0, first + pltpu.roll(first, 7, 0), second + pltpu.roll(second, 1, 0))
    high = jnp.where((row & 1) == 0, third + pltpu.roll(third, 7, 0), 0.0)
    return jnp.where((row & 2) == 0, low + pltpu.roll(low, 6, 0), high + pltpu.roll(high, 2, 0))


def align_pair(tile):
    row, _ = rows_and_lanes()
    return jnp.where(row < 4, tile, pltpu.roll(tile, LANES - NODES, 1))


def edges_kernel(field, near, far, sems):
    length = field.shape[2]
    even = lax.axis_index("sub") % 2 == 0

    def edge_copies(near_row, far_row):
        return [
            pltpu.make_async_copy(field.at[:, :, pl.ds(row, 2), :], into, sems.at[n])
            for n, (row, into) in enumerate(((near_row, near), (far_row, far)))
        ]

    @pl.when(even)
    def _():
        for copy in edge_copies(length - 2, 0):
            copy.start()

    @pl.when(jnp.logical_not(even))
    def _():
        for copy in edge_copies(0, length - 2):
            copy.start()

    for copy in edge_copies(0, 0):
        copy.wait()


def load_kernel(field, base, padded, table, sems):
    depth, length, cells = field.shape[1:]
    copies = [pltpu.make_async_copy(base, table, sems.at[0])]
    for tile in range(cells // LANES):
        copies.append(
            pltpu.make_async_copy(
                field.at[:, :, :, pl.ds(tile * LANES, LANES)],
                padded.at[:, pl.ds(MARGIN, depth), tile, pl.ds(TOP, length), :],
                sems.at[1 + tile],
            )
        )
    for copy in copies:
        copy.start()
    for copy in copies:
        copy.wait()


def fill_halo(padded, shape, far, near, planes):
    comps, _, tiles, rows = shape
    even = lax.axis_index("sub") % 2 == 0
    below, above = TOP - 2, rows - TOP
    near_row, far_row = jnp.where(even, above, below), jnp.where(even, below, above)
    for c in range(comps):
        for x in planes:
            for tile in range(tiles):
                lanes = slice(tile * LANES, (tile + 1) * LANES)
                start = ((MARGIN + x) * tiles + tile) * rows
                padded[c, pl.ds(start + near_row, 2), :] = near[c, x, :, lanes]
                padded[c, pl.ds(start + far_row, 2), :] = far[c, x, :, lanes]


def boxes_kernel(table, live, far, near, padded_in, box_table, padded, acc, *, shape):
    comps, depth = shape[:2]
    fill_halo(padded, shape, far, near, range(2, depth - 2))
    acc[...] = jnp.zeros_like(acc)

    def one_group(group, _):
        parts = [[jnp.zeros((8, LANES), jnp.float32)] * comps for _ in range(2)]
        for slot in range(GROUP):
            b = group * GROUP + slot
            x = table[0, b]
            starts = first_rows(shape, table[1, b], table[2, b])
            valid = ((x >= 0, x >= -1), (x < depth - 2, x < depth - 3))
            for pair in range(2):
                found, mask = gather_pair(padded, shape, x + 2 * pair, valid[pair], starts, slot)
                parts[pair] = [jnp.where(mask, new, old) for new, old in zip(found, parts[pair])]
        for pair in range(2):
            for c in range(comps):
                acc[group, pair, c] = parts[pair][c]
        return 0

    lax.fori_loop(0, (live[0] + GROUP - 1) // GROUP, one_group, 0)
    for group in range(box_table.shape[0]):
        for pair in range(2):
            rows = flatten_pair([acc[group, pair, c] for c in range(comps)])
            box_table[group, 8 * pair : 8 * pair + 8, :] = align_pair(rows)


def hits_kernel(upper_base, lower_base, hits, *, depth):
    bins = upper_base.shape[1]
    row = lax.broadcasted_iota(jnp.int32, (8, bins), 0)
    lane = lax.broadcasted_iota(jnp.int32, (8, bins), 1)
    x, y, z = [jnp.where(row == 0, upper_base[d : d + 1, :], lower_base[d : d + 1, :]) for d in range(3)]
    wanted = ((row == 0) & (x < 0)) | ((row == 1) & (x > depth - 4))
    marks = jnp.where(wanted, 1.0, 0.0)
    earlier = lax.broadcasted_iota(jnp.int32, (bins, bins), 0) < lax.broadcasted_iota(jnp.int32, (bins, bins), 1)
    rank = jnp.dot(marks, jnp.where(earlier, 1.0, 0.0), preferred_element_type=jnp.float32)
    rank = jnp.where(row == 1, rank + jnp.sum(marks[0:1], axis=1, keepdims=True), rank)
    rank = jnp.where(wanted, rank, -1.0)
    places = ((row * bins + lane) * 64 + (x + 2)).astype(jnp.float32)
    cells = (z * 64 + (y + 2)).astype(jnp.float32)
    found = jnp.sum(marks).astype(jnp.int32)
    hits[4, 0] = found

    def list_hit(at, chosen):
        place = jnp.sum(jnp.where(chosen, places, 0.0)).astype(jnp.int32)
        cell = jnp.sum(jnp.where(chosen, cells, 0.0)).astype(jnp.int32)
        hits[0, at] = lax.shift_right_logical(place, 6)
        hits[1, at] = (place & 63) - 2
        hits[2, at] = (cell & 63) - 2
        hits[3, at] = lax.shift_right_logical(cell, 6)

    for at in range(ALWAYS):
        list_hit(at, rank == float(at))

    def some_hits(n, _):
        for k in range(UNROLL):
            at = ALWAYS + n * UNROLL + k
            list_hit(at, rank == at.astype(jnp.float32))
        return 0

    lax.fori_loop(0, (jnp.maximum(found - ALWAYS, 0) + UNROLL - 1) // UNROLL, some_hits, 0)


def answers_kernel(hits, padded_in, far, near, upper_out, lower_out, padded, acc, *, shape):
    comps, depth = shape[:2]
    groups = upper_out.shape[0]
    bins = groups * GROUP
    fill_halo(padded, shape, far, near, [0, 1, depth - 2, depth - 1])
    acc[...] = jnp.zeros_like(acc)
    found = hits[4, 0]

    def some_bins(n, _):
        for k in range(UNROLL):
            at = n * UNROLL + k
            n_th = jnp.minimum(at, found - 1)
            entry, first_x, first_y, first_z = [hits[d, n_th] for d in range(4)]
            from_upper = entry < bins
            x = first_x + jnp.where(from_upper, depth, 2 - depth)
            valid = [(at < found) & (cell >= 0) & (cell < depth) for cell in (x, x + 1)]
            starts = first_rows(shape, first_y, first_z)
            gathered, mask = gather_pair(padded, shape, x, valid, starts, entry & (GROUP - 1))
            group = lax.shift_right_logical(entry, GROUP_BITS)
            for c in range(comps):
                acc[group, c] += jnp.where(mask, gathered[c], 0.0)
        return 0

    lax.fori_loop(0, (found + UNROLL - 1) // UNROLL, some_bins, 0)
    for g in range(groups):
        upper_out[g] = align_pair(flatten_pair([acc[g, c] for c in range(comps)]))
        lower_out[g] = align_pair(flatten_pair([acc[groups + g, c] for c in range(comps)]))


def unscaled_weights(t):
    plus, minus, minus_two = t + 1.0, t - 1.0, t - 2.0
    inner, outer = t * minus, plus * minus_two
    return inner * minus_two, outer * minus, outer * t, inner * plus


def node_factor(node):
    return jnp.where(node == 0, -1.0 / 6.0, jnp.where(node == 1, 0.5, jnp.where(node == 2, -0.5, 1.0 / 6.0)))


def split(x):
    head = x.astype(jnp.bfloat16)
    return head, (x - head.astype(jnp.float32)).astype(jnp.bfloat16)


def group_matrix(box):
    row = lax.broadcasted_iota(jnp.int32, box.shape, 0)
    lane = lax.broadcasted_iota(jnp.int32, box.shape, 1)
    box = box * (node_factor(row // 4) * node_factor(lane // 4 % 4) * node_factor(lane % 4))
    box = jnp.take_along_axis(box, lane % GROUP * NODES + lane // GROUP, axis=1)
    head = box.astype(jnp.bfloat16).astype(jnp.float32)
    own = lax.broadcasted_iota(jnp.int32, (GROUP, LANES), 1) % GROUP == lax.broadcasted_iota(
        jnp.int32, (GROUP, LANES), 0
    )

    def spread(part):
        rows = [
            jnp.where(own, jnp.broadcast_to(part[4 * i + c : 4 * i + c + 1], (GROUP, LANES)), 0.0)
            for i in range(4)
            for c in range(3)
        ]
        return jnp.concatenate(rows, axis=0).astype(jnp.bfloat16)

    heads, tails = spread(head), spread(box - head)
    return jnp.concatenate(
        [jnp.concatenate([heads, heads], axis=1), jnp.concatenate([tails, jnp.zeros_like(tails)], axis=1)], axis=0
    )


def sample(matrix, position):
    along_x, along_y, along_z = (unscaled_weights(t) for t in position)
    weights = jnp.concatenate([y * z for y in along_y for z in along_z], axis=0)
    head, tail = split(weights)
    planes = jnp.dot(matrix, jnp.concatenate([head, tail], axis=0), preferred_element_type=jnp.float32)
    half = planes.shape[0] // 2
    planes = planes[:half] + planes[half:]
    result = []
    for c in range(3):
        plane = [planes[8 * (3 * i + c) : 8 * (3 * i + c) + 8] for i in range(4)]
        result.append(
            (plane[0] * along_x[0] + plane[1] * along_x[1]) + (plane[2] * along_x[2] + plane[3] * along_x[3])
        )
    return result


def move_groups(groups, count, box_table, from_lower, from_upper, state, stokes, out):
    matrices, carry, rates, alive = [], [], [], []
    for g in range(groups):
        rows = slice(g * GROUP, (g + 1) * GROUP)
        answers = jnp.concatenate([from_lower[g], from_upper[g]], axis=0)
        matrices.append(group_matrix(box_table[g] + answers))
        rates.append(1.0 / stokes[rows, :])
        kept = g * GROUP + lax.broadcasted_iota(jnp.int32, rates[g].shape, 0) < count
        alive.append(kept)
        start = [jnp.where(kept, state[c, rows, :], 0.0) for c in range(6)]
        carry.append((start[:3], start[3:]))
    for _ in range(SUBSTEPS):
        moved = []
        for g in range(groups):
            position, velocity = carry[g]
            rate = rates[g]
            middle_pos = [x + 0.5 * STEP_SIZE * v for x, v in zip(position, velocity)]
            here = sample(matrices[g], position)
            there = sample(matrices[g], middle_pos)
            middle_vel = [v + 0.5 * STEP_SIZE * ((u - v) * rate) for u, v in zip(here, velocity)]
            moved.append(
                (
                    [x + STEP_SIZE * m for x, m in zip(position, middle_vel)],
                    [v + STEP_SIZE * (u - m) * rate for v, u, m in zip(velocity, there, middle_vel)],
                )
            )
        carry = moved
    for g in range(groups):
        rows = slice(g * GROUP, (g + 1) * GROUP)
        for c, value in enumerate([*carry[g][0], *carry[g][1]]):
            out[c, rows, :] = jnp.where(alive[g], value, state[c, rows, :])
    if groups < box_table.shape[0]:
        out[:, groups * GROUP :, :] = state[:, groups * GROUP :, :]


def move_kernel(live, box_table, from_lower, from_upper, state, stokes, out):
    count = live[0]
    groups = box_table.shape[0]
    fewer = 0
    for some in sorted({1, max(1, groups // 2), groups}):

        @pl.when((count > fewer * GROUP) & (count <= some * GROUP))
        def _(some=some):
            move_groups(some, count, box_table, from_lower, from_upper, state, stokes, out)

        fewer = some


def in_smem():
    return pl.BlockSpec(memory_space=pltpu.SMEM)


def in_vmem():
    return pl.BlockSpec(memory_space=pltpu.VMEM)


def exchange(near, far, axis):
    devices = lax.axis_size(axis)
    near_pairs = [(i, i ^ 1) for i in range(devices)]
    far_pairs = [(i, (i + 1 if i % 2 else i - 1) % devices) for i in range(devices)]
    far = lax.ppermute(far, axis, far_pairs)
    return lax.ppermute(near, axis, near_pairs), far


def shift(array, axis, step):
    devices = lax.axis_size(axis)
    return lax.ppermute(array, axis, [(i, (i + step) % devices) for i in range(devices)])


def body(velocity_field, particle_state, stokes_time, box_base, live_bins):
    comps, depth, length, cells = velocity_field.shape
    bins = box_base.shape[0]
    tiles = cells // LANES
    groups = bins // GROUP
    table = box_base.T
    state = particle_state.transpose(1, 0, 2)
    block = pltpu.with_memory_space_constraint(velocity_field, pltpu.HBM)
    params = pltpu.CompilerParams(vmem_limit_bytes=VMEM_LIMIT)

    lower_table, upper_table = shift(table, "slab", 1), shift(table, "slab", -1)
    shape = (comps, depth, tiles, length + 2 * TOP)
    planes = depth + 2 * MARGIN
    rows_of_block = pltpu.VMEM((comps, planes * tiles * (length + 2 * TOP), LANES), jnp.float32)
    edge_rows = jax.ShapeDtypeStruct((comps, depth, 2, cells), jnp.float32)
    near, far = pl.pallas_call(
        edges_kernel,
        out_shape=(edge_rows, edge_rows),
        in_specs=[pl.BlockSpec(memory_space=pl.ANY)],
        out_specs=(in_vmem(), in_vmem()),
        scratch_shapes=[pltpu.SemaphoreType.DMA((2,))],
        compiler_params=params,
        name="edges",
    )(block)
    near, far = exchange(near, far, "sub")

    smem_table = pltpu.SMEM(table.shape, jnp.int32)
    padded, own_table = pl.pallas_call(
        load_kernel,
        out_shape=(pltpu.VMEM((comps, planes, tiles, length + 2 * TOP, LANES), jnp.float32), smem_table),
        in_specs=[pl.BlockSpec(memory_space=pl.ANY)] * 2,
        out_specs=(in_vmem(), in_smem()),
        scratch_shapes=[pltpu.SemaphoreType.DMA((1 + tiles,))],
        compiler_params=params,
        cost_estimate=pl.CostEstimate(flops=1_000_000, bytes_accessed=6_000_000, transcendentals=0),
        name="load",
    )(block, pltpu.with_memory_space_constraint(table, pltpu.HBM))

    padded = padded.reshape(rows_of_block.shape)
    hits = pl.pallas_call(
        functools.partial(hits_kernel, depth=depth),
        out_shape=pltpu.SMEM((5, 2 * bins), jnp.int32),
        in_specs=[in_vmem(), in_vmem()],
        out_specs=in_smem(),
        compiler_params=params,
        name="hits",
    )(upper_table, lower_table)
    answer = jax.ShapeDtypeStruct((groups, 8, LANES), jnp.float32)
    for_upper, for_lower, padded = pl.pallas_call(
        functools.partial(answers_kernel, shape=shape),
        out_shape=(answer, answer, rows_of_block),
        in_specs=[in_smem(), in_vmem(), in_vmem(), in_vmem()],
        out_specs=(in_vmem(), in_vmem(), in_vmem()),
        scratch_shapes=[pltpu.VMEM((2 * groups, comps, 8, LANES), jnp.float32)],
        input_output_aliases={1: 2},
        compiler_params=params,
        name="answers",
    )(hits, padded, far, near)
    from_lower, from_upper = shift(for_upper, "slab", 1), shift(for_lower, "slab", -1)

    box_table, _ = pl.pallas_call(
        functools.partial(boxes_kernel, shape=shape),
        out_shape=(jax.ShapeDtypeStruct((groups, NODES, LANES), jnp.float32), rows_of_block),
        in_specs=[in_smem(), in_smem(), in_vmem(), in_vmem(), in_vmem()],
        out_specs=(in_vmem(), in_vmem()),
        scratch_shapes=[pltpu.VMEM((groups, 2, comps, 8, LANES), jnp.float32)],
        input_output_aliases={4: 1},
        compiler_params=params,
        cost_estimate=pl.CostEstimate(flops=1_000_000, bytes_accessed=4_000_000, transcendentals=0),
        name="boxes",
    )(own_table, live_bins, far, near, padded)

    moved = pl.pallas_call(
        move_kernel,
        out_shape=jax.ShapeDtypeStruct(state.shape, jnp.float32),
        in_specs=[in_smem()] + [in_vmem()] * 5,
        out_specs=in_vmem(),
        compiler_params=params,
        name="move",
    )(live_bins, box_table, from_lower, from_upper, state, stokes_time)
    return moved.transpose(1, 0, 2)


def solution(mesh):
    placed = (
        P(None, "slab", "sub", None),
        P(("slab", "sub"), None, None),
        P(("slab", "sub"), None),
        P(("slab", "sub"), None),
        P(("slab", "sub")),
    )
    return jax.shard_map(
        body, mesh=mesh, in_specs=placed, out_specs=P(("slab", "sub"), None, None), check_vma=False
    )
```

```python
import functools

import jax
import jax.numpy as jnp
from jax import lax
from jax.experimental import pallas as pl
from jax.experimental.pallas import tpu as pltpu
from jax.sharding import PartitionSpec as P

SUBSTEPS = 4
STEP_SIZE = 0.2
LANES = 128
LANE_BITS = 7
NODES = 16
GROUP = 8
GROUP_BITS = 3
MARGIN = 2
TOP = 8
UNROLL = 8
ALWAYS = 16
VMEM_LIMIT = 32 * 1024 * 1024


def rows_and_lanes():
    return lax.broadcasted_iota(jnp.int32, (8, LANES), 0), lax.broadcasted_iota(jnp.int32, (8, LANES), 1)


def first_rows(shape, first_y, first_z):
    _, _, tiles, rows = shape
    tile = lax.shift_right_logical(first_z, LANE_BITS)
    beside = jnp.where(tile == tiles - 1, 0, tile + 1)
    start = MARGIN * tiles * rows + TOP + first_y
    return start + tile * rows, start + beside * rows, first_z & (LANES - 1)


def gather_pair(padded, shape, x, valid, starts, slot):
    comps, _, tiles, rows = shape
    row, lane = rows_and_lanes()
    here, there, offset = starts
    upper, left = row < 4, lane >= offset
    plane = x * (tiles * rows)
    shift = (NODES * slot - offset) & (LANES - 1)
    wanted = jnp.where(upper, jnp.where(valid[0], 4 * slot, -1), jnp.where(valid[1], 4 * slot, -1))
    found = []
    for c in range(comps):
        near, far = [
            jnp.where(
                upper, padded[c, pl.ds(plane + start, 8), :], padded[c, pl.ds(plane + start + (tiles * rows - 4), 8), :]
            )
            for start in (here, there)
        ]
        found.append(pltpu.roll(jnp.where(left, near, far), shift, 1))
    return found, lax.shift_right_logical(lane, 2) == wanted


def flatten_pair(parts):
    row, _ = rows_and_lanes()
    first, second, third = [pltpu.roll(part, 0, 1, stride=4, stride_axis=0) for part in parts]
    low = jnp.where((row & 1) == 0, first + pltpu.roll(first, 7, 0), second + pltpu.roll(second, 1, 0))
    high = jnp.where((row & 1) == 0, third + pltpu.roll(third, 7, 0), 0.0)
    return jnp.where((row & 2) == 0, low + pltpu.roll(low, 6, 0), high + pltpu.roll(high, 2, 0))


def align_pair(tile):
    row, _ = rows_and_lanes()
    return jnp.where(row < 4, tile, pltpu.roll(tile, LANES - NODES, 1))


def edges_kernel(field, near, far, sems):
    length = field.shape[2]
    even = lax.axis_index("sub") % 2 == 0

    def edge_copies(near_row, far_row):
        return [
            pltpu.make_async_copy(field.at[:, :, pl.ds(row, 2), :], into, sems.at[n])
            for n, (row, into) in enumerate(((near_row, near), (far_row, far)))
        ]

    @pl.when(even)
    def _():
        for copy in edge_copies(length - 2, 0):
            copy.start()

    @pl.when(jnp.logical_not(even))
    def _():
        for copy in edge_copies(0, length - 2):
            copy.start()

    for copy in edge_copies(0, 0):
        copy.wait()


def load_kernel(field, base, padded, table, sems):
    depth, length, cells = field.shape[1:]
    copies = [pltpu.make_async_copy(base, table, sems.at[0])]
    for tile in range(cells // LANES):
        copies.append(
            pltpu.make_async_copy(
                field.at[:, :, :, pl.ds(tile * LANES, LANES)],
                padded.at[:, pl.ds(MARGIN, depth), tile, pl.ds(TOP, length), :],
                sems.at[1 + tile],
            )
        )
    for copy in copies:
        copy.start()
    for copy in copies:
        copy.wait()


def fill_halo(padded, shape, far, near, planes):
    comps, _, tiles, rows = shape
    even = lax.axis_index("sub") % 2 == 0
    below, above = TOP - 2, rows - TOP
    near_row, far_row = jnp.where(even, above, below), jnp.where(even, below, above)
    for c in range(comps):
        for x in planes:
            for tile in range(tiles):
                lanes = slice(tile * LANES, (tile + 1) * LANES)
                start = ((MARGIN + x) * tiles + tile) * rows
                padded[c, pl.ds(start + near_row, 2), :] = near[c, x, :, lanes]
                padded[c, pl.ds(start + far_row, 2), :] = far[c, x, :, lanes]


def boxes_kernel(table, live, far, near, padded_in, box_table, padded, acc, *, shape):
    comps, depth = shape[:2]
    fill_halo(padded, shape, far, near, range(2, depth - 2))
    acc[...] = jnp.zeros_like(acc)

    def one_group(group, _):
        parts = [[jnp.zeros((8, LANES), jnp.float32)] * comps for _ in range(2)]
        for slot in range(GROUP):
            b = group * GROUP + slot
            x = table[0, b]
            starts = first_rows(shape, table[1, b], table[2, b])
            valid = ((x >= 0, x >= -1), (x < depth - 2, x < depth - 3))
            for pair in range(2):
                found, mask = gather_pair(padded, shape, x + 2 * pair, valid[pair], starts, slot)
                parts[pair] = [jnp.where(mask, new, old) for new, old in zip(found, parts[pair])]
        for pair in range(2):
            for c in range(comps):
                acc[group, pair, c] = parts[pair][c]
        return 0

    lax.fori_loop(0, (live[0] + GROUP - 1) // GROUP, one_group, 0)
    for group in range(box_table.shape[0]):
        for pair in range(2):
            rows = flatten_pair([acc[group, pair, c] for c in range(comps)])
            box_table[group, 8 * pair : 8 * pair + 8, :] = align_pair(rows)


def hits_kernel(upper_base, lower_base, hits, *, depth):
    bins = upper_base.shape[1]
    row = lax.broadcasted_iota(jnp.int32, (8, bins), 0)
    lane = lax.broadcasted_iota(jnp.int32, (8, bins), 1)
    x, y, z = [jnp.where(row == 0, upper_base[d : d + 1, :], lower_base[d : d + 1, :]) for d in range(3)]
    wanted = ((row == 0) & (x < 0)) | ((row == 1) & (x > depth - 4))
    marks = jnp.where(wanted, 1.0, 0.0)
    earlier = lax.broadcasted_iota(jnp.int32, (bins, bins), 0) < lax.broadcasted_iota(jnp.int32, (bins, bins), 1)
    rank = jnp.dot(marks, jnp.where(earlier, 1.0, 0.0), preferred_element_type=jnp.float32)
    rank = jnp.where(row == 1, rank + jnp.sum(marks[0:1], axis=1, keepdims=True), rank)
    rank = jnp.where(wanted, rank, -1.0)
    places = ((row * bins + lane) * 64 + (x + 2)).astype(jnp.float32)
    cells = (z * 64 + (y + 2)).astype(jnp.float32)
    found = jnp.sum(marks).astype(jnp.int32)
    hits[4, 0] = found

    def list_hit(at, chosen):
        place = jnp.sum(jnp.where(chosen, places, 0.0)).astype(jnp.int32)
        cell = jnp.sum(jnp.where(chosen, cells, 0.0)).astype(jnp.int32)
        hits[0, at] = lax.shift_right_logical(place, 6)
        hits[1, at] = (place & 63) - 2
        hits[2, at] = (cell & 63) - 2
        hits[3, at] = lax.shift_right_logical(cell, 6)

    for at in range(ALWAYS):
        list_hit(at, rank == float(at))

    def some_hits(n, _):
        for k in range(UNROLL):
            at = ALWAYS + n * UNROLL + k
            list_hit(at, rank == at.astype(jnp.float32))
        return 0

    lax.fori_loop(0, (jnp.maximum(found - ALWAYS, 0) + UNROLL - 1) // UNROLL, some_hits, 0)


def answers_kernel(hits, padded_in, far, near, upper_out, lower_out, padded, acc, *, shape):
    comps, depth = shape[:2]
    groups = upper_out.shape[0]
    bins = groups * GROUP
    fill_halo(padded, shape, far, near, [0, 1, depth - 2, depth - 1])
    acc[...] = jnp.zeros_like(acc)
    found = hits[4, 0]

    def one_bin(at, place):
        entry, first_x, first_y, first_z = [hits[d, place] for d in range(4)]
        from_upper = entry < bins
        x = first_x + jnp.where(from_upper, depth, 2 - depth)
        valid = [(at < found) & (cell >= 0) & (cell < depth) for cell in (x, x + 1)]
        starts = first_rows(shape, first_y, first_z)
        gathered, mask = gather_pair(padded, shape, x, valid, starts, entry & (GROUP - 1))
        group = lax.shift_right_logical(entry, GROUP_BITS)
        for c in range(comps):
            acc[group, c] += jnp.where(mask, gathered[c], 0.0)

    def some_bins(n, _):
        for k in range(UNROLL):
            at = UNROLL + n * UNROLL + k
            one_bin(at, jnp.minimum(at, found - 1))
        return 0

    for at in range(UNROLL):
        one_bin(at, at)
    lax.fori_loop(0, (jnp.maximum(found - UNROLL, 0) + UNROLL - 1) // UNROLL, some_bins, 0)
    for g in range(groups):
        upper_out[g] = align_pair(flatten_pair([acc[g, c] for c in range(comps)]))
        lower_out[g] = align_pair(flatten_pair([acc[groups + g, c] for c in range(comps)]))


def unscaled_weights(t):
    plus, minus, minus_two = t + 1.0, t - 1.0, t - 2.0
    inner, outer = t * minus, plus * minus_two
    return inner * minus_two, outer * minus, outer * t, inner * plus


def node_factor(node):
    return jnp.where(node == 0, -1.0 / 6.0, jnp.where(node == 1, 0.5, jnp.where(node == 2, -0.5, 1.0 / 6.0)))


def split(x):
    head = x.astype(jnp.bfloat16)
    return head, (x - head.astype(jnp.float32)).astype(jnp.bfloat16)


def group_matrix(box):
    row = lax.broadcasted_iota(jnp.int32, box.shape, 0)
    lane = lax.broadcasted_iota(jnp.int32, box.shape, 1)
    box = box * (node_factor(row // 4) * node_factor(lane // 4 % 4) * node_factor(lane % 4))
    box = jnp.take_along_axis(box, lane % GROUP * NODES + lane // GROUP, axis=1)
    head = box.astype(jnp.bfloat16).astype(jnp.float32)
    own = lax.broadcasted_iota(jnp.int32, (GROUP, LANES), 1) % GROUP == lax.broadcasted_iota(
        jnp.int32, (GROUP, LANES), 0
    )

    def spread(part):
        rows = [
            jnp.where(own, jnp.broadcast_to(part[4 * i + c : 4 * i + c + 1], (GROUP, LANES)), 0.0)
            for i in range(4)
            for c in range(3)
        ]
        return jnp.concatenate(rows, axis=0).astype(jnp.bfloat16)

    heads, tails = spread(head), spread(box - head)
    return jnp.concatenate(
        [jnp.concatenate([heads, heads], axis=1), jnp.concatenate([tails, jnp.zeros_like(tails)], axis=1)], axis=0
    )


def sample(matrix, position):
    along_x, along_y, along_z = (unscaled_weights(t) for t in position)
    weights = jnp.concatenate([y * z for y in along_y for z in along_z], axis=0)
    head, tail = split(weights)
    planes = jnp.dot(matrix, jnp.concatenate([head, tail], axis=0), preferred_element_type=jnp.float32)
    half = planes.shape[0] // 2
    planes = planes[:half] + planes[half:]
    result = []
    for c in range(3):
        plane = [planes[8 * (3 * i + c) : 8 * (3 * i + c) + 8] for i in range(4)]
        result.append(
            (plane[0] * along_x[0] + plane[1] * along_x[1]) + (plane[2] * along_x[2] + plane[3] * along_x[3])
        )
    return result


def move_groups(groups, count, box_table, from_lower, from_upper, state, stokes, out):
    matrices, carry, rates, alive = [], [], [], []
    for g in range(groups):
        rows = slice(g * GROUP, (g + 1) * GROUP)
        answers = jnp.concatenate([from_lower[g], from_upper[g]], axis=0)
        matrices.append(group_matrix(box_table[g] + answers))
        rates.append(1.0 / stokes[rows, :])
        kept = g * GROUP + lax.broadcasted_iota(jnp.int32, rates[g].shape, 0) < count
        alive.append(kept)
        start = [jnp.where(kept, state[c, rows, :], 0.0) for c in range(6)]
        carry.append((start[:3], start[3:]))
    for _ in range(SUBSTEPS):
        moved = []
        for g in range(groups):
            position, velocity = carry[g]
            rate = rates[g]
            middle_pos = [x + 0.5 * STEP_SIZE * v for x, v in zip(position, velocity)]
            here = sample(matrices[g], position)
            there = sample(matrices[g], middle_pos)
            middle_vel = [v + 0.5 * STEP_SIZE * ((u - v) * rate) for u, v in zip(here, velocity)]
            moved.append(
                (
                    [x + STEP_SIZE * m for x, m in zip(position, middle_vel)],
                    [v + STEP_SIZE * (u - m) * rate for v, u, m in zip(velocity, there, middle_vel)],
                )
            )
        carry = moved
    for g in range(groups):
        rows = slice(g * GROUP, (g + 1) * GROUP)
        for c, value in enumerate([*carry[g][0], *carry[g][1]]):
            out[c, rows, :] = jnp.where(alive[g], value, state[c, rows, :])
    if groups < box_table.shape[0]:
        out[:, groups * GROUP :, :] = state[:, groups * GROUP :, :]


def move_kernel(live, box_table, from_lower, from_upper, state, stokes, out):
    count = live[0]
    groups = box_table.shape[0]
    fewer = 0
    for some in sorted({1, max(1, groups // 2), groups}):

        @pl.when((count > fewer * GROUP) & (count <= some * GROUP))
        def _(some=some):
            move_groups(some, count, box_table, from_lower, from_upper, state, stokes, out)

        fewer = some


def in_smem():
    return pl.BlockSpec(memory_space=pltpu.SMEM)


def in_vmem():
    return pl.BlockSpec(memory_space=pltpu.VMEM)


def exchange(near, far, axis):
    devices = lax.axis_size(axis)
    near_pairs = [(i, i ^ 1) for i in range(devices)]
    far_pairs = [(i, (i + 1 if i % 2 else i - 1) % devices) for i in range(devices)]
    far = lax.ppermute(far, axis, far_pairs)
    return lax.ppermute(near, axis, near_pairs), far


def shift(array, axis, step):
    devices = lax.axis_size(axis)
    return lax.ppermute(array, axis, [(i, (i + step) % devices) for i in range(devices)])


def body(velocity_field, particle_state, stokes_time, box_base, live_bins):
    comps, depth, length, cells = velocity_field.shape
    bins = box_base.shape[0]
    tiles = cells // LANES
    groups = bins // GROUP
    table = box_base.T
    state = particle_state.transpose(1, 0, 2)
    block = pltpu.with_memory_space_constraint(velocity_field, pltpu.HBM)
    params = pltpu.CompilerParams(vmem_limit_bytes=VMEM_LIMIT)

    lower_table, upper_table = shift(table, "slab", 1), shift(table, "slab", -1)
    shape = (comps, depth, tiles, length + 2 * TOP)
    planes = depth + 2 * MARGIN
    rows_of_block = pltpu.VMEM((comps, planes * tiles * (length + 2 * TOP), LANES), jnp.float32)
    edge_rows = jax.ShapeDtypeStruct((comps, depth, 2, cells), jnp.float32)
    near, far = pl.pallas_call(
        edges_kernel,
        out_shape=(edge_rows, edge_rows),
        in_specs=[pl.BlockSpec(memory_space=pl.ANY)],
        out_specs=(in_vmem(), in_vmem()),
        scratch_shapes=[pltpu.SemaphoreType.DMA((2,))],
        compiler_params=params,
        name="edges",
    )(block)
    near, far = exchange(near, far, "sub")

    smem_table = pltpu.SMEM(table.shape, jnp.int32)
    padded, own_table = pl.pallas_call(
        load_kernel,
        out_shape=(pltpu.VMEM((comps, planes, tiles, length + 2 * TOP, LANES), jnp.float32), smem_table),
        in_specs=[pl.BlockSpec(memory_space=pl.ANY)] * 2,
        out_specs=(in_vmem(), in_smem()),
        scratch_shapes=[pltpu.SemaphoreType.DMA((1 + tiles,))],
        compiler_params=params,
        cost_estimate=pl.CostEstimate(flops=1_000_000, bytes_accessed=6_000_000, transcendentals=0),
        name="load",
    )(block, pltpu.with_memory_space_constraint(table, pltpu.HBM))

    padded = padded.reshape(rows_of_block.shape)
    hits = pl.pallas_call(
        functools.partial(hits_kernel, depth=depth),
        out_shape=pltpu.SMEM((5, 2 * bins), jnp.int32),
        in_specs=[in_vmem(), in_vmem()],
        out_specs=in_smem(),
        compiler_params=params,
        name="hits",
    )(upper_table, lower_table)
    answer = jax.ShapeDtypeStruct((groups, 8, LANES), jnp.float32)
    for_upper, for_lower, padded = pl.pallas_call(
        functools.partial(answers_kernel, shape=shape),
        out_shape=(answer, answer, rows_of_block),
        in_specs=[in_smem(), in_vmem(), in_vmem(), in_vmem()],
        out_specs=(in_vmem(), in_vmem(), in_vmem()),
        scratch_shapes=[pltpu.VMEM((2 * groups, comps, 8, LANES), jnp.float32)],
        input_output_aliases={1: 2},
        compiler_params=params,
        name="answers",
    )(hits, padded, far, near)
    from_lower, from_upper = shift(for_upper, "slab", 1), shift(for_lower, "slab", -1)

    box_table, _ = pl.pallas_call(
        functools.partial(boxes_kernel, shape=shape),
        out_shape=(jax.ShapeDtypeStruct((groups, NODES, LANES), jnp.float32), rows_of_block),
        in_specs=[in_smem(), in_smem(), in_vmem(), in_vmem(), in_vmem()],
        out_specs=(in_vmem(), in_vmem()),
        scratch_shapes=[pltpu.VMEM((groups, 2, comps, 8, LANES), jnp.float32)],
        input_output_aliases={4: 1},
        compiler_params=params,
        cost_estimate=pl.CostEstimate(flops=1_000_000, bytes_accessed=4_000_000, transcendentals=0),
        name="boxes",
    )(own_table, live_bins, far, near, padded)

    moved = pl.pallas_call(
        move_kernel,
        out_shape=jax.ShapeDtypeStruct(state.shape, jnp.float32),
        in_specs=[in_smem()] + [in_vmem()] * 5,
        out_specs=in_vmem(),
        compiler_params=params,
        name="move",
    )(live_bins, box_table, from_lower, from_upper, state, stokes_time)
    return moved.transpose(1, 0, 2)


def solution(mesh):
    placed = (
        P(None, "slab", "sub", None),
        P(("slab", "sub"), None, None),
        P(("slab", "sub"), None),
        P(("slab", "sub"), None),
        P(("slab", "sub")),
    )
    return jax.shard_map(
        body, mesh=mesh, in_specs=placed, out_specs=P(("slab", "sub"), None, None), check_vma=False
    )
```

```python
import functools

import jax
import jax.numpy as jnp
from jax import lax
from jax.experimental import pallas as pl
from jax.experimental.pallas import tpu as pltpu
from jax.sharding import PartitionSpec as P

SUBSTEPS = 4
STEP_SIZE = 0.2
LANES = 128
LANE_BITS = 7
NODES = 16
GROUP = 8
GROUP_BITS = 3
MARGIN = 2
TOP = 8
UNROLL = 8
ALWAYS = 16
VMEM_LIMIT = 32 * 1024 * 1024


def rows_and_lanes():
    return lax.broadcasted_iota(jnp.int32, (8, LANES), 0), lax.broadcasted_iota(jnp.int32, (8, LANES), 1)


def first_rows(shape, first_y, first_z):
    _, _, tiles, rows = shape
    tile = lax.shift_right_logical(first_z, LANE_BITS)
    beside = jnp.where(tile == tiles - 1, 0, tile + 1)
    start = MARGIN * tiles * rows + TOP + first_y
    return start + tile * rows, start + beside * rows, first_z & (LANES - 1)


def gather_pair(padded, shape, x, valid, starts, slot):
    comps, _, tiles, rows = shape
    row, lane = rows_and_lanes()
    here, there, offset = starts
    upper, left = row < 4, lane >= offset
    plane = x * (tiles * rows)
    shift = (NODES * slot - offset) & (LANES - 1)
    wanted = jnp.where(upper, jnp.where(valid[0], 4 * slot, -1), jnp.where(valid[1], 4 * slot, -1))
    found = []
    for c in range(comps):
        near, far = [
            jnp.where(
                upper, padded[c, pl.ds(plane + start, 8), :], padded[c, pl.ds(plane + start + (tiles * rows - 4), 8), :]
            )
            for start in (here, there)
        ]
        found.append(pltpu.roll(jnp.where(left, near, far), shift, 1))
    return found, lax.shift_right_logical(lane, 2) == wanted


def flatten_pair(parts):
    row, _ = rows_and_lanes()
    first, second, third = [pltpu.roll(part, 0, 1, stride=4, stride_axis=0) for part in parts]
    low = jnp.where((row & 1) == 0, first + pltpu.roll(first, 7, 0), second + pltpu.roll(second, 1, 0))
    high = jnp.where((row & 1) == 0, third + pltpu.roll(third, 7, 0), 0.0)
    return jnp.where((row & 2) == 0, low + pltpu.roll(low, 6, 0), high + pltpu.roll(high, 2, 0))


def align_pair(tile):
    row, _ = rows_and_lanes()
    return jnp.where(row < 4, tile, pltpu.roll(tile, LANES - NODES, 1))


def edges_kernel(field, near, far, sems):
    length = field.shape[2]
    even = lax.axis_index("sub") % 2 == 0

    def edge_copies(near_row, far_row):
        return [
            pltpu.make_async_copy(field.at[:, :, pl.ds(row, 2), :], into, sems.at[n])
            for n, (row, into) in enumerate(((near_row, near), (far_row, far)))
        ]

    @pl.when(even)
    def _():
        for copy in edge_copies(length - 2, 0):
            copy.start()

    @pl.when(jnp.logical_not(even))
    def _():
        for copy in edge_copies(0, length - 2):
            copy.start()

    for copy in edge_copies(0, 0):
        copy.wait()


def load_kernel(field, base, padded, table, sems):
    depth, length, cells = field.shape[1:]
    copies = [pltpu.make_async_copy(base, table, sems.at[0])]
    for tile in range(cells // LANES):
        copies.append(
            pltpu.make_async_copy(
                field.at[:, :, :, pl.ds(tile * LANES, LANES)],
                padded.at[:, pl.ds(MARGIN, depth), tile, pl.ds(TOP, length), :],
                sems.at[1 + tile],
            )
        )
    for copy in copies:
        copy.start()
    for copy in copies:
        copy.wait()


def fill_halo(padded, shape, far, near, planes):
    comps, _, tiles, rows = shape
    even = lax.axis_index("sub") % 2 == 0
    below, above = TOP - 2, rows - TOP
    near_row, far_row = jnp.where(even, above, below), jnp.where(even, below, above)
    for c in range(comps):
        for x in planes:
            for tile in range(tiles):
                lanes = slice(tile * LANES, (tile + 1) * LANES)
                start = ((MARGIN + x) * tiles + tile) * rows
                padded[c, pl.ds(start + near_row, 2), :] = near[c, x, :, lanes]
                padded[c, pl.ds(start + far_row, 2), :] = far[c, x, :, lanes]


def boxes_kernel(table, live, far, near, padded_in, box_table, padded, acc, *, shape):
    comps, depth = shape[:2]
    fill_halo(padded, shape, far, near, range(2, depth - 2))
    acc[...] = jnp.zeros_like(acc)

    def one_group(group, _):
        parts = [[jnp.zeros((8, LANES), jnp.float32)] * comps for _ in range(2)]
        for slot in range(GROUP):
            b = group * GROUP + slot
            x = table[0, b]
            starts = first_rows(shape, table[1, b], table[2, b])
            valid = ((x >= 0, x >= -1), (x < depth - 2, x < depth - 3))
            for pair in range(2):
                found, mask = gather_pair(padded, shape, x + 2 * pair, valid[pair], starts, slot)
                parts[pair] = [jnp.where(mask, new, old) for new, old in zip(found, parts[pair])]
        for pair in range(2):
            for c in range(comps):
                acc[group, pair, c] = parts[pair][c]
        return 0

    lax.fori_loop(0, (live[0] + GROUP - 1) // GROUP, one_group, 0)
    for group in range(box_table.shape[0]):
        for pair in range(2):
            rows = flatten_pair([acc[group, pair, c] for c in range(comps)])
            box_table[group, 8 * pair : 8 * pair + 8, :] = align_pair(rows)


def hits_kernel(upper_base, lower_base, hits, *, depth):
    bins = upper_base.shape[1]
    row = lax.broadcasted_iota(jnp.int32, (8, bins), 0)
    lane = lax.broadcasted_iota(jnp.int32, (8, bins), 1)
    x, y, z = [jnp.where(row == 0, upper_base[d : d + 1, :], lower_base[d : d + 1, :]) for d in range(3)]
    wanted = ((row == 0) & (x < 0)) | ((row == 1) & (x > depth - 4))
    marks = jnp.where(wanted, 1.0, 0.0)
    earlier = lax.broadcasted_iota(jnp.int32, (bins, bins), 0) < lax.broadcasted_iota(jnp.int32, (bins, bins), 1)
    rank = jnp.dot(marks, jnp.where(earlier, 1.0, 0.0), preferred_element_type=jnp.float32)
    rank = jnp.where(row == 1, rank + jnp.sum(marks[0:1], axis=1, keepdims=True), rank)
    rank = jnp.where(wanted, rank, -1.0)
    places = ((row * bins + lane) * 64 + (x + 2)).astype(jnp.float32)
    cells = (z * 64 + (y + 2)).astype(jnp.float32)
    found = jnp.sum(marks).astype(jnp.int32)
    hits[4, 0] = found

    def list_hit(at, chosen):
        place = jnp.sum(jnp.where(chosen, places, 0.0)).astype(jnp.int32)
        cell = jnp.sum(jnp.where(chosen, cells, 0.0)).astype(jnp.int32)
        hits[0, at] = lax.shift_right_logical(place, 6)
        hits[1, at] = (place & 63) - 2
        hits[2, at] = (cell & 63) - 2
        hits[3, at] = lax.shift_right_logical(cell, 6)

    for at in range(ALWAYS):
        list_hit(at, rank == float(at))

    def some_hits(n, _):
        for k in range(UNROLL):
            at = ALWAYS + n * UNROLL + k
            list_hit(at, rank == at.astype(jnp.float32))
        return 0

    lax.fori_loop(0, (jnp.maximum(found - ALWAYS, 0) + UNROLL - 1) // UNROLL, some_hits, 0)


def answers_kernel(hits, padded_in, far, near, upper_out, lower_out, padded, acc, *, shape):
    comps, depth = shape[:2]
    groups = upper_out.shape[0]
    bins = groups * GROUP
    fill_halo(padded, shape, far, near, [0, 1, depth - 2, depth - 1])
    acc[...] = jnp.zeros_like(acc)
    found = hits[4, 0]

    def one_bin(at, place):
        entry, first_x, first_y, first_z = [hits[d, place] for d in range(4)]
        from_upper = entry < bins
        x = first_x + jnp.where(from_upper, depth, 2 - depth)
        valid = [(at < found) & (cell >= 0) & (cell < depth) for cell in (x, x + 1)]
        starts = first_rows(shape, first_y, first_z)
        gathered, mask = gather_pair(padded, shape, x, valid, starts, entry & (GROUP - 1))
        group = lax.shift_right_logical(entry, GROUP_BITS)
        for c in range(comps):
            acc[group, c] += jnp.where(mask, gathered[c], 0.0)

    def some_bins(n, _):
        for k in range(UNROLL):
            at = UNROLL + n * UNROLL + k
            one_bin(at, jnp.minimum(at, found - 1))
        return 0

    for at in range(UNROLL):
        one_bin(at, at)
    lax.fori_loop(0, (jnp.maximum(found - UNROLL, 0) + UNROLL - 1) // UNROLL, some_bins, 0)
    for g in range(groups):
        upper_out[g] = align_pair(flatten_pair([acc[g, c] for c in range(comps)]))
        lower_out[g] = align_pair(flatten_pair([acc[groups + g, c] for c in range(comps)]))


def unscaled_weights(t):
    plus, minus, minus_two = t + 1.0, t - 1.0, t - 2.0
    inner, outer = t * minus, plus * minus_two
    return inner * minus_two, outer * minus, outer * t, inner * plus


def node_factor(node):
    return jnp.where(node == 0, -1.0 / 6.0, jnp.where(node == 1, 0.5, jnp.where(node == 2, -0.5, 1.0 / 6.0)))


def split(x):
    head = x.astype(jnp.bfloat16)
    return head, (x - head.astype(jnp.float32)).astype(jnp.bfloat16)


def group_matrix(box):
    row = lax.broadcasted_iota(jnp.int32, box.shape, 0)
    lane = lax.broadcasted_iota(jnp.int32, box.shape, 1)
    box = box * (node_factor(row // 4) * node_factor(lane // 4 % 4) * node_factor(lane % 4))
    box = jnp.take_along_axis(box, lane % GROUP * NODES + lane // GROUP, axis=1)
    head = box.astype(jnp.bfloat16).astype(jnp.float32)
    own = lax.broadcasted_iota(jnp.int32, (GROUP, LANES), 1) % GROUP == lax.broadcasted_iota(
        jnp.int32, (GROUP, LANES), 0
    )

    def spread(part):
        rows = [
            jnp.where(own, jnp.broadcast_to(part[4 * i + c : 4 * i + c + 1], (GROUP, LANES)), 0.0)
            for i in range(4)
            for c in range(3)
        ]
        return jnp.concatenate(rows, axis=0).astype(jnp.bfloat16)

    heads, tails = spread(head), spread(box - head)
    return jnp.concatenate(
        [jnp.concatenate([heads, heads], axis=1), jnp.concatenate([tails, jnp.zeros_like(tails)], axis=1)], axis=0
    )


def sample(matrix, position):
    along_x, along_y, along_z = (unscaled_weights(t) for t in position)
    weights = jnp.concatenate([y * z for y in along_y for z in along_z], axis=0)
    head, tail = split(weights)
    planes = jnp.dot(matrix, jnp.concatenate([head, tail], axis=0), preferred_element_type=jnp.float32)
    half = planes.shape[0] // 2
    planes = planes[:half] + planes[half:]
    result = []
    for c in range(3):
        plane = [planes[8 * (3 * i + c) : 8 * (3 * i + c) + 8] for i in range(4)]
        result.append(
            (plane[0] * along_x[0] + plane[1] * along_x[1]) + (plane[2] * along_x[2] + plane[3] * along_x[3])
        )
    return result


def move_groups(groups, count, box_table, from_lower, from_upper, state, stokes, out):
    matrices, carry, rates, alive = [], [], [], []
    for g in range(groups):
        rows = slice(g * GROUP, (g + 1) * GROUP)
        answers = jnp.concatenate([from_lower[g], from_upper[g]], axis=0)
        matrices.append(group_matrix(box_table[g] + answers))
        rates.append(1.0 / stokes[rows, :])
        kept = g * GROUP + lax.broadcasted_iota(jnp.int32, rates[g].shape, 0) < count
        alive.append(kept)
        start = [jnp.where(kept, state[c, rows, :], 0.0) for c in range(6)]
        carry.append((start[:3], start[3:]))
    for _ in range(SUBSTEPS):
        moved = []
        for g in range(groups):
            position, velocity = carry[g]
            rate = rates[g]
            middle_pos = [x + 0.5 * STEP_SIZE * v for x, v in zip(position, velocity)]
            here = sample(matrices[g], position)
            there = sample(matrices[g], middle_pos)
            middle_vel = [v + 0.5 * STEP_SIZE * ((u - v) * rate) for u, v in zip(here, velocity)]
            moved.append(
                (
                    [x + STEP_SIZE * m for x, m in zip(position, middle_vel)],
                    [v + STEP_SIZE * (u - m) * rate for v, u, m in zip(velocity, there, middle_vel)],
                )
            )
        carry = moved
    for g in range(groups):
        rows = slice(g * GROUP, (g + 1) * GROUP)
        for c, value in enumerate([*carry[g][0], *carry[g][1]]):
            out[c, rows, :] = jnp.where(alive[g], value, state[c, rows, :])
    if groups < box_table.shape[0]:
        out[:, groups * GROUP :, :] = state[:, groups * GROUP :, :]


def move_kernel(live, box_table, from_lower, from_upper, state, stokes, out):
    count = live[0]
    groups = box_table.shape[0]
    fewer = 0
    for some in range(1, groups + 1):

        @pl.when((count > fewer * GROUP) & (count <= some * GROUP))
        def _(some=some):
            move_groups(some, count, box_table, from_lower, from_upper, state, stokes, out)

        fewer = some


def in_smem():
    return pl.BlockSpec(memory_space=pltpu.SMEM)


def in_vmem():
    return pl.BlockSpec(memory_space=pltpu.VMEM)


def exchange(near, far, axis):
    devices = lax.axis_size(axis)
    near_pairs = [(i, i ^ 1) for i in range(devices)]
    far_pairs = [(i, (i + 1 if i % 2 else i - 1) % devices) for i in range(devices)]
    far = lax.ppermute(far, axis, far_pairs)
    return lax.ppermute(near, axis, near_pairs), far


def shift(array, axis, step):
    devices = lax.axis_size(axis)
    return lax.ppermute(array, axis, [(i, (i + step) % devices) for i in range(devices)])


def body(velocity_field, particle_state, stokes_time, box_base, live_bins):
    comps, depth, length, cells = velocity_field.shape
    bins = box_base.shape[0]
    tiles = cells // LANES
    groups = bins // GROUP
    table = box_base.T
    state = particle_state.transpose(1, 0, 2)
    block = pltpu.with_memory_space_constraint(velocity_field, pltpu.HBM)
    params = pltpu.CompilerParams(vmem_limit_bytes=VMEM_LIMIT)

    lower_table, upper_table = shift(table, "slab", 1), shift(table, "slab", -1)
    shape = (comps, depth, tiles, length + 2 * TOP)
    planes = depth + 2 * MARGIN
    rows_of_block = pltpu.VMEM((comps, planes * tiles * (length + 2 * TOP), LANES), jnp.float32)
    edge_rows = jax.ShapeDtypeStruct((comps, depth, 2, cells), jnp.float32)
    near, far = pl.pallas_call(
        edges_kernel,
        out_shape=(edge_rows, edge_rows),
        in_specs=[pl.BlockSpec(memory_space=pl.ANY)],
        out_specs=(in_vmem(), in_vmem()),
        scratch_shapes=[pltpu.SemaphoreType.DMA((2,))],
        compiler_params=params,
        name="edges",
    )(block)
    near, far = exchange(near, far, "sub")

    smem_table = pltpu.SMEM(table.shape, jnp.int32)
    padded, own_table = pl.pallas_call(
        load_kernel,
        out_shape=(pltpu.VMEM((comps, planes, tiles, length + 2 * TOP, LANES), jnp.float32), smem_table),
        in_specs=[pl.BlockSpec(memory_space=pl.ANY)] * 2,
        out_specs=(in_vmem(), in_smem()),
        scratch_shapes=[pltpu.SemaphoreType.DMA((1 + tiles,))],
        compiler_params=params,
        cost_estimate=pl.CostEstimate(flops=1_000_000, bytes_accessed=6_000_000, transcendentals=0),
        name="load",
    )(block, pltpu.with_memory_space_constraint(table, pltpu.HBM))

    padded = padded.reshape(rows_of_block.shape)
    hits = pl.pallas_call(
        functools.partial(hits_kernel, depth=depth),
        out_shape=pltpu.SMEM((5, 2 * bins), jnp.int32),
        in_specs=[in_vmem(), in_vmem()],
        out_specs=in_smem(),
        compiler_params=params,
        name="hits",
    )(upper_table, lower_table)
    answer = jax.ShapeDtypeStruct((groups, 8, LANES), jnp.float32)
    for_upper, for_lower, padded = pl.pallas_call(
        functools.partial(answers_kernel, shape=shape),
        out_shape=(answer, answer, rows_of_block),
        in_specs=[in_smem(), in_vmem(), in_vmem(), in_vmem()],
        out_specs=(in_vmem(), in_vmem(), in_vmem()),
        scratch_shapes=[pltpu.VMEM((2 * groups, comps, 8, LANES), jnp.float32)],
        input_output_aliases={1: 2},
        compiler_params=params,
        name="answers",
    )(hits, padded, far, near)
    from_lower, from_upper = shift(for_upper, "slab", 1), shift(for_lower, "slab", -1)

    box_table, _ = pl.pallas_call(
        functools.partial(boxes_kernel, shape=shape),
        out_shape=(jax.ShapeDtypeStruct((groups, NODES, LANES), jnp.float32), rows_of_block),
        in_specs=[in_smem(), in_smem(), in_vmem(), in_vmem(), in_vmem()],
        out_specs=(in_vmem(), in_vmem()),
        scratch_shapes=[pltpu.VMEM((groups, 2, comps, 8, LANES), jnp.float32)],
        input_output_aliases={4: 1},
        compiler_params=params,
        cost_estimate=pl.CostEstimate(flops=1_000_000, bytes_accessed=4_000_000, transcendentals=0),
        name="boxes",
    )(own_table, live_bins, far, near, padded)

    moved = pl.pallas_call(
        move_kernel,
        out_shape=jax.ShapeDtypeStruct(state.shape, jnp.float32),
        in_specs=[in_smem()] + [in_vmem()] * 5,
        out_specs=in_vmem(),
        compiler_params=params,
        name="move",
    )(live_bins, box_table, from_lower, from_upper, state, stokes_time)
    return moved.transpose(1, 0, 2)


def solution(mesh):
    placed = (
        P(None, "slab", "sub", None),
        P(("slab", "sub"), None, None),
        P(("slab", "sub"), None),
        P(("slab", "sub"), None),
        P(("slab", "sub")),
    )
    return jax.shard_map(
        body, mesh=mesh, in_specs=placed, out_specs=P(("slab", "sub"), None, None), check_vma=False
    )
```

```python
import functools

import jax
import jax.numpy as jnp
from jax import lax
from jax.experimental import pallas as pl
from jax.experimental.pallas import tpu as pltpu
from jax.sharding import PartitionSpec as P

SUBSTEPS = 4
STEP_SIZE = 0.2
LANES = 128
LANE_BITS = 7
NODES = 16
GROUP = 8
GROUP_BITS = 3
MARGIN = 2
TOP = 8
UNROLL = 8
ALWAYS = 16
VMEM_LIMIT = 32 * 1024 * 1024


def rows_and_lanes():
    return lax.broadcasted_iota(jnp.int32, (8, LANES), 0), lax.broadcasted_iota(jnp.int32, (8, LANES), 1)


def first_rows(shape, first_y, first_z):
    _, _, tiles, rows = shape
    tile = lax.shift_right_logical(first_z, LANE_BITS)
    beside = jnp.where(tile == tiles - 1, 0, tile + 1)
    start = MARGIN * tiles * rows + TOP + first_y
    return start + tile * rows, start + beside * rows, first_z & (LANES - 1)


def gather_pair(padded, shape, x, valid, starts, slot):
    comps, _, tiles, rows = shape
    row, lane = rows_and_lanes()
    here, there, offset = starts
    upper, left = row < 4, lane >= offset
    plane = x * (tiles * rows)
    shift = (NODES * slot - offset) & (LANES - 1)
    wanted = jnp.where(upper, jnp.where(valid[0], 4 * slot, -1), jnp.where(valid[1], 4 * slot, -1))
    found = []
    for c in range(comps):
        near, far = [
            jnp.where(
                upper, padded[c, pl.ds(plane + start, 8), :], padded[c, pl.ds(plane + start + (tiles * rows - 4), 8), :]
            )
            for start in (here, there)
        ]
        found.append(pltpu.roll(jnp.where(left, near, far), shift, 1))
    return found, lax.shift_right_logical(lane, 2) == wanted


def flatten_pair(parts):
    row, _ = rows_and_lanes()
    first, second, third = [pltpu.roll(part, 0, 1, stride=4, stride_axis=0) for part in parts]
    low = jnp.where((row & 1) == 0, first + pltpu.roll(first, 7, 0), second + pltpu.roll(second, 1, 0))
    high = jnp.where((row & 1) == 0, third + pltpu.roll(third, 7, 0), 0.0)
    return jnp.where((row & 2) == 0, low + pltpu.roll(low, 6, 0), high + pltpu.roll(high, 2, 0))


def align_pair(tile):
    row, _ = rows_and_lanes()
    return jnp.where(row < 4, tile, pltpu.roll(tile, LANES - NODES, 1))


def edges_kernel(field, near, far, sems):
    length = field.shape[2]
    even = lax.axis_index("sub") % 2 == 0

    def edge_copies(near_row, far_row):
        return [
            pltpu.make_async_copy(field.at[:, :, pl.ds(row, 2), :], into, sems.at[n])
            for n, (row, into) in enumerate(((near_row, near), (far_row, far)))
        ]

    @pl.when(even)
    def _():
        for copy in edge_copies(length - 2, 0):
            copy.start()

    @pl.when(jnp.logical_not(even))
    def _():
        for copy in edge_copies(0, length - 2):
            copy.start()

    for copy in edge_copies(0, 0):
        copy.wait()


def load_kernel(field, base, padded, table, sems):
    depth, length, cells = field.shape[1:]
    copies = [pltpu.make_async_copy(base, table, sems.at[0])]
    for tile in range(cells // LANES):
        copies.append(
            pltpu.make_async_copy(
                field.at[:, :, :, pl.ds(tile * LANES, LANES)],
                padded.at[:, pl.ds(MARGIN, depth), tile, pl.ds(TOP, length), :],
                sems.at[1 + tile],
            )
        )
    for copy in copies:
        copy.start()
    for copy in copies:
        copy.wait()


def fill_halo(padded, shape, far, near, planes):
    comps, _, tiles, rows = shape
    even = lax.axis_index("sub") % 2 == 0
    below, above = TOP - 2, rows - TOP
    near_row, far_row = jnp.where(even, above, below), jnp.where(even, below, above)
    for c in range(comps):
        for x in planes:
            for tile in range(tiles):
                lanes = slice(tile * LANES, (tile + 1) * LANES)
                start = ((MARGIN + x) * tiles + tile) * rows
                padded[c, pl.ds(start + near_row, 2), :] = near[c, x, :, lanes]
                padded[c, pl.ds(start + far_row, 2), :] = far[c, x, :, lanes]


def boxes_kernel(table, live, far, near, padded_in, box_table, padded, acc, *, shape):
    comps, depth = shape[:2]
    fill_halo(padded, shape, far, near, range(2, depth - 2))
    acc[...] = jnp.zeros_like(acc)

    def one_group(group, _):
        parts = [[jnp.zeros((8, LANES), jnp.float32)] * comps for _ in range(2)]
        for slot in range(GROUP):
            b = group * GROUP + slot
            x = table[0, b]
            starts = first_rows(shape, table[1, b], table[2, b])
            valid = ((x >= 0, x >= -1), (x < depth - 2, x < depth - 3))
            for pair in range(2):
                found, mask = gather_pair(padded, shape, x + 2 * pair, valid[pair], starts, slot)
                parts[pair] = [jnp.where(mask, new, old) for new, old in zip(found, parts[pair])]
        for pair in range(2):
            for c in range(comps):
                acc[group, pair, c] = parts[pair][c]
        return 0

    lax.fori_loop(0, (live[0] + GROUP - 1) // GROUP, one_group, 0)
    for group in range(box_table.shape[0]):
        for pair in range(2):
            rows = flatten_pair([acc[group, pair, c] for c in range(comps)])
            box_table[group, 8 * pair : 8 * pair + 8, :] = align_pair(rows)


def hits_kernel(upper_base, lower_base, hits, *, depth):
    bins = upper_base.shape[1]
    row = lax.broadcasted_iota(jnp.int32, (8, bins), 0)
    lane = lax.broadcasted_iota(jnp.int32, (8, bins), 1)
    x, y, z = [jnp.where(row == 0, upper_base[d : d + 1, :], lower_base[d : d + 1, :]) for d in range(3)]
    wanted = ((row == 0) & (x < 0)) | ((row == 1) & (x > depth - 4))
    marks = jnp.where(wanted, 1.0, 0.0)
    earlier = lax.broadcasted_iota(jnp.int32, (bins, bins), 0) < lax.broadcasted_iota(jnp.int32, (bins, bins), 1)
    rank = jnp.dot(marks, jnp.where(earlier, 1.0, 0.0), preferred_element_type=jnp.float32)
    rank = jnp.where(row == 1, rank + jnp.sum(marks[0:1], axis=1, keepdims=True), rank)
    rank = jnp.where(wanted, rank, -1.0)
    places = ((row * bins + lane) * 64 + (x + 2)).astype(jnp.float32)
    cells = (z * 64 + (y + 2)).astype(jnp.float32)
    found = jnp.sum(marks).astype(jnp.int32)
    hits[4, 0] = found

    def list_hit(at, chosen):
        place = jnp.sum(jnp.where(chosen, places, 0.0)).astype(jnp.int32)
        cell = jnp.sum(jnp.where(chosen, cells, 0.0)).astype(jnp.int32)
        hits[0, at] = lax.shift_right_logical(place, 6)
        hits[1, at] = (place & 63) - 2
        hits[2, at] = (cell & 63) - 2
        hits[3, at] = lax.shift_right_logical(cell, 6)

    for at in range(ALWAYS):
        list_hit(at, rank == float(at))

    def some_hits(n, _):
        for k in range(UNROLL):
            at = ALWAYS + n * UNROLL + k
            list_hit(at, rank == at.astype(jnp.float32))
        return 0

    lax.fori_loop(0, (jnp.maximum(found - ALWAYS, 0) + UNROLL - 1) // UNROLL, some_hits, 0)


def answers_kernel(hits, padded_in, far, near, upper_out, lower_out, padded, acc, *, shape):
    comps, depth = shape[:2]
    groups = upper_out.shape[0]
    bins = groups * GROUP
    fill_halo(padded, shape, far, near, [0, 1, depth - 2, depth - 1])
    acc[...] = jnp.zeros_like(acc)
    found = hits[4, 0]

    def one_bin(at, place):
        entry, first_x, first_y, first_z = [hits[d, place] for d in range(4)]
        from_upper = entry < bins
        x = first_x + jnp.where(from_upper, depth, 2 - depth)
        valid = [(at < found) & (cell >= 0) & (cell < depth) for cell in (x, x + 1)]
        starts = first_rows(shape, first_y, first_z)
        gathered, mask = gather_pair(padded, shape, x, valid, starts, entry & (GROUP - 1))
        group = lax.shift_right_logical(entry, GROUP_BITS)
        for c in range(comps):
            acc[group, c] += jnp.where(mask, gathered[c], 0.0)

    def some_bins(n, _):
        for k in range(UNROLL // 2):
            at = UNROLL + n * (UNROLL // 2) + k
            one_bin(at, jnp.minimum(at, found - 1))
        return 0

    for at in range(UNROLL):
        one_bin(at, at)
    lax.fori_loop(0, (jnp.maximum(found - UNROLL, 0) + UNROLL // 2 - 1) // (UNROLL // 2), some_bins, 0)
    for g in range(groups):
        upper_out[g] = align_pair(flatten_pair([acc[g, c] for c in range(comps)]))
        lower_out[g] = align_pair(flatten_pair([acc[groups + g, c] for c in range(comps)]))


def unscaled_weights(t):
    plus, minus, minus_two = t + 1.0, t - 1.0, t - 2.0
    inner, outer = t * minus, plus * minus_two
    return inner * minus_two, outer * minus, outer * t, inner * plus


def node_factor(node):
    return jnp.where(node == 0, -1.0 / 6.0, jnp.where(node == 1, 0.5, jnp.where(node == 2, -0.5, 1.0 / 6.0)))


def split(x):
    head = x.astype(jnp.bfloat16)
    return head, (x - head.astype(jnp.float32)).astype(jnp.bfloat16)


def group_matrix(box):
    row = lax.broadcasted_iota(jnp.int32, box.shape, 0)
    lane = lax.broadcasted_iota(jnp.int32, box.shape, 1)
    box = box * (node_factor(row // 4) * node_factor(lane // 4 % 4) * node_factor(lane % 4))
    box = jnp.take_along_axis(box, lane % GROUP * NODES + lane // GROUP, axis=1)
    head = box.astype(jnp.bfloat16).astype(jnp.float32)
    own = lax.broadcasted_iota(jnp.int32, (GROUP, LANES), 1) % GROUP == lax.broadcasted_iota(
        jnp.int32, (GROUP, LANES), 0
    )

    def spread(part):
        rows = [
            jnp.where(own, jnp.broadcast_to(part[4 * i + c : 4 * i + c + 1], (GROUP, LANES)), 0.0)
            for i in range(4)
            for c in range(3)
        ]
        return jnp.concatenate(rows, axis=0).astype(jnp.bfloat16)

    heads, tails = spread(head), spread(box - head)
    return jnp.concatenate(
        [jnp.concatenate([heads, heads], axis=1), jnp.concatenate([tails, jnp.zeros_like(tails)], axis=1)], axis=0
    )


def sample(matrix, position):
    along_x, along_y, along_z = (unscaled_weights(t) for t in position)
    weights = jnp.concatenate([y * z for y in along_y for z in along_z], axis=0)
    head, tail = split(weights)
    planes = jnp.dot(matrix, jnp.concatenate([head, tail], axis=0), preferred_element_type=jnp.float32)
    half = planes.shape[0] // 2
    planes = planes[:half] + planes[half:]
    result = []
    for c in range(3):
        plane = [planes[8 * (3 * i + c) : 8 * (3 * i + c) + 8] for i in range(4)]
        result.append(
            (plane[0] * along_x[0] + plane[1] * along_x[1]) + (plane[2] * along_x[2] + plane[3] * along_x[3])
        )
    return result


def move_groups(groups, count, box_table, from_lower, from_upper, state, stokes, out):
    matrices, carry, rates, alive = [], [], [], []
    for g in range(groups):
        rows = slice(g * GROUP, (g + 1) * GROUP)
        answers = jnp.concatenate([from_lower[g], from_upper[g]], axis=0)
        matrices.append(group_matrix(box_table[g] + answers))
        rates.append(1.0 / stokes[rows, :])
        kept = g * GROUP + lax.broadcasted_iota(jnp.int32, rates[g].shape, 0) < count
        alive.append(kept)
        start = [jnp.where(kept, state[c, rows, :], 0.0) for c in range(6)]
        carry.append((start[:3], start[3:]))
    for _ in range(SUBSTEPS):
        moved = []
        for g in range(groups):
            position, velocity = carry[g]
            rate = rates[g]
            middle_pos = [x + 0.5 * STEP_SIZE * v for x, v in zip(position, velocity)]
            here = sample(matrices[g], position)
            there = sample(matrices[g], middle_pos)
            middle_vel = [v + 0.5 * STEP_SIZE * ((u - v) * rate) for u, v in zip(here, velocity)]
            moved.append(
                (
                    [x + STEP_SIZE * m for x, m in zip(position, middle_vel)],
                    [v + STEP_SIZE * (u - m) * rate for v, u, m in zip(velocity, there, middle_vel)],
                )
            )
        carry = moved
    for g in range(groups):
        rows = slice(g * GROUP, (g + 1) * GROUP)
        for c, value in enumerate([*carry[g][0], *carry[g][1]]):
            out[c, rows, :] = jnp.where(alive[g], value, state[c, rows, :])
    if groups < box_table.shape[0]:
        out[:, groups * GROUP :, :] = state[:, groups * GROUP :, :]


def move_kernel(live, box_table, from_lower, from_upper, state, stokes, out):
    count = live[0]
    groups = box_table.shape[0]
    fewer = 0
    for some in sorted({1, max(1, groups // 2), groups}):

        @pl.when((count > fewer * GROUP) & (count <= some * GROUP))
        def _(some=some):
            move_groups(some, count, box_table, from_lower, from_upper, state, stokes, out)

        fewer = some


def in_smem():
    return pl.BlockSpec(memory_space=pltpu.SMEM)


def in_vmem():
    return pl.BlockSpec(memory_space=pltpu.VMEM)


def exchange(near, far, axis):
    devices = lax.axis_size(axis)
    near_pairs = [(i, i ^ 1) for i in range(devices)]
    far_pairs = [(i, (i + 1 if i % 2 else i - 1) % devices) for i in range(devices)]
    far = lax.ppermute(far, axis, far_pairs)
    return lax.ppermute(near, axis, near_pairs), far


def shift(array, axis, step):
    devices = lax.axis_size(axis)
    return lax.ppermute(array, axis, [(i, (i + step) % devices) for i in range(devices)])


def body(velocity_field, particle_state, stokes_time, box_base, live_bins):
    comps, depth, length, cells = velocity_field.shape
    bins = box_base.shape[0]
    tiles = cells // LANES
    groups = bins // GROUP
    table = box_base.T
    state = particle_state.transpose(1, 0, 2)
    block = pltpu.with_memory_space_constraint(velocity_field, pltpu.HBM)
    params = pltpu.CompilerParams(vmem_limit_bytes=VMEM_LIMIT)

    lower_table, upper_table = shift(table, "slab", 1), shift(table, "slab", -1)
    shape = (comps, depth, tiles, length + 2 * TOP)
    planes = depth + 2 * MARGIN
    rows_of_block = pltpu.VMEM((comps, planes * tiles * (length + 2 * TOP), LANES), jnp.float32)
    edge_rows = jax.ShapeDtypeStruct((comps, depth, 2, cells), jnp.float32)
    near, far = pl.pallas_call(
        edges_kernel,
        out_shape=(edge_rows, edge_rows),
        in_specs=[pl.BlockSpec(memory_space=pl.ANY)],
        out_specs=(in_vmem(), in_vmem()),
        scratch_shapes=[pltpu.SemaphoreType.DMA((2,))],
        compiler_params=params,
        name="edges",
    )(block)
    near, far = exchange(near, far, "sub")

    smem_table = pltpu.SMEM(table.shape, jnp.int32)
    padded, own_table = pl.pallas_call(
        load_kernel,
        out_shape=(pltpu.VMEM((comps, planes, tiles, length + 2 * TOP, LANES), jnp.float32), smem_table),
        in_specs=[pl.BlockSpec(memory_space=pl.ANY)] * 2,
        out_specs=(in_vmem(), in_smem()),
        scratch_shapes=[pltpu.SemaphoreType.DMA((1 + tiles,))],
        compiler_params=params,
        cost_estimate=pl.CostEstimate(flops=1_000_000, bytes_accessed=6_000_000, transcendentals=0),
        name="load",
    )(block, pltpu.with_memory_space_constraint(table, pltpu.HBM))

    padded = padded.reshape(rows_of_block.shape)
    hits = pl.pallas_call(
        functools.partial(hits_kernel, depth=depth),
        out_shape=pltpu.SMEM((5, 2 * bins), jnp.int32),
        in_specs=[in_vmem(), in_vmem()],
        out_specs=in_smem(),
        compiler_params=params,
        name="hits",
    )(upper_table, lower_table)
    answer = jax.ShapeDtypeStruct((groups, 8, LANES), jnp.float32)
    for_upper, for_lower, padded = pl.pallas_call(
        functools.partial(answers_kernel, shape=shape),
        out_shape=(answer, answer, rows_of_block),
        in_specs=[in_smem(), in_vmem(), in_vmem(), in_vmem()],
        out_specs=(in_vmem(), in_vmem(), in_vmem()),
        scratch_shapes=[pltpu.VMEM((2 * groups, comps, 8, LANES), jnp.float32)],
        input_output_aliases={1: 2},
        compiler_params=params,
        name="answers",
    )(hits, padded, far, near)
    from_lower, from_upper = shift(for_upper, "slab", 1), shift(for_lower, "slab", -1)

    box_table, _ = pl.pallas_call(
        functools.partial(boxes_kernel, shape=shape),
        out_shape=(jax.ShapeDtypeStruct((groups, NODES, LANES), jnp.float32), rows_of_block),
        in_specs=[in_smem(), in_smem(), in_vmem(), in_vmem(), in_vmem()],
        out_specs=(in_vmem(), in_vmem()),
        scratch_shapes=[pltpu.VMEM((groups, 2, comps, 8, LANES), jnp.float32)],
        input_output_aliases={4: 1},
        compiler_params=params,
        cost_estimate=pl.CostEstimate(flops=1_000_000, bytes_accessed=4_000_000, transcendentals=0),
        name="boxes",
    )(own_table, live_bins, far, near, padded)

    moved = pl.pallas_call(
        move_kernel,
        out_shape=jax.ShapeDtypeStruct(state.shape, jnp.float32),
        in_specs=[in_smem()] + [in_vmem()] * 5,
        out_specs=in_vmem(),
        compiler_params=params,
        name="move",
    )(live_bins, box_table, from_lower, from_upper, state, stokes_time)
    return moved.transpose(1, 0, 2)


def solution(mesh):
    placed = (
        P(None, "slab", "sub", None),
        P(("slab", "sub"), None, None),
        P(("slab", "sub"), None),
        P(("slab", "sub"), None),
        P(("slab", "sub")),
    )
    return jax.shard_map(
        body, mesh=mesh, in_specs=placed, out_specs=P(("slab", "sub"), None, None), check_vma=False
    )
```
